32 devices in a mesh: dom: 8 (over z, x), cls: 4 (over y, core).
Axes of the slice: x: 2, y: 2, z: 4, core: 2. Of those that a mesh axis runs over, the one named last changes fastest.
Arguments:
- images: bfloat16 [4096, 4096], P(('dom', 'cls')), may hold values from -96 to 96
- destinations: int32 [4096, 1], P(('dom', 'cls')), may hold values from 0 to 7; in each aligned block of 128 rows (0 to 127, 128 to 255, ...) at most 32 rows name the same one
- group_ids: int32 [4096], P(('dom', 'cls')), may hold values from 0 to 15
- offsets: int32 [3, 2], replicated, may hold values from -4 to 4
- inv_noise: float32 [2048], replicated, may hold values from 0.02 to 0.2
- ctf_table: float32 [16, 2048], replicated, may hold values from -1 to 1
- references: bfloat16 [288, 4096], P('cls', 'dom'), may hold values from -16 to 16
Outputs:
- posteriors: float32 [8192, 288], P('dom', 'cls')
- log_norms: float32 [8192], P('dom')
The draws below stay inside these ranges and needn't reach their ends.
Inputs may be any that keep to these rules, and one draw needn't show every extreme that they name: `destinations`: in the rows of one device no destination is named more than 32 times.
All inputs are finite; a program needn't handle non-finite values.
Results may differ from the reference program's by a relative error of at most 0.00061.
Values may be sent and summed in bfloat16 or wider, within the bound.
A program may use at most 64 MiB of HBM per device.

```python
import math
import jax
import jax.numpy as jnp
import numpy as np
from jax import lax

SIDE = 64
F = 2048
ROT = 36
NT = 3
G = 16
P_DEV = 128
CAP = 32
SLOTS = 256
K = 8
PARTICLES = 4096
ROWS_OUT = 8192
N_DOM = 8
N_CLS = 4


def class_amplitudes(key):
    first_key = jax.random.fold_in(jax.random.fold_in(key, 201), 0)
    amplitudes = jnp.exp(jax.random.uniform(first_key, (K,), jnp.float32, math.log(0.2), math.log(0.55)))
    return amplitudes


def reference_rows(key):
    amplitudes = class_amplitudes(key)
    first_key = jax.random.fold_in(jax.random.fold_in(key, 202), 0)
    base = jnp.clip(jax.random.normal(first_key, (K * ROT, 2 * F), jnp.float32), -6.0, 6.0)
    row_amplitude = jnp.repeat(amplitudes, ROT)
    return base * row_amplitude[:, None]


def ctf_values(key):
    return jax.random.uniform(jax.random.fold_in(key, 203), (G, F), jnp.float32, -1.0, 1.0)


def group_values(key):
    return jax.random.randint(jax.random.fold_in(key, 204), (PARTICLES,), 0, G).astype(jnp.int32)


def offset_values(key):
    return jax.random.randint(jax.random.fold_in(key, 205), (NT, 2), -4, 5).astype(jnp.int32)


def phase_values(offsets):
    freq_index = jnp.arange(F, dtype=jnp.int32)
    half_side = SIDE // 2
    row_freq = freq_index // half_side
    col_freq = freq_index % half_side
    row_freq = jnp.where(row_freq >= half_side, row_freq - SIDE, row_freq)
    turns = jnp.mod(offsets[:, 0:1] * row_freq[None, :] + offsets[:, 1:2] * col_freq[None, :], SIDE)
    angles = turns.astype(jnp.float32) * (2.0 * math.pi / SIDE)
    return (jnp.cos(angles), jnp.sin(angles))


def draw_references(key, part):
    return reference_rows(key).astype(jnp.bfloat16)


def draw_ctf_table(key, part):
    return ctf_values(key)


def draw_group_ids(key, part):
    return group_values(key)


def draw_offsets(key, part):
    return offset_values(key)


def draw_images(key, part):
    refs = reference_rows(key).astype(jnp.bfloat16).astype(jnp.float32)
    ctf = ctf_values(key)
    groups = group_values(key)
    cosines, sines = phase_values(offset_values(key))
    match_key, shift_key, noise_key = jax.random.split(jax.random.fold_in(key, 206), 3)
    matched = jax.random.randint(match_key, (PARTICLES,), 0, K * ROT).astype(jnp.int32)
    shift_pick = jax.random.randint(shift_key, (PARTICLES,), 0, NT).astype(jnp.int32)
    block_rows = 512

    def one_block(block_index):
        start = (block_index * block_rows).astype(jnp.int32)
        match_rows = lax.dynamic_slice_in_dim(matched, start, block_rows, 0)
        group_rows = lax.dynamic_slice_in_dim(groups, start, block_rows, 0)
        shift_rows = lax.dynamic_slice_in_dim(shift_pick, start, block_rows, 0)
        chosen = refs[match_rows]
        ref_real = chosen[:, :F]
        ref_imag = chosen[:, F:]
        ctf_rows = ctf[group_rows]
        cosine = cosines[shift_rows]
        sine = sines[shift_rows]
        signal_real = ctf_rows * (ref_real * cosine + ref_imag * sine)
        signal_imag = ctf_rows * (ref_imag * cosine - ref_real * sine)
        block_key = jax.random.fold_in(noise_key, block_index)
        noise = jnp.clip(jax.random.normal(block_key, (block_rows, 2 * F), jnp.float32), -6.0, 6.0)
        return jnp.concatenate([signal_real, signal_imag], axis=1) + noise
    values = lax.map(one_block, jnp.arange(PARTICLES // block_rows, dtype=jnp.int32))
    return values.reshape(PARTICLES, 2 * F).astype(jnp.bfloat16)


def deal_out(key, own, number, rows, count, top, most, slope):
    ranking = jax.random.permutation(key, count)
    heavy_load, ordinary = load_shares(count, rows * top, most, slope, True), load_shares(count, rows * top, most, slope, False)
    places = jnp.arange(count)

    def named(tallies, offset_by):
        used = int((tallies > 0).sum())
        fixed = max(1, used // 4)
        moved = fixed + (places - fixed + offset_by * (used - fixed)) % max(1, count - fixed)
        return jnp.zeros((count,), jnp.int32).at[ranking[jnp.where(places < fixed, places, moved)]].set(jnp.asarray(tallies, jnp.int32))

    tallies = jnp.where(number % 4 == 0, named(heavy_load, number // 4), named(ordinary, number - number // 4 - 1))
    mixed = jax.random.permutation(jax.random.fold_in(own, 3), count)
    giver, receiver = mixed[0:count // 2 * 2:2], mixed[1:count // 2 * 2:2]
    room = jnp.minimum(tallies[giver] - 1, most - tallies[receiver]) // 2
    room = jnp.where((giver == ranking[0]) | (receiver == ranking[0]) | (tallies[receiver] == 0), 0, jnp.maximum(room, 0))
    moved = jax.random.randint(jax.random.fold_in(own, 4), (count // 2,), 0, 1 << 20) % (room + 1)
    tallies = tallies.at[giver].add(-moved).at[receiver].add(moved)
    labels = jnp.searchsorted(jnp.cumsum(tallies), jnp.arange(rows * top), side="right").astype(jnp.int32)
    grid = labels.reshape(top, rows).T
    grid = grid[jax.random.permutation(jax.random.fold_in(own, 1), rows)]
    offset_by = jax.random.randint(jax.random.fold_in(own, 2), (rows, 1), 0, top)
    return jnp.take_along_axis(grid, (jnp.arange(top)[None, :] + offset_by) % top, axis=1)


def load_shares(amount, total, reach, slope, full):
    portions = [(1 << 20) // math.isqrt(standing ** slope) + 1 for standing in range(1, amount + 1)]
    largest = reach if full else min(reach, max(-(-total // amount), total * portions[0] // sum(portions)))
    least = 1 if total - largest >= amount - 1 else 0
    given, spare = [largest] + [least] * (amount - 1), total - largest - least * (amount - 1)
    while spare > 0:
        candidates = [i for i in range(1, amount) if given[i] < largest] or [i for i in range(1, amount) if given[i] < reach]
        whole, budget = sum([portions[i] for i in candidates]), spare
        for i in candidates:
            more = min(reach - given[i], max(1, budget * portions[i] // whole), spare)
            given[i] = given[i] + more
            spare = spare - more
    return np.array(given)


def setup_inputs(seed: int = 0) -> dict:
    key_list = jax.random.split(jax.random.key(seed), 8)
    images = draw_images(jax.random.fold_in(key_list[7], 71), 0)
    destinations_keys = jax.random.split(jax.random.fold_in(key_list[1], 1), PARTICLES // P_DEV)
    destinations_turns = jax.random.permutation(jax.random.fold_in(key_list[1], 3), PARTICLES // P_DEV)
    destinations = jax.vmap(lambda own, number: deal_out(jax.random.fold_in(key_list[1], 2), own, number, P_DEV, N_DOM, 1, CAP, 1))(destinations_keys, destinations_turns).reshape((PARTICLES, 1))
    group_ids = draw_group_ids(jax.random.fold_in(key_list[7], 71), 0)
    offsets = draw_offsets(jax.random.fold_in(key_list[7], 71), 0)
    inv_noise = jnp.clip(jnp.exp(jax.random.uniform(key_list[4], (F,), jnp.float32, math.log(0.02), math.log(0.2))), 0.02, 0.2)
    ctf_table = draw_ctf_table(jax.random.fold_in(key_list[7], 71), 0)
    references = draw_references(jax.random.fold_in(key_list[7], 71), 0)
    return {"images": images, "destinations": destinations, "group_ids": group_ids, "offsets": offsets, "inv_noise": inv_noise, "ctf_table": ctf_table, "references": references}


def phase_tables(offsets):
    freq_index = jnp.arange(F, dtype=jnp.int32)
    half_side = SIDE // 2
    row_freq = freq_index // half_side
    col_freq = freq_index % half_side
    row_freq = jnp.where(row_freq >= half_side, row_freq - SIDE, row_freq)
    turns = jnp.mod(offsets[:, 0:1] * row_freq[None, :] + offsets[:, 1:2] * col_freq[None, :], SIDE)
    angles = turns.astype(jnp.float32) * (2.0 * math.pi / SIDE)
    return jnp.cos(angles), jnp.sin(angles)


def shifted_rows(block_images, weight, cosines, sines):
    real_part = block_images[:, :F].astype(jnp.float32)
    imag_part = block_images[:, F:].astype(jnp.float32)
    pieces = []
    for shift_index in range(NT):
        cosine = cosines[shift_index][None, :]
        sine = sines[shift_index][None, :]
        both = jnp.concatenate([weight * (real_part * cosine - imag_part * sine), weight * (real_part * sine + imag_part * cosine)], axis=1)
        pieces.append(both.astype(jnp.bfloat16))
    return jnp.concatenate(pieces, axis=0)


def reference(images, destinations, group_ids, offsets, inv_noise, ctf_table, references):
    blocks = N_DOM * N_CLS
    target = destinations[:, 0].reshape(blocks, P_DEV)
    target_hot = (target[:, :, None] == jnp.arange(N_DOM, dtype=jnp.int32)[None, None, :]).astype(jnp.int32)
    earlier = jnp.cumsum(target_hot, axis=1) - target_hot
    position_rank = jnp.sum(earlier * target_hot, axis=2)
    block_ids = jnp.arange(blocks, dtype=jnp.int32)
    source_dom = block_ids // N_CLS
    source_cls = block_ids % N_CLS
    out_rows = (target * (N_CLS * SLOTS) + source_cls[:, None] * SLOTS + source_dom[:, None] * CAP + position_rank).reshape(-1).astype(jnp.int32)
    cosines, sines = phase_tables(offsets)
    refs_float = references.astype(jnp.float32)
    squared = refs_float * refs_float
    noise_ctf = inv_noise[None, :] * ctf_table * ctf_table
    doubled = jnp.concatenate([noise_ctf, noise_ctf], axis=1)
    group_norms = jnp.dot(doubled, squared.T, precision=lax.Precision.HIGHEST, preferred_element_type=jnp.float32)
    refs_columns = references.T
    block_rows = 512

    def score_block(inputs):
        block_images, block_groups = inputs
        weight = inv_noise[None, :] * ctf_table[block_groups]
        shifted = shifted_rows(block_images, weight, cosines, sines)
        cross = jnp.dot(shifted, refs_columns, preferred_element_type=jnp.float32).reshape(NT, block_rows, K * ROT)
        scores = cross - 0.5 * group_norms[block_groups][None, :, :]
        row_peak = jnp.max(scores, axis=(0, 2))
        row_total = jnp.sum(jnp.exp(scores - row_peak[None, :, None]), axis=(0, 2))
        log_norm = row_peak + jnp.log(row_total)
        posterior = jnp.sum(jnp.exp(scores - log_norm[None, :, None]), axis=0)
        return posterior, log_norm

    posterior_all, norm_all = lax.map(score_block, (images.reshape(-1, block_rows, 2 * F), group_ids.reshape(-1, block_rows)))
    posteriors = jnp.zeros((ROWS_OUT, K * ROT), jnp.float32).at[out_rows].set(posterior_all.reshape(-1, K * ROT))
    log_norms = jnp.zeros((ROWS_OUT,), jnp.float32).at[out_rows].set(norm_all.reshape(-1))
    return posteriors, log_norms
```

```python
import math

import jax
import jax.numpy as jnp
from jax import lax
from jax.sharding import PartitionSpec as P

SIDE = 64


def phase_tables(offsets, kept):
    freq_index = jnp.arange(kept, dtype=jnp.int32)
    half_side = SIDE // 2
    row_freq = freq_index // half_side
    col_freq = freq_index % half_side
    row_freq = jnp.where(row_freq >= half_side, row_freq - SIDE, row_freq)
    turns = jnp.mod(offsets[:, 0:1] * row_freq[None, :] + offsets[:, 1:2] * col_freq[None, :], SIDE)
    angles = turns.astype(jnp.float32) * (2.0 * math.pi / SIDE)
    return (jnp.cos(angles), jnp.sin(angles))


def shifted_rows(images, group_hot, offsets, inv_noise, ctf_table):
    kept = inv_noise.shape[0]
    cosines, sines = phase_tables(offsets, kept)
    ctf_rows = jnp.dot(
        group_hot, ctf_table, precision=lax.Precision.HIGHEST, preferred_element_type=jnp.float32
    )
    weight = inv_noise[None, :] * ctf_rows
    real_part = images[:, :kept].astype(jnp.float32)
    imag_part = images[:, kept:].astype(jnp.float32)
    pieces = []
    for shift_index in range(offsets.shape[0]):
        cosine = cosines[shift_index][None, :]
        sine = sines[shift_index][None, :]
        both = jnp.concatenate(
            [
                weight * (real_part * cosine - imag_part * sine),
                weight * (real_part * sine + imag_part * cosine),
            ],
            axis=1,
        )
        pieces.append(both.astype(jnp.bfloat16))
    return jnp.concatenate(pieces, axis=0)


def slots_of(target, dom_size, capacity):
    local_count = target.shape[0]
    target_hot = (target[:, None] == jnp.arange(dom_size, dtype=jnp.int32)[None, :]).astype(
        jnp.float32
    )
    local_index = jnp.arange(local_count, dtype=jnp.int32)
    lower = (local_index[:, None] > local_index[None, :]).astype(jnp.float32)
    earlier = jnp.dot(lower, target_hot, preferred_element_type=jnp.float32)
    position_rank = jnp.sum(earlier * target_hot, axis=1).astype(jnp.int32)
    return target * capacity + position_rank


def plain_shards(images, destinations, group_ids, offsets, inv_noise, ctf_table, references):
    dom_size = lax.axis_size("dom")
    cls_size = lax.axis_size("cls")
    local_count = images.shape[0]
    shift_count = offsets.shape[0]
    group_count = ctf_table.shape[0]
    class_count = references.shape[0]
    capacity = 2 * local_count // dom_size
    slot_count = dom_size * capacity
    class_rows = lax.all_gather(references, "cls", axis=0, tiled=True)
    every_ref = lax.all_gather(class_rows, "dom", axis=1, tiled=True)
    slot_of = slots_of(destinations[:, 0], dom_size, capacity)
    chosen = (jnp.arange(slot_count, dtype=jnp.int32)[:, None] == slot_of[None, :]).astype(
        jnp.float32
    )
    group_hot = (group_ids[:, None] == jnp.arange(group_count, dtype=jnp.int32)[None, :]).astype(
        jnp.float32
    )
    noise_ctf = inv_noise[None, :] * ctf_table * ctf_table
    noise_terms = jnp.concatenate([noise_ctf, noise_ctf], axis=1)
    shifted = shifted_rows(images, group_hot, offsets, inv_noise, ctf_table)
    contract = (((1,), (1,)), ((), ()))
    cross = lax.dot_general(shifted, every_ref, contract, preferred_element_type=jnp.float32)
    ref_float = every_ref.astype(jnp.float32)
    norms = lax.dot_general(
        noise_terms,
        ref_float * ref_float,
        contract,
        precision=lax.Precision.HIGHEST,
        preferred_element_type=jnp.float32,
    )
    selected = jnp.dot(
        group_hot, norms, precision=lax.Precision.HIGHEST, preferred_element_type=jnp.float32
    )
    scores = cross.reshape(shift_count, local_count, -1) - 0.5 * selected[None, :, :]
    row_peak = jnp.max(scores, axis=(0, 2))
    weights = jnp.exp(scores - row_peak[None, :, None])
    row_total = jnp.sum(weights, axis=(0, 2))
    log_norm = row_peak + jnp.log(row_total)
    posterior = jnp.sum(weights, axis=0) / row_total[:, None]
    posterior = posterior.reshape(local_count, cls_size, class_count)
    spread = jnp.broadcast_to(log_norm[:, None, None], (local_count, cls_size, 1))
    rows = jnp.concatenate([posterior, spread], axis=2).reshape(local_count, -1)
    slots = jnp.dot(
        chosen, rows, precision=lax.Precision.HIGHEST, preferred_element_type=jnp.float32
    )
    blocks = slots.reshape(dom_size, capacity, cls_size, class_count + 1).transpose(0, 2, 1, 3)
    blocks = blocks.reshape(dom_size * cls_size, capacity, class_count + 1)
    blocks = lax.all_to_all(blocks, ("dom", "cls"), split_axis=0, concat_axis=0, tiled=True)
    blocks = blocks.reshape(dom_size, cls_size, capacity, class_count + 1).transpose(1, 0, 2, 3)
    blocks = blocks.reshape(cls_size * slot_count, class_count + 1)
    return (blocks[:, :class_count], blocks[:, class_count])


def solution(mesh):
    return jax.shard_map(
        plain_shards,
        mesh=mesh,
        in_specs=(
            P(("dom", "cls"), None),
            P(("dom", "cls"), None),
            P(("dom", "cls")),
            P(),
            P(),
            P(),
            P("cls", "dom"),
        ),
        out_specs=(P("dom", "cls"), P("dom")),
        check_vma=False,
    )
```

```python
import functools
import math

import jax
import jax.numpy as jnp
from jax import lax
from jax.experimental import pallas as pl
from jax.experimental.pallas import tpu as pltpu
from jax.sharding import PartitionSpec as P

SIDE = 64


def phase_tables(offsets, kept):
    freq_index = jnp.arange(kept, dtype=jnp.int32)
    half_side = SIDE // 2
    row_freq = freq_index // half_side
    col_freq = freq_index % half_side
    row_freq = jnp.where(row_freq >= half_side, row_freq - SIDE, row_freq)
    turns = jnp.mod(offsets[:, 0:1] * row_freq[None, :] + offsets[:, 1:2] * col_freq[None, :], SIDE)
    angles = turns.astype(jnp.float32) * (2.0 * math.pi / SIDE)
    return (jnp.cos(angles), jnp.sin(angles))


def shifted_rows(images, group_hot, offsets, inv_noise, ctf_table):
    kept = inv_noise.shape[0]
    cosines, sines = phase_tables(offsets, kept)
    ctf_rows = jnp.dot(
        group_hot, ctf_table, precision=lax.Precision.HIGHEST, preferred_element_type=jnp.float32
    )
    weight = inv_noise[None, :] * ctf_rows
    real_part = images[:, :kept].astype(jnp.float32)
    imag_part = images[:, kept:].astype(jnp.float32)
    pieces = []
    for shift_index in range(offsets.shape[0]):
        cosine = cosines[shift_index][None, :]
        sine = sines[shift_index][None, :]
        both = jnp.concatenate(
            [
                weight * (real_part * cosine - imag_part * sine),
                weight * (real_part * sine + imag_part * cosine),
            ],
            axis=1,
        )
        pieces.append(both.astype(jnp.bfloat16))
    return jnp.concatenate(pieces, axis=0)


def slots_of(target, dom_size, capacity):
    local_count = target.shape[0]
    target_hot = (target[:, None] == jnp.arange(dom_size, dtype=jnp.int32)[None, :]).astype(
        jnp.float32
    )
    local_index = jnp.arange(local_count, dtype=jnp.int32)
    lower = (local_index[:, None] > local_index[None, :]).astype(jnp.float32)
    earlier = jnp.dot(lower, target_hot, preferred_element_type=jnp.float32)
    position_rank = jnp.sum(earlier * target_hot, axis=1).astype(jnp.int32)
    return target * capacity + position_rank


def plain_shards(images, destinations, group_ids, offsets, inv_noise, ctf_table, references):
    dom_size = lax.axis_size("dom")
    cls_size = lax.axis_size("cls")
    local_count = images.shape[0]
    shift_count = offsets.shape[0]
    group_count = ctf_table.shape[0]
    class_count = references.shape[0]
    capacity = 2 * local_count // dom_size
    slot_count = dom_size * capacity
    class_rows = lax.all_gather(references, "cls", axis=0, tiled=True)
    every_ref = lax.all_gather(class_rows, "dom", axis=1, tiled=True)
    slot_of = slots_of(destinations[:, 0], dom_size, capacity)
    chosen = (jnp.arange(slot_count, dtype=jnp.int32)[:, None] == slot_of[None, :]).astype(
        jnp.float32
    )
    group_hot = (group_ids[:, None] == jnp.arange(group_count, dtype=jnp.int32)[None, :]).astype(
        jnp.float32
    )
    noise_ctf = inv_noise[None, :] * ctf_table * ctf_table
    noise_terms = jnp.concatenate([noise_ctf, noise_ctf], axis=1)
    shifted = shifted_rows(images, group_hot, offsets, inv_noise, ctf_table)
    contract = (((1,), (1,)), ((), ()))
    cross = lax.dot_general(shifted, every_ref, contract, preferred_element_type=jnp.float32)
    ref_float = every_ref.astype(jnp.float32)
    norms = lax.dot_general(
        noise_terms,
        ref_float * ref_float,
        contract,
        precision=lax.Precision.HIGHEST,
        preferred_element_type=jnp.float32,
    )
    selected = jnp.dot(
        group_hot, norms, precision=lax.Precision.HIGHEST, preferred_element_type=jnp.float32
    )
    scores = cross.reshape(shift_count, local_count, -1) - 0.5 * selected[None, :, :]
    row_peak = jnp.max(scores, axis=(0, 2))
    weights = jnp.exp(scores - row_peak[None, :, None])
    row_total = jnp.sum(weights, axis=(0, 2))
    log_norm = row_peak + jnp.log(row_total)
    posterior = jnp.sum(weights, axis=0) / row_total[:, None]
    posterior = posterior.reshape(local_count, cls_size, class_count)
    spread = jnp.broadcast_to(log_norm[:, None, None], (local_count, cls_size, 1))
    rows = jnp.concatenate([posterior, spread], axis=2).reshape(local_count, -1)
    slots = jnp.dot(
        chosen, rows, precision=lax.Precision.HIGHEST, preferred_element_type=jnp.float32
    )
    blocks = slots.reshape(dom_size, capacity, cls_size, class_count + 1).transpose(0, 2, 1, 3)
    blocks = blocks.reshape(dom_size * cls_size, capacity, class_count + 1)
    blocks = lax.all_to_all(blocks, ("dom", "cls"), split_axis=0, concat_axis=0, tiled=True)
    blocks = blocks.reshape(dom_size, cls_size, capacity, class_count + 1).transpose(1, 0, 2, 3)
    blocks = blocks.reshape(cls_size * slot_count, class_count + 1)
    return (blocks[:, :class_count], blocks[:, class_count])


MESH = pl.DeviceIdType.MESH
NT_DIMS = (((1,), (1,)), ((), ()))


def three_parts(value):
    high = value.astype(jnp.bfloat16)
    rest = value - high.astype(jnp.float32)
    middle = rest.astype(jnp.bfloat16)
    low = (rest - middle.astype(jnp.float32)).astype(jnp.bfloat16)
    return [high, middle, low]


def e_step_kernel(
    dom_size,
    cls_size,
    offsets_ref,
    images_ref,
    target_ref,
    group_ref,
    inv_noise_ref,
    ctf_ref,
    refs_ref,
    out_ref,
    held,
    shifted,
    ctf_parts,
    noise_parts,
    phases,
    cross,
    norms,
    stage,
    send_sem,
    recv_sem,
    post_send,
    post_recv,
    own_sem,
):
    z_size = dom_size // 2
    class_count, block_columns = refs_ref.shape
    half_columns = block_columns // 2
    padded = held.shape[3]
    local_count = images_ref.shape[0]
    kept = inv_noise_ref.shape[1]
    group_count = ctf_ref.shape[0]
    shift_count = offsets_ref.shape[0]
    slot_count = stage.shape[1]
    capacity = slot_count // dom_size
    dom = lax.axis_index("dom")
    cls = lax.axis_index("cls")
    z, x = dom // 2, dom % 2
    y, core = cls // 2, cls % 2

    barrier = pltpu.get_barrier_semaphore()
    partners = [
        (lax.rem(dom + i, dom_size), lax.rem(cls + j, cls_size))
        for i in range(dom_size)
        for j in range(cls_size)
        if i or j
    ]
    for partner in partners:
        pl.semaphore_signal(barrier, inc=1, device_id=partner, device_id_type=MESH)

    for half in range(2):
        held[half, dom, cls, 0:class_count, :] = refs_ref[
            :, half * half_columns : (half + 1) * half_columns
        ]
        held[half, dom, cls, class_count:padded, :] = jnp.zeros(
            (padded - class_count, half_columns), jnp.bfloat16
        )
    pl.semaphore_wait(barrier, len(partners))

    sends = []

    def block_copy(half, block_dom, block_cls, device, index):
        block = held.at[half, block_dom, block_cls]
        return pltpu.make_async_remote_copy(
            src_ref=block,
            dst_ref=block,
            send_sem=send_sem.at[index],
            recv_sem=recv_sem.at[half, block_dom, block_cls],
            device_id=device,
            device_id_type=MESH,
        )

    def send(half, block_dom, block_cls, device):
        copy = block_copy(half, block_dom, block_cls, device, len(sends))
        copy.start()
        sends.append(copy)

    def arrived(half, block_dom, block_cls):
        block_copy(half, block_dom, block_cls, over_core, 0).wait_recv()

    over_x = (z * 2 + (1 - x), cls)
    over_y = (dom, (1 - y) * 2 + core)
    over_core = (dom, y * 2 + (1 - core))
    first = [over_x, over_y]
    last = [over_y, over_x]

    for half in range(2):
        send(half, dom, cls, first[half])
    for step in range(1, z_size):
        for half in range(2):
            send(half, dom, cls, (lax.rem(z + step, z_size) * 2 + x, cls))
    for half in range(2):
        send(half, dom, cls, last[half])
        send(half, dom, cls, over_core)

    freq = lax.broadcasted_iota(jnp.int32, (1, kept), 1)
    half_side = SIDE // 2
    row_freq = freq // half_side
    col_freq = freq % half_side
    row_freq = jnp.where(row_freq >= half_side, row_freq - SIDE, row_freq)
    for t in range(shift_count):
        turns = (offsets_ref[t, 0] * row_freq + offsets_ref[t, 1] * col_freq) & (SIDE - 1)
        angles = turns.astype(jnp.float32) * (2.0 * math.pi / SIDE)
        phases[2 * t : 2 * t + 1, :] = jnp.cos(angles)
        phases[2 * t + 1 : 2 * t + 2, :] = jnp.sin(angles)
    ctf = ctf_ref[...]
    noise_terms = inv_noise_ref[...] * ctf * ctf
    for index, part in enumerate(three_parts(ctf)):
        ctf_parts[index * group_count : (index + 1) * group_count, :] = part
    for index, part in enumerate(three_parts(noise_terms)):
        noise_parts[index * group_count : (index + 1) * group_count, :] = part
    square = (local_count, local_count)
    sub = lax.broadcasted_iota(jnp.int32, square, 0)
    lane = lax.broadcasted_iota(jnp.int32, square, 1)
    group_row = group_ref[...]
    group_col = jnp.sum(jnp.where(sub == lane, group_row, 0), axis=1, keepdims=True)
    part_lane = lax.broadcasted_iota(jnp.int32, (local_count, 3 * group_count), 1)
    group_hot = jnp.where(part_lane % group_count == group_col, 1.0, 0.0).astype(jnp.bfloat16)

    chunk = kept // z_size

    def shift_chunk(step):
        low = step * chunk
        columns = slice(low, low + chunk)
        imag_columns = slice(kept + low, kept + low + chunk)
        weight = inv_noise_ref[:, columns] * jnp.dot(
            group_hot, ctf_parts[:, columns], preferred_element_type=jnp.float32
        )
        real_part = images_ref[:, columns].astype(jnp.float32)
        imag_part = images_ref[:, imag_columns].astype(jnp.float32)
        for t in range(shift_count):
            cosine = phases[2 * t : 2 * t + 1, columns]
            sine = phases[2 * t + 1 : 2 * t + 2, columns]
            rows = slice(t * local_count, (t + 1) * local_count)
            shifted[rows, columns] = (
                weight * (real_part * cosine - imag_part * sine)
            ).astype(jnp.bfloat16)
            shifted[rows, imag_columns] = (
                weight * (real_part * sine + imag_part * cosine)
            ).astype(jnp.bfloat16)

    z_order = [0, 1, z_size - 1] + list(range(2, z_size - 1))
    z_order = z_order[:z_size]
    shift_chunk(0)
    for count, step in enumerate(z_order[1:]):
        block = lax.rem(z + step, z_size) * 2 + x
        for half in range(2):
            arrived(half, block, cls)
            send(half, block, cls, first[half])
        for half in range(2):
            send(half, block, cls, last[half])
            send(half, block, cls, over_core)
        shift_chunk(count + 1)

    for step in z_order:
        block_z = lax.rem(z + step, z_size)
        for half in range(2):
            block = (block_z * 2 + (1 - x), cls) if half == 0 else (block_z * 2 + x, over_y[1])
            arrived(half, *block)
            send(half, *block, last[half])
            send(half, *block, over_core)

    cross[...] = jnp.zeros_like(cross)
    norms[...] = jnp.zeros_like(norms)

    def add_block(half, block_dom):
        sibling = lax.rem(core + 1, 2)
        arrived(half, block_dom, sibling)
        arrived(half, block_dom, 2 + sibling)
        rows = held[half, block_dom].reshape(cls_size * padded, half_columns)
        low = pl.multiple_of(block_dom * block_columns + half * half_columns, half_columns)
        cross[...] += lax.dot_general(
            rows, shifted[:, pl.ds(low, half_columns)], NT_DIMS, preferred_element_type=jnp.float32
        )
        wide = rows.astype(jnp.float32)
        squares = wide * wide
        high = squares.astype(jnp.bfloat16)
        rest = (squares - high.astype(jnp.float32)).astype(jnp.bfloat16)
        low = pl.multiple_of(lax.rem(low, kept), half_columns)
        noise = noise_parts[:, pl.ds(low, half_columns)]
        norms[...] += lax.dot_general(
            high, noise, NT_DIMS, preferred_element_type=jnp.float32
        ) + lax.dot_general(rest, noise, NT_DIMS, preferred_element_type=jnp.float32)

    waiting = []
    for near in range(2):
        for step in z_order:
            block_z = lax.rem(z + step, z_size)
            for half in range(2):
                if half == 0:
                    block_x = x if near == 0 else 1 - x
                    block_dom = block_z * 2 + block_x
                    block = (block_dom, over_y[1])
                else:
                    block_dom = block_z * 2 + (1 - x)
                    block = (block_dom, cls if near == 0 else over_y[1])
                arrived(half, *block)
                send(half, *block, over_core)
                if half == 0:
                    waiting.append((0, block_dom))
                elif near == 0:
                    waiting.append((1, block_z * 2 + x))
                else:
                    waiting.append((1, block_dom))
                if len(waiting) > 2:
                    add_block(*waiting.pop(0))
    for item in waiting:
        add_block(*item)

    rows_all = cls_size * padded
    hot_rows = lax.broadcasted_iota(jnp.int32, (9 * group_count, local_count), 0)
    hot_groups = jnp.where(hot_rows % group_count == group_row, 1.0, 0.0).astype(jnp.bfloat16)
    selected = 0.5 * jnp.dot(
        jnp.concatenate(three_parts(norms[...]), axis=1),
        hot_groups,
        preferred_element_type=jnp.float32,
    )
    row = lax.broadcasted_iota(jnp.int32, (rows_all, local_count), 0) % padded
    real_row = row < class_count
    scores = []
    for t in range(shift_count):
        value = cross[:, t * local_count : (t + 1) * local_count] - selected
        scores.append(jnp.where(real_row, value, -jnp.inf))
    peak = functools.reduce(jnp.maximum, scores)
    peak = jnp.max(peak, axis=0, keepdims=True)
    weights = functools.reduce(jnp.add, [jnp.exp(value - peak) for value in scores])
    total = jnp.sum(weights, axis=0, keepdims=True)
    log_norm = peak + jnp.log(total)
    table = jnp.where(row == class_count, log_norm, weights / total)
    table = jnp.concatenate(three_parts(table), axis=1)

    target_col = target_ref[...]
    target_row = jnp.sum(jnp.where(sub == lane, target_col, 0), axis=0, keepdims=True)
    ahead = (target_col == target_row) & (sub < lane)
    rank = jnp.sum(jnp.where(ahead, 1, 0), axis=0, keepdims=True)
    slot_of = target_row * capacity + rank
    slot = lax.broadcasted_iota(jnp.int32, (slot_count, local_count), 0)
    hot = jnp.where(slot == slot_of, 1.0, 0.0).astype(jnp.bfloat16)
    hot = jnp.concatenate([hot, hot, hot], axis=1)
    for block in range(cls_size):
        stage[block, :, 0:padded] = lax.dot_general(
            hot,
            table[block * padded : (block + 1) * padded, :],
            NT_DIMS,
            preferred_element_type=jnp.float32,
        )

    def landing(source_dom, source_cls):
        start = pl.multiple_of(source_cls * slot_count + source_dom * capacity, capacity)
        return out_ref.at[pl.ds(start, capacity), :]

    def source(to_dom, to_cls):
        start = pl.multiple_of(to_dom * capacity, capacity)
        return stage.at[to_cls, pl.ds(start, capacity), :]

    posts = []
    for index, (to_dom, to_cls) in enumerate(partners):
        copy = pltpu.make_async_remote_copy(
            src_ref=source(to_dom, to_cls),
            dst_ref=landing(dom, cls),
            send_sem=post_send.at[index],
            recv_sem=post_recv.at[dom, cls],
            device_id=(to_dom, to_cls),
            device_id_type=MESH,
        )
        copy.start()
        posts.append(copy)
    own = pltpu.make_async_copy(source(dom, cls), landing(dom, cls), own_sem)
    own.start()
    for copy in sends:
        copy.wait_send()
    for copy in posts:
        copy.wait_send()
    own.wait()
    for from_dom, from_cls in partners:
        pltpu.make_async_remote_copy(
            src_ref=source(from_dom, from_cls),
            dst_ref=landing(from_dom, from_cls),
            send_sem=post_send.at[0],
            recv_sem=post_recv.at[from_dom, from_cls],
            device_id=(from_dom, from_cls),
            device_id_type=MESH,
        ).wait_recv()


def kernel_shards(images, destinations, group_ids, offsets, inv_noise, ctf_table, references):
    dom_size = lax.axis_size("dom")
    cls_size = lax.axis_size("cls")
    local_count, columns = images.shape
    kept = inv_noise.shape[0]
    group_count = ctf_table.shape[0]
    shift_count = offsets.shape[0]
    class_count, block_columns = references.shape
    slot_count = 2 * local_count
    padded = -(-(class_count + 1) // 16) * 16
    device_count = dom_size * cls_size
    vmem = pl.BlockSpec(memory_space=pltpu.VMEM)
    out = pl.pallas_call(
        functools.partial(e_step_kernel, dom_size, cls_size),
        out_shape=jax.ShapeDtypeStruct((cls_size * slot_count, 128), jnp.float32),
        in_specs=[pl.BlockSpec(memory_space=pltpu.SMEM)] + [vmem] * 6,
        out_specs=pl.BlockSpec(memory_space=pl.ANY),
        scratch_shapes=[
            pltpu.VMEM((2, dom_size, cls_size, padded, block_columns // 2), jnp.bfloat16),
            pltpu.VMEM((shift_count * local_count, columns), jnp.bfloat16),
            pltpu.VMEM((3 * group_count, kept), jnp.bfloat16),
            pltpu.VMEM((3 * group_count, kept), jnp.bfloat16),
            pltpu.VMEM((2 * shift_count, kept), jnp.float32),
            pltpu.VMEM((cls_size * padded, shift_count * local_count), jnp.float32),
            pltpu.VMEM((cls_size * padded, 3 * group_count), jnp.float32),
            pltpu.VMEM((cls_size, slot_count, 128), jnp.float32),
            pltpu.SemaphoreType.DMA((2 * device_count + dom_size,)),
            pltpu.SemaphoreType.DMA((2, dom_size, cls_size)),
            pltpu.SemaphoreType.DMA((device_count,)),
            pltpu.SemaphoreType.DMA((dom_size, cls_size)),
            pltpu.SemaphoreType.DMA,
        ],
        compiler_params=pltpu.CompilerParams(
            collective_id=0, has_side_effects=True, vmem_limit_bytes=40 * 1024 * 1024
        ),
    )(
        offsets,
        images,
        destinations,
        group_ids[None, :],
        inv_noise[None, :],
        ctf_table,
        references,
    )
    return (out[:, :class_count], out[:, class_count])


def fits_kernel(mesh, images, references):
    dom_size, cls_size = mesh.shape["dom"], mesh.shape["cls"]
    local_count = images.shape[0] // (dom_size * cls_size)
    block_columns = references.shape[1] // dom_size
    return (
        cls_size == 4
        and dom_size % 2 == 0
        and local_count == 128
        and 2 * local_count // dom_size % 8 == 0
        and block_columns % 256 == 0
        and references.shape[0] // cls_size < 128
    )


def solution(mesh):
    def e_step(*arrays):
        shards = kernel_shards if fits_kernel(mesh, arrays[0], arrays[-1]) else plain_shards
        return mapped(mesh, shards)(*arrays)

    return e_step


def mapped(mesh, shards):
    return jax.shard_map(
        shards,
        mesh=mesh,
        in_specs=(
            P(("dom", "cls"), None),
            P(("dom", "cls"), None),
            P(("dom", "cls")),
            P(),
            P(),
            P(),
            P("cls", "dom"),
        ),
        out_specs=(P("dom", "cls"), P("dom")),
        check_vma=False,
    )
```

```python
import functools
import math

import jax
import jax.numpy as jnp
from jax import lax
from jax.experimental import pallas as pl
from jax.experimental.pallas import tpu as pltpu
from jax.sharding import PartitionSpec as P

SIDE = 64


def phase_tables(offsets, kept):
    freq_index = jnp.arange(kept, dtype=jnp.int32)
    half_side = SIDE // 2
    row_freq = freq_index // half_side
    col_freq = freq_index % half_side
    row_freq = jnp.where(row_freq >= half_side, row_freq - SIDE, row_freq)
    turns = jnp.mod(offsets[:, 0:1] * row_freq[None, :] + offsets[:, 1:2] * col_freq[None, :], SIDE)
    angles = turns.astype(jnp.float32) * (2.0 * math.pi / SIDE)
    return (jnp.cos(angles), jnp.sin(angles))


def shifted_rows(images, group_hot, offsets, inv_noise, ctf_table):
    kept = inv_noise.shape[0]
    cosines, sines = phase_tables(offsets, kept)
    ctf_rows = jnp.dot(
        group_hot, ctf_table, precision=lax.Precision.HIGHEST, preferred_element_type=jnp.float32
    )
    weight = inv_noise[None, :] * ctf_rows
    real_part = images[:, :kept].astype(jnp.float32)
    imag_part = images[:, kept:].astype(jnp.float32)
    pieces = []
    for shift_index in range(offsets.shape[0]):
        cosine = cosines[shift_index][None, :]
        sine = sines[shift_index][None, :]
        both = jnp.concatenate(
            [
                weight * (real_part * cosine - imag_part * sine),
                weight * (real_part * sine + imag_part * cosine),
            ],
            axis=1,
        )
        pieces.append(both.astype(jnp.bfloat16))
    return jnp.concatenate(pieces, axis=0)


def slots_of(target, dom_size, capacity):
    local_count = target.shape[0]
    target_hot = (target[:, None] == jnp.arange(dom_size, dtype=jnp.int32)[None, :]).astype(
        jnp.float32
    )
    local_index = jnp.arange(local_count, dtype=jnp.int32)
    lower = (local_index[:, None] > local_index[None, :]).astype(jnp.float32)
    earlier = jnp.dot(lower, target_hot, preferred_element_type=jnp.float32)
    position_rank = jnp.sum(earlier * target_hot, axis=1).astype(jnp.int32)
    return target * capacity + position_rank


def plain_shards(images, destinations, group_ids, offsets, inv_noise, ctf_table, references):
    dom_size = lax.axis_size("dom")
    cls_size = lax.axis_size("cls")
    local_count = images.shape[0]
    shift_count = offsets.shape[0]
    group_count = ctf_table.shape[0]
    class_count = references.shape[0]
    capacity = 2 * local_count // dom_size
    slot_count = dom_size * capacity
    class_rows = lax.all_gather(references, "cls", axis=0, tiled=True)
    every_ref = lax.all_gather(class_rows, "dom", axis=1, tiled=True)
    slot_of = slots_of(destinations[:, 0], dom_size, capacity)
    chosen = (jnp.arange(slot_count, dtype=jnp.int32)[:, None] == slot_of[None, :]).astype(
        jnp.float32
    )
    group_hot = (group_ids[:, None] == jnp.arange(group_count, dtype=jnp.int32)[None, :]).astype(
        jnp.float32
    )
    noise_ctf = inv_noise[None, :] * ctf_table * ctf_table
    noise_terms = jnp.concatenate([noise_ctf, noise_ctf], axis=1)
    shifted = shifted_rows(images, group_hot, offsets, inv_noise, ctf_table)
    contract = (((1,), (1,)), ((), ()))
    cross = lax.dot_general(shifted, every_ref, contract, preferred_element_type=jnp.float32)
    ref_float = every_ref.astype(jnp.float32)
    norms = lax.dot_general(
        noise_terms,
        ref_float * ref_float,
        contract,
        precision=lax.Precision.HIGHEST,
        preferred_element_type=jnp.float32,
    )
    selected = jnp.dot(
        group_hot, norms, precision=lax.Precision.HIGHEST, preferred_element_type=jnp.float32
    )
    scores = cross.reshape(shift_count, local_count, -1) - 0.5 * selected[None, :, :]
    row_peak = jnp.max(scores, axis=(0, 2))
    weights = jnp.exp(scores - row_peak[None, :, None])
    row_total = jnp.sum(weights, axis=(0, 2))
    log_norm = row_peak + jnp.log(row_total)
    posterior = jnp.sum(weights, axis=0) / row_total[:, None]
    posterior = posterior.reshape(local_count, cls_size, class_count)
    spread = jnp.broadcast_to(log_norm[:, None, None], (local_count, cls_size, 1))
    rows = jnp.concatenate([posterior, spread], axis=2).reshape(local_count, -1)
    slots = jnp.dot(
        chosen, rows, precision=lax.Precision.HIGHEST, preferred_element_type=jnp.float32
    )
    blocks = slots.reshape(dom_size, capacity, cls_size, class_count + 1).transpose(0, 2, 1, 3)
    blocks = blocks.reshape(dom_size * cls_size, capacity, class_count + 1)
    blocks = lax.all_to_all(blocks, ("dom", "cls"), split_axis=0, concat_axis=0, tiled=True)
    blocks = blocks.reshape(dom_size, cls_size, capacity, class_count + 1).transpose(1, 0, 2, 3)
    blocks = blocks.reshape(cls_size * slot_count, class_count + 1)
    return (blocks[:, :class_count], blocks[:, class_count])


MESH = pl.DeviceIdType.MESH
NT_DIMS = (((1,), (1,)), ((), ()))


def three_parts(value):
    high = value.astype(jnp.bfloat16)
    rest = value - high.astype(jnp.float32)
    middle = rest.astype(jnp.bfloat16)
    low = (rest - middle.astype(jnp.float32)).astype(jnp.bfloat16)
    return [high, middle, low]


def quarter_turns(turns):
    quarter, eighth = SIDE // 4, SIDE // 8
    quadrant = (turns + eighth) // quarter
    angle = (turns - quadrant * quarter).astype(jnp.float32) * (2.0 * math.pi / SIDE)
    square = angle * angle
    sine = 1.0 / 362880.0
    for term in (-1.0 / 5040.0, 1.0 / 120.0, -1.0 / 6.0, 1.0):
        sine = sine * square + term
    sine = sine * angle
    cosine = -1.0 / 3628800.0
    for term in (1.0 / 40320.0, -1.0 / 720.0, 1.0 / 24.0, -0.5, 1.0):
        cosine = cosine * square + term
    quadrant = quadrant & 3
    odd = (quadrant & 1) == 1
    first = jnp.where(odd, sine, cosine)
    second = jnp.where(odd, cosine, sine)
    return (
        jnp.where((quadrant == 1) | (quadrant == 2), -first, first),
        jnp.where(quadrant >= 2, -second, second),
    )


def e_step_kernel(
    dom_size,
    cls_size,
    offsets_ref,
    images_hbm,
    target_ref,
    group_ref,
    inv_noise_hbm,
    ctf_hbm,
    refs_hbm,
    out_ref,
    log_ref,
    images_ref,
    inv_noise_ref,
    ctf_ref,
    refs_ref,
    held,
    shifted,
    ctf_parts,
    cosines,
    sines,
    cross,
    norms,
    slot_hot,
    group_hot_rows,
    stage,
    landed,
    load_sem,
    send_sem,
    recv_sem,
    post_send,
    post_recv,
):
    z_size = dom_size // 2
    class_count, block_columns = refs_ref.shape
    half_columns = block_columns // 2
    padded = held.shape[3]
    local_count = images_ref.shape[0]
    kept = inv_noise_ref.shape[1]
    group_count = ctf_ref.shape[0]
    shift_count = offsets_ref.shape[1]
    slot_count = slot_hot.shape[0]
    capacity = slot_count // dom_size
    piece_rows, lanes = stage.shape[2:]
    group_size = lanes // capacity
    pieces = group_size - 1
    dom = lax.axis_index("dom")
    cls = lax.axis_index("cls")
    z, x = dom // 2, dom % 2
    y, core = cls // 2, cls % 2

    loads = [
        pltpu.make_async_copy(source, place, load_sem.at[index])
        for index, (source, place) in enumerate(
            [
                (refs_hbm, refs_ref),
                (ctf_hbm, ctf_ref),
                (inv_noise_hbm, inv_noise_ref),
                (images_hbm, images_ref),
            ]
        )
    ]
    for load in loads:
        load.start()
    barrier = pltpu.get_barrier_semaphore()
    partners = [
        (lax.rem(dom + i, dom_size), lax.rem(cls + j, cls_size))
        for i in sorted(range(dom_size), key=lambda i: (abs(i - dom_size // 2), i))
        for j in range(cls_size)
        if i or j
    ]
    for partner in partners:
        pl.semaphore_signal(barrier, inc=1, device_id=partner, device_id_type=MESH)

    for load in loads[:3]:
        load.wait()
    wide = refs_ref[...].astype(jnp.float32)
    squares = jnp.concatenate(
        [wide * wide, jnp.zeros((padded - class_count, block_columns), jnp.float32)], axis=0
    )
    high = squares.astype(jnp.bfloat16)
    rest = (squares - high.astype(jnp.float32)).astype(jnp.bfloat16)
    low = pl.multiple_of(lax.rem(dom * block_columns, kept), block_columns)
    own_ctf = ctf_ref[:, pl.ds(low, block_columns)]
    noise_terms = inv_noise_ref[:, pl.ds(low, block_columns)] * own_ctf * own_ctf
    sums = lax.dot_general(
        jnp.concatenate(three_parts(noise_terms), axis=0),
        jnp.concatenate([high, rest], axis=0),
        NT_DIMS,
        preferred_element_type=jnp.float32,
    )
    sums = sums[:, :padded] + sums[:, padded:]
    own_norms = (
        sums[:group_count] + sums[group_count : 2 * group_count] + sums[2 * group_count :]
    )
    tail = jnp.concatenate(
        [part.astype(jnp.float32) for part in three_parts(own_norms)]
        + [jnp.zeros((group_count, half_columns - 3 * padded), jnp.float32)],
        axis=1,
    )
    for half in range(2):
        rows = wide[:, half * half_columns : (half + 1) * half_columns]
        extra = padded - class_count
        block = jnp.concatenate([rows, tail[half * extra : (half + 1) * extra]], axis=0)
        held[half, dom, cls] = block.astype(jnp.bfloat16)
    pl.semaphore_wait(barrier, len(partners))

    sends = []

    def block_copy(half, block_dom, block_cls, device, index):
        block = held.at[half, block_dom, block_cls]
        return pltpu.make_async_remote_copy(
            src_ref=block,
            dst_ref=block,
            send_sem=send_sem.at[index],
            recv_sem=recv_sem.at[half, block_dom, block_cls],
            device_id=device,
            device_id_type=MESH,
        )

    def send(half, block_dom, block_cls, device):
        copy = block_copy(half, block_dom, block_cls, device, len(sends))
        copy.start()
        sends.append(copy)

    def arrived(half, block_dom, block_cls):
        block_copy(half, block_dom, block_cls, over_core, 0).wait_recv()

    over_x = (z * 2 + (1 - x), cls)
    over_y = (dom, (1 - y) * 2 + core)
    over_core = (dom, y * 2 + (1 - core))
    first = [over_x, over_y]
    last = [over_y, over_x]

    for half in range(2):
        send(half, dom, cls, first[half])
    for step in range(1, z_size):
        for half in range(2):
            send(half, dom, cls, (lax.rem(z + step, z_size) * 2 + x, cls))
    for half in range(2):
        send(half, dom, cls, last[half])
        send(half, dom, cls, over_core)

    table_shape = (cosines.shape[0], kept)
    freq = lax.broadcasted_iota(jnp.int32, table_shape, 1)
    shift_row = lax.broadcasted_iota(jnp.int32, table_shape, 0)
    half_side = SIDE // 2
    row_freq = freq // half_side
    col_freq = freq % half_side
    row_freq = jnp.where(row_freq >= half_side, row_freq - SIDE, row_freq)
    turns = jnp.zeros(table_shape, jnp.int32)
    for t in range(shift_count):
        turn = offsets_ref[0, t] * row_freq + offsets_ref[1, t] * col_freq
        turns = jnp.where(shift_row == t, turn & (SIDE - 1), turns)
    cosines[...], sines[...] = quarter_turns(turns)
    for index, part in enumerate(three_parts(ctf_ref[...])):
        ctf_parts[index * group_count : (index + 1) * group_count, :] = part
    square = (local_count, local_count)
    sub = lax.broadcasted_iota(jnp.int32, square, 0)
    lane = lax.broadcasted_iota(jnp.int32, square, 1)
    group_row = group_ref[...]
    group_col = jnp.sum(jnp.where(sub == lane, group_row, 0), axis=1, keepdims=True)
    part_lane = lax.broadcasted_iota(jnp.int32, (local_count, 3 * group_count), 1)
    group_hot = jnp.where(part_lane % group_count == group_col, 1.0, 0.0).astype(jnp.bfloat16)

    chunk = kept // z_size

    def shift_chunk(step):
        low = step * chunk
        columns = slice(low, low + chunk)
        imag_columns = slice(kept + low, kept + low + chunk)
        weight = inv_noise_ref[:, columns] * jnp.dot(
            group_hot, ctf_parts[:, columns], preferred_element_type=jnp.float32
        )
        real_part = images_ref[:, columns].astype(jnp.float32)
        imag_part = images_ref[:, imag_columns].astype(jnp.float32)
        for t in range(shift_count):
            cosine = cosines[t : t + 1, columns]
            sine = sines[t : t + 1, columns]
            rows = slice(t * local_count, (t + 1) * local_count)
            shifted[rows, columns] = (
                weight * (real_part * cosine - imag_part * sine)
            ).astype(jnp.bfloat16)
            shifted[rows, imag_columns] = (
                weight * (real_part * sine + imag_part * cosine)
            ).astype(jnp.bfloat16)

    z_order = [0, 1, z_size - 1] + list(range(2, z_size - 1))
    z_order = z_order[:z_size]
    loads[3].wait()
    shift_chunk(0)
    for count, step in enumerate(z_order[1:]):
        block = lax.rem(z + step, z_size) * 2 + x
        for half in range(2):
            arrived(half, block, cls)
            send(half, block, cls, first[half])
        for half in range(2):
            send(half, block, cls, last[half])
            send(half, block, cls, over_core)
        shift_chunk(count + 1)

    hot_rows = lax.broadcasted_iota(jnp.int32, group_hot_rows.shape, 0)
    group_hot_rows[...] = jnp.where(hot_rows % group_count == group_row, 1.0, 0.0).astype(
        jnp.bfloat16
    )
    target_row = target_ref[...]
    target_col = jnp.sum(jnp.where(sub == lane, target_row, 0), axis=1, keepdims=True)
    ahead = (target_col == target_row) & (sub < lane)
    rank = jnp.sum(jnp.where(ahead, 1, 0), axis=0, keepdims=True)
    slot_of = target_row * capacity + rank
    slot = lax.broadcasted_iota(jnp.int32, (slot_count, local_count), 0)
    hot = jnp.where(slot == slot_of, 1.0, 0.0).astype(jnp.bfloat16)
    for index in range(3):
        slot_hot[:, index * local_count : (index + 1) * local_count] = hot
    cross[...] = jnp.zeros_like(cross)
    norms[...] = jnp.zeros_like(norms)

    for step in z_order:
        block_z = lax.rem(z + step, z_size)
        for half in range(2):
            block = (block_z * 2 + (1 - x), cls) if half == 0 else (block_z * 2 + x, over_y[1])
            arrived(half, *block)
            send(half, *block, last[half])
            send(half, *block, over_core)

    sibling = 1 - core

    def add_block(block_dom):
        for half in range(2):
            arrived(half, block_dom, sibling)
            arrived(half, block_dom, 2 + sibling)
        rows = jnp.concatenate(
            [held[half, block_dom].reshape(cls_size * padded, half_columns) for half in range(2)],
            axis=1,
        )
        low = pl.multiple_of(block_dom * block_columns, block_columns)
        cross[...] += lax.dot_general(
            rows, shifted[:, pl.ds(low, block_columns)], NT_DIMS, preferred_element_type=jnp.float32
        )
        for half in range(2):
            last_rows = held[half, block_dom, :, padded - 16 : padded, :].astype(jnp.float32)
            norms[half] += last_rows[:, 8:16, :]

    waiting = []
    for near in range(2):
        for step in z_order:
            block_z = lax.rem(z + step, z_size)
            block_dom = block_z * 2 + (x if near == 0 else 1 - x)
            far_block = block_z * 2 + (1 - x)
            for half in range(2):
                if half == 0:
                    block = (block_dom, over_y[1])
                else:
                    block = (far_block, cls if near == 0 else over_y[1])
                arrived(half, *block)
                send(half, *block, over_core)
            waiting.append(block_dom)
            if len(waiting) > 1:
                add_block(waiting.pop(0))
    for item in waiting:
        add_block(item)

    selected = []
    for block in range(cls_size):
        both = jnp.concatenate([norms[0, block], norms[1, block]], axis=0)
        total_norm = sum(both[:, p * padded : (p + 1) * padded] for p in range(3))
        selected.append(
            lax.dot_general(
                jnp.concatenate(three_parts(total_norm), axis=0),
                group_hot_rows[...],
                (((0,), (0,)), ((), ())),
                preferred_element_type=jnp.float32,
            )
        )
    selected = 0.5 * jnp.concatenate(selected, axis=0)
    row = lax.broadcasted_iota(jnp.int32, (cls_size * padded, local_count), 0) % padded
    real_row = row < class_count
    scores = []
    for t in range(shift_count):
        value = cross[:, t * local_count : (t + 1) * local_count] - selected
        scores.append(jnp.where(real_row, value, -jnp.inf))
    peak = functools.reduce(jnp.maximum, scores)
    peak = jnp.max(peak, axis=0, keepdims=True)
    weights = functools.reduce(jnp.add, [jnp.exp(value - peak) for value in scores])
    total = jnp.sum(weights, axis=0, keepdims=True)
    log_norm = peak + jnp.log(total)
    table = jnp.where(row == class_count, log_norm, weights / total)

    slots = lax.dot_general(
        jnp.concatenate(three_parts(table), axis=1),
        slot_hot[...],
        NT_DIMS,
        preferred_element_type=jnp.float32,
    )
    lane_group = lax.broadcasted_iota(jnp.int32, (piece_rows, lanes), 1) // capacity

    def turned(value, groups):
        amount = groups % group_size * capacity
        return pltpu.roll(value, amount, 1) if amount else value

    for block in range(cls_size):
        part = slots[block * padded : (block + 1) * padded]
        for to_dom in range(dom_size):
            place, member = to_dom // group_size, to_dom % group_size
            tile = part[:, place * lanes : (place + 1) * lanes]
            norm_rows = jnp.concatenate(
                [tile[class_count:padded], tile[: piece_rows - (padded - class_count)]], axis=0
            )
            message = turned(norm_rows, pieces - member)
            for k in range(pieces):
                piece = tile[k * piece_rows : (k + 1) * piece_rows]
                message = jnp.where(lane_group == k, turned(piece, k - member), message)
            stage[to_dom, block] = message

    posts = []
    for index, (to_dom, to_cls) in enumerate(partners):
        copy = pltpu.make_async_remote_copy(
            src_ref=stage.at[to_dom, to_cls],
            dst_ref=landed.at[cls, dom],
            send_sem=post_send.at[index],
            recv_sem=post_recv.at[cls, dom],
            device_id=(to_dom, to_cls),
            device_id_type=MESH,
        )
        copy.start()
        posts.append(copy)
    landed[cls, dom] = stage[dom, cls]
    for copy in sends:
        copy.wait_send()
    for copy in posts:
        copy.wait_send()
    for from_dom, from_cls in reversed(partners):
        pltpu.make_async_remote_copy(
            src_ref=stage.at[from_dom, from_cls],
            dst_ref=landed.at[from_cls, from_dom],
            send_sem=post_send.at[0],
            recv_sem=post_recv.at[from_cls, from_dom],
            device_id=(from_dom, from_cls),
            device_id_type=MESH,
        ).wait_recv()

    for from_cls in range(cls_size):
        for place in range(dom_size // group_size):
            low = from_cls * slot_count + place * lanes
            got = [landed[from_cls, place * group_size + member] for member in range(group_size)]
            for k in range(group_size):
                value = turned(got[0], 0 - k)
                for member in range(1, group_size):
                    value = jnp.where(
                        lane_group == member, turned(got[member], member - k), value
                    )
                if k < pieces:
                    out_ref[k * piece_rows : (k + 1) * piece_rows, low : low + lanes] = value
                else:
                    log_ref[:, low : low + lanes] = value[0:1]


def kernel_shards(images, destinations, group_ids, offsets, inv_noise, ctf_table, references):
    dom_size = lax.axis_size("dom")
    cls_size = lax.axis_size("cls")
    local_count, columns = images.shape
    kept = inv_noise.shape[0]
    group_count = ctf_table.shape[0]
    shift_count = offsets.shape[0]
    class_count, block_columns = references.shape
    slot_count = 2 * local_count
    lanes = 128
    piece_rows = class_count // (lanes // (slot_count // dom_size) - 1)
    padded = class_count + 8
    device_count = dom_size * cls_size
    table_rows = -(-shift_count // 8) * 8
    vmem = pl.BlockSpec(memory_space=pltpu.VMEM)
    hbm = pl.BlockSpec(memory_space=pltpu.HBM)
    posteriors, log_norms = pl.pallas_call(
        functools.partial(e_step_kernel, dom_size, cls_size),
        out_shape=(
            jax.ShapeDtypeStruct((class_count, cls_size * slot_count), jnp.float32),
            jax.ShapeDtypeStruct((1, cls_size * slot_count), jnp.float32),
        ),
        in_specs=[pl.BlockSpec(memory_space=pltpu.SMEM), hbm, vmem, vmem, hbm, hbm, hbm],
        out_specs=(vmem, vmem),
        scratch_shapes=[
            pltpu.VMEM((local_count, columns), jnp.bfloat16),
            pltpu.VMEM((1, kept), jnp.float32),
            pltpu.VMEM((group_count, kept), jnp.float32),
            pltpu.VMEM((class_count, block_columns), jnp.bfloat16),
            pltpu.VMEM((2, dom_size, cls_size, padded, block_columns // 2), jnp.bfloat16),
            pltpu.VMEM((shift_count * local_count, columns), jnp.bfloat16),
            pltpu.VMEM((3 * group_count, kept), jnp.bfloat16),
            pltpu.VMEM((table_rows, kept), jnp.float32),
            pltpu.VMEM((table_rows, kept), jnp.float32),
            pltpu.VMEM((cls_size * padded, shift_count * local_count), jnp.float32),
            pltpu.VMEM((2, cls_size, 8, block_columns // 2), jnp.float32),
            pltpu.VMEM((slot_count, 3 * local_count), jnp.bfloat16),
            pltpu.VMEM((3 * group_count, local_count), jnp.bfloat16),
            pltpu.VMEM((dom_size, cls_size, piece_rows, lanes), jnp.float32),
            pltpu.VMEM((cls_size, dom_size, piece_rows, lanes), jnp.float32),
            pltpu.SemaphoreType.DMA((4,)),
            pltpu.SemaphoreType.DMA((2 * device_count + dom_size,)),
            pltpu.SemaphoreType.DMA((2, dom_size, cls_size)),
            pltpu.SemaphoreType.DMA((device_count,)),
            pltpu.SemaphoreType.DMA((cls_size, dom_size)),
        ],
        compiler_params=pltpu.CompilerParams(
            collective_id=0, has_side_effects=True, vmem_limit_bytes=56 * 1024 * 1024
        ),
    )(
        offsets.T,
        images,
        destinations.T,
        group_ids[None, :],
        inv_noise[None, :],
        ctf_table,
        references,
    )
    return (posteriors.T, log_norms[0])


def fits_kernel(mesh, images, ctf_table, references):
    dom_size, cls_size = mesh.shape["dom"], mesh.shape["cls"]
    local_count = images.shape[0] // (dom_size * cls_size)
    capacity = 2 * local_count // dom_size
    class_count = references.shape[0] // cls_size
    half_columns = references.shape[1] // dom_size // 2
    if cls_size != 4 or dom_size % 2 or local_count != 128 or 128 % capacity:
        return False
    group_size = 128 // capacity
    return (
        group_size > 1
        and dom_size % group_size == 0
        and class_count % (8 * (group_size - 1)) == 0
        and (class_count + 8) % 16 == 0
        and half_columns % 128 == 0
        and 3 * (class_count + 8) < half_columns
        and ctf_table.shape[0] == 16
    )


def solution(mesh):
    def e_step(*arrays):
        shards = kernel_shards if fits_kernel(mesh, arrays[0], arrays[-2], arrays[-1]) else plain_shards
        return mapped(mesh, shards)(*arrays)

    return e_step


def mapped(mesh, shards):
    return jax.shard_map(
        shards,
        mesh=mesh,
        in_specs=(
            P(("dom", "cls"), None),
            P(("dom", "cls"), None),
            P(("dom", "cls")),
            P(),
            P(),
            P(),
            P("cls", "dom"),
        ),
        out_specs=(P("dom", "cls"), P("dom")),
        check_vma=False,
    )
```

```python
import functools
import math

import jax
import jax.numpy as jnp
from jax import lax
from jax.experimental import pallas as pl
from jax.experimental.pallas import tpu as pltpu
from jax.sharding import PartitionSpec as P

SIDE = 64


def phase_tables(offsets, kept):
    freq_index = jnp.arange(kept, dtype=jnp.int32)
    half_side = SIDE // 2
    row_freq = freq_index // half_side
    col_freq = freq_index % half_side
    row_freq = jnp.where(row_freq >= half_side, row_freq - SIDE, row_freq)
    turns = jnp.mod(offsets[:, 0:1] * row_freq[None, :] + offsets[:, 1:2] * col_freq[None, :], SIDE)
    angles = turns.astype(jnp.float32) * (2.0 * math.pi / SIDE)
    return (jnp.cos(angles), jnp.sin(angles))


def shifted_rows(images, group_hot, offsets, inv_noise, ctf_table):
    kept = inv_noise.shape[0]
    cosines, sines = phase_tables(offsets, kept)
    ctf_rows = jnp.dot(
        group_hot, ctf_table, precision=lax.Precision.HIGHEST, preferred_element_type=jnp.float32
    )
    weight = inv_noise[None, :] * ctf_rows
    real_part = images[:, :kept].astype(jnp.float32)
    imag_part = images[:, kept:].astype(jnp.float32)
    pieces = []
    for shift_index in range(offsets.shape[0]):
        cosine = cosines[shift_index][None, :]
        sine = sines[shift_index][None, :]
        both = jnp.concatenate(
            [
                weight * (real_part * cosine - imag_part * sine),
                weight * (real_part * sine + imag_part * cosine),
            ],
            axis=1,
        )
        pieces.append(both.astype(jnp.bfloat16))
    return jnp.concatenate(pieces, axis=0)


def slots_of(target, dom_size, capacity):
    local_count = target.shape[0]
    target_hot = (target[:, None] == jnp.arange(dom_size, dtype=jnp.int32)[None, :]).astype(
        jnp.float32
    )
    local_index = jnp.arange(local_count, dtype=jnp.int32)
    lower = (local_index[:, None] > local_index[None, :]).astype(jnp.float32)
    earlier = jnp.dot(lower, target_hot, preferred_element_type=jnp.float32)
    position_rank = jnp.sum(earlier * target_hot, axis=1).astype(jnp.int32)
    return target * capacity + position_rank


def plain_shards(images, destinations, group_ids, offsets, inv_noise, ctf_table, references):
    dom_size = lax.axis_size("dom")
    cls_size = lax.axis_size("cls")
    local_count = images.shape[0]
    shift_count = offsets.shape[0]
    group_count = ctf_table.shape[0]
    class_count = references.shape[0]
    capacity = 2 * local_count // dom_size
    slot_count = dom_size * capacity
    class_rows = lax.all_gather(references, "cls", axis=0, tiled=True)
    every_ref = lax.all_gather(class_rows, "dom", axis=1, tiled=True)
    slot_of = slots_of(destinations[:, 0], dom_size, capacity)
    chosen = (jnp.arange(slot_count, dtype=jnp.int32)[:, None] == slot_of[None, :]).astype(
        jnp.float32
    )
    group_hot = (group_ids[:, None] == jnp.arange(group_count, dtype=jnp.int32)[None, :]).astype(
        jnp.float32
    )
    noise_ctf = inv_noise[None, :] * ctf_table * ctf_table
    noise_terms = jnp.concatenate([noise_ctf, noise_ctf], axis=1)
    shifted = shifted_rows(images, group_hot, offsets, inv_noise, ctf_table)
    contract = (((1,), (1,)), ((), ()))
    cross = lax.dot_general(shifted, every_ref, contract, preferred_element_type=jnp.float32)
    ref_float = every_ref.astype(jnp.float32)
    norms = lax.dot_general(
        noise_terms,
        ref_float * ref_float,
        contract,
        precision=lax.Precision.HIGHEST,
        preferred_element_type=jnp.float32,
    )
    selected = jnp.dot(
        group_hot, norms, precision=lax.Precision.HIGHEST, preferred_element_type=jnp.float32
    )
    scores = cross.reshape(shift_count, local_count, -1) - 0.5 * selected[None, :, :]
    row_peak = jnp.max(scores, axis=(0, 2))
    weights = jnp.exp(scores - row_peak[None, :, None])
    row_total = jnp.sum(weights, axis=(0, 2))
    log_norm = row_peak + jnp.log(row_total)
    posterior = jnp.sum(weights, axis=0) / row_total[:, None]
    posterior = posterior.reshape(local_count, cls_size, class_count)
    spread = jnp.broadcast_to(log_norm[:, None, None], (local_count, cls_size, 1))
    rows = jnp.concatenate([posterior, spread], axis=2).reshape(local_count, -1)
    slots = jnp.dot(
        chosen, rows, precision=lax.Precision.HIGHEST, preferred_element_type=jnp.float32
    )
    blocks = slots.reshape(dom_size, capacity, cls_size, class_count + 1).transpose(0, 2, 1, 3)
    blocks = blocks.reshape(dom_size * cls_size, capacity, class_count + 1)
    blocks = lax.all_to_all(blocks, ("dom", "cls"), split_axis=0, concat_axis=0, tiled=True)
    blocks = blocks.reshape(dom_size, cls_size, capacity, class_count + 1).transpose(1, 0, 2, 3)
    blocks = blocks.reshape(cls_size * slot_count, class_count + 1)
    return (blocks[:, :class_count], blocks[:, class_count])


MESH = pl.DeviceIdType.MESH
NT_DIMS = (((1,), (1,)), ((), ()))


def three_parts(value):
    high = value.astype(jnp.bfloat16)
    rest = value - high.astype(jnp.float32)
    middle = rest.astype(jnp.bfloat16)
    low = (rest - middle.astype(jnp.float32)).astype(jnp.bfloat16)
    return [high, middle, low]


def quarter_turns(turns):
    quarter, eighth = SIDE // 4, SIDE // 8
    quadrant = (turns + eighth) // quarter
    angle = (turns - quadrant * quarter).astype(jnp.float32) * (2.0 * math.pi / SIDE)
    square = angle * angle
    sine = 1.0 / 362880.0
    for term in (-1.0 / 5040.0, 1.0 / 120.0, -1.0 / 6.0, 1.0):
        sine = sine * square + term
    sine = sine * angle
    cosine = -1.0 / 3628800.0
    for term in (1.0 / 40320.0, -1.0 / 720.0, 1.0 / 24.0, -0.5, 1.0):
        cosine = cosine * square + term
    quadrant = quadrant & 3
    odd = (quadrant & 1) == 1
    first = jnp.where(odd, sine, cosine)
    second = jnp.where(odd, cosine, sine)
    return (
        jnp.where((quadrant == 1) | (quadrant == 2), -first, first),
        jnp.where(quadrant >= 2, -second, second),
    )


def e_step_kernel(
    dom_size,
    cls_size,
    offsets_ref,
    images_hbm,
    target_ref,
    group_ref,
    inv_noise_hbm,
    ctf_hbm,
    refs_hbm,
    out_ref,
    log_ref,
    images_ref,
    inv_noise_ref,
    ctf_ref,
    refs_ref,
    held,
    shifted,
    ctf_parts,
    cosines,
    sines,
    cross,
    norms,
    slot_hot,
    group_hot_rows,
    stage,
    landed,
    load_sem,
    send_sem,
    recv_sem,
    post_send,
    post_recv,
):
    z_size = dom_size // 2
    class_count, block_columns = refs_ref.shape
    half_columns = block_columns // 2
    padded = held.shape[3]
    local_count = images_ref.shape[0]
    kept = inv_noise_ref.shape[1]
    group_count = ctf_ref.shape[0]
    shift_count = offsets_ref.shape[1]
    slot_count = slot_hot.shape[0]
    capacity = slot_count // dom_size
    piece_rows, lanes = stage.shape[2:]
    group_size = lanes // capacity
    dom = lax.axis_index("dom")
    cls = lax.axis_index("cls")
    z, x = dom // 2, dom % 2
    y, core = cls // 2, cls % 2

    loads = [
        pltpu.make_async_copy(source, place, load_sem.at[index])
        for index, (source, place) in enumerate(
            [
                (refs_hbm, refs_ref),
                (ctf_hbm, ctf_ref),
                (inv_noise_hbm, inv_noise_ref),
                (images_hbm, images_ref),
            ]
        )
    ]
    for load in loads:
        load.start()
    barrier = pltpu.get_barrier_semaphore()
    partners = [
        (lax.rem(dom + i, dom_size), lax.rem(cls + j, cls_size))
        for i in sorted(range(dom_size), key=lambda i: (abs(i - dom_size // 2), i))
        for j in range(cls_size)
        if i or j
    ]
    for partner in partners:
        pl.semaphore_signal(barrier, inc=1, device_id=partner, device_id_type=MESH)

    for load in loads[:3]:
        load.wait()
    wide = refs_ref[...].astype(jnp.float32)
    squares = jnp.concatenate(
        [wide * wide, jnp.zeros((padded - class_count, block_columns), jnp.float32)], axis=0
    )
    high = squares.astype(jnp.bfloat16)
    rest = (squares - high.astype(jnp.float32)).astype(jnp.bfloat16)
    low = pl.multiple_of(lax.rem(dom * block_columns, kept), block_columns)
    own_ctf = ctf_ref[:, pl.ds(low, block_columns)]
    noise_terms = inv_noise_ref[:, pl.ds(low, block_columns)] * own_ctf * own_ctf
    sums = lax.dot_general(
        jnp.concatenate(three_parts(noise_terms), axis=0),
        jnp.concatenate([high, rest], axis=0),
        NT_DIMS,
        preferred_element_type=jnp.float32,
    )
    sums = sums[:, :padded] + sums[:, padded:]
    own_norms = (
        sums[:group_count] + sums[group_count : 2 * group_count] + sums[2 * group_count :]
    )
    tail = jnp.concatenate(
        [part.astype(jnp.float32) for part in three_parts(own_norms)]
        + [jnp.zeros((group_count, half_columns - 3 * padded), jnp.float32)],
        axis=1,
    )
    for half in range(2):
        rows = wide[:, half * half_columns : (half + 1) * half_columns]
        extra = padded - class_count
        block = jnp.concatenate([rows, tail[half * extra : (half + 1) * extra]], axis=0)
        held[half, dom, cls] = block.astype(jnp.bfloat16)
    pl.semaphore_wait(barrier, len(partners))

    sends = []

    def block_copy(half, block_dom, block_cls, device, index):
        halves, sem = (slice(None), 0) if half is None else (half, half)
        block = held.at[halves, block_dom, block_cls]
        return pltpu.make_async_remote_copy(
            src_ref=block,
            dst_ref=block,
            send_sem=send_sem.at[index],
            recv_sem=recv_sem.at[sem, block_dom, block_cls],
            device_id=device,
            device_id_type=MESH,
        )

    def send(half, block_dom, block_cls, device):
        copy = block_copy(half, block_dom, block_cls, device, len(sends))
        copy.start()
        sends.append(copy)

    def arrived(half, block_dom, block_cls):
        block_copy(half, block_dom, block_cls, over_core, 0).wait_recv()

    def z_partner(step):
        other, bit = z, 1
        while bit < z_size:
            if step & bit:
                other = other + bit - 2 * bit * ((z // bit) % 2)
            bit *= 2
        return other

    over_x = (z * 2 + (1 - x), cls)
    over_y = (dom, (1 - y) * 2 + core)
    over_core = (dom, y * 2 + (1 - core))

    send(0, dom, cls, over_x)
    send(1, dom, cls, over_y)
    for step in range(1, min(2, z_size)):
        send(None, dom, cls, (z_partner(step) * 2 + x, cls))
    send(1, dom, cls, over_x)
    send(0, dom, cls, over_y)
    for step in range(2, z_size):
        send(None, dom, cls, (z_partner(step) * 2 + x, cls))
    send(None, dom, cls, over_core)

    table_shape = (cosines.shape[0], kept)
    freq = lax.broadcasted_iota(jnp.int32, table_shape, 1)
    shift_row = lax.broadcasted_iota(jnp.int32, table_shape, 0)
    half_side = SIDE // 2
    row_freq = freq // half_side
    col_freq = freq % half_side
    row_freq = jnp.where(row_freq >= half_side, row_freq - SIDE, row_freq)
    turns = jnp.zeros(table_shape, jnp.int32)
    for t in range(shift_count):
        turn = offsets_ref[0, t] * row_freq + offsets_ref[1, t] * col_freq
        turns = jnp.where(shift_row == t, turn & (SIDE - 1), turns)
    cosines[...], sines[...] = quarter_turns(turns)
    for index, part in enumerate(three_parts(ctf_ref[...])):
        ctf_parts[index * group_count : (index + 1) * group_count, :] = part
    square = (local_count, local_count)
    sub = lax.broadcasted_iota(jnp.int32, square, 0)
    lane = lax.broadcasted_iota(jnp.int32, square, 1)
    group_row = group_ref[...]
    group_col = jnp.sum(jnp.where(sub == lane, group_row, 0), axis=1, keepdims=True)
    part_lane = lax.broadcasted_iota(jnp.int32, (local_count, 3 * group_count), 1)
    group_hot = jnp.where(part_lane % group_count == group_col, 1.0, 0.0).astype(jnp.bfloat16)

    chunk = kept // 4

    def shift_chunk(step):
        low = step * chunk
        columns = slice(low, low + chunk)
        imag_columns = slice(kept + low, kept + low + chunk)
        weight = inv_noise_ref[:, columns] * jnp.dot(
            group_hot, ctf_parts[:, columns], preferred_element_type=jnp.float32
        )
        real_part = images_ref[:, columns].astype(jnp.float32)
        imag_part = images_ref[:, imag_columns].astype(jnp.float32)
        for t in range(shift_count):
            cosine = cosines[t : t + 1, columns]
            sine = sines[t : t + 1, columns]
            rows = slice(t * local_count, (t + 1) * local_count)
            shifted[rows, columns] = (
                weight * (real_part * cosine - imag_part * sine)
            ).astype(jnp.bfloat16)
            shifted[rows, imag_columns] = (
                weight * (real_part * sine + imag_part * cosine)
            ).astype(jnp.bfloat16)

    hot_rows = lax.broadcasted_iota(jnp.int32, group_hot_rows.shape, 0)
    group_hot_rows[...] = jnp.where(hot_rows % group_count == group_row, 1.0, 0.0).astype(
        jnp.bfloat16
    )
    target_row = target_ref[...]
    target_col = jnp.sum(jnp.where(sub == lane, target_row, 0), axis=1, keepdims=True)
    ahead = (target_col == target_row) & (sub < lane)
    rank = jnp.sum(jnp.where(ahead, 1, 0), axis=0, keepdims=True)
    slot_of = target_row * capacity + rank
    slot = lax.broadcasted_iota(jnp.int32, (slot_count, local_count), 0)
    hot = jnp.where(slot == slot_of, 1.0, 0.0).astype(jnp.bfloat16)
    for index in range(3):
        slot_hot[:, index * local_count : (index + 1) * local_count] = hot
    cross[...] = jnp.zeros_like(cross)
    norms[...] = jnp.zeros_like(norms)

    def from_z(step):
        block = z_partner(step) * 2 + x
        arrived(None, block, cls)
        send(0, block, cls, over_x)
        send(1, block, cls, over_y)
        send(1, block, cls, over_x)
        send(0, block, cls, over_y)
        send(None, block, cls, over_core)

    def from_first(step):
        near, far = z_partner(step) * 2 + x, z_partner(step) * 2 + (1 - x)
        arrived(0, far, cls)
        send(0, far, cls, over_y)
        arrived(1, near, over_y[1])
        send(1, near, over_y[1], over_x)
        send(0, far, cls, over_core)
        send(1, near, over_y[1], over_core)

    def from_last(step):
        near, far = z_partner(step) * 2 + x, z_partner(step) * 2 + (1 - x)
        arrived(0, near, over_y[1])
        send(0, near, over_y[1], over_core)
        arrived(1, far, cls)
        send(1, far, cls, over_core)
        arrived(0, far, over_y[1])
        arrived(1, far, over_y[1])
        send(None, far, over_y[1], over_core)

    sibling, far_sibling = over_core[1], (1 - y) * 2 + (1 - core)

    def add_block(block_dom):
        rows = jnp.concatenate(
            [held[half, block_dom].reshape(cls_size * padded, half_columns) for half in range(2)],
            axis=1,
        )
        low = pl.multiple_of(block_dom * block_columns, block_columns)
        cross[...] += lax.dot_general(
            rows, shifted[:, pl.ds(low, block_columns)], NT_DIMS, preferred_element_type=jnp.float32
        )
        for half in range(2):
            last_rows = held[half, block_dom, :, padded - 16 : padded, :].astype(jnp.float32)
            norms[half] += last_rows[:, 8:16, :]

    def multiply(step):
        while chunks:
            shift_chunk(chunks.pop(0))
        near, far = z_partner(step) * 2 + x, z_partner(step) * 2 + (1 - x)
        arrived(None, near, sibling)
        arrived(0, near, far_sibling)
        arrived(1, near, far_sibling)
        add_block(near)
        arrived(0, far, sibling)
        arrived(1, far, sibling)
        arrived(None, far, far_sibling)
        add_block(far)

    chunks = list(range(4))
    loads[3].wait()
    shift_chunk(chunks.pop(0))
    for step in range(z_size + 2):
        if 0 < step < z_size:
            from_z(step)
        if step == 1:
            shift_chunk(chunks.pop(0))
        if step >= 2:
            multiply(step - 2)
        if step < z_size:
            from_first(step)
        if step == 1:
            shift_chunk(chunks.pop(0))
        if 0 < step <= z_size:
            from_last(step - 1)

    selected = []
    for block in range(cls_size):
        both = jnp.concatenate([norms[0, block], norms[1, block]], axis=0)
        total_norm = sum(both[:, p * padded : (p + 1) * padded] for p in range(3))
        selected.append(
            lax.dot_general(
                jnp.concatenate(three_parts(total_norm), axis=0),
                group_hot_rows[...],
                (((0,), (0,)), ((), ())),
                preferred_element_type=jnp.float32,
            )
        )
    selected = 0.5 * jnp.concatenate(selected, axis=0)
    row = lax.broadcasted_iota(jnp.int32, (cls_size * padded, local_count), 0) % padded
    real_row = row < class_count
    scores = []
    for t in range(shift_count):
        value = cross[:, t * local_count : (t + 1) * local_count] - selected
        scores.append(jnp.where(real_row, value, -jnp.inf))
    peak = functools.reduce(jnp.maximum, scores)
    peak = jnp.max(peak, axis=0, keepdims=True)
    weights = functools.reduce(jnp.add, [jnp.exp(value - peak) for value in scores])
    total = jnp.sum(weights, axis=0, keepdims=True)
    log_norm = peak + jnp.log(total)
    table = jnp.where(row == class_count, log_norm, weights / total)

    slots = lax.dot_general(
        jnp.concatenate(three_parts(table), axis=1),
        slot_hot[...],
        NT_DIMS,
        preferred_element_type=jnp.float32,
    )
    lane_group = lax.broadcasted_iota(jnp.int32, (8, lanes), 1) // capacity
    whole = class_count // (8 * group_size)
    left_over = (class_count - whole * 8 * group_size) // group_size

    def turned(value, groups):
        amount = groups % group_size * capacity
        return pltpu.roll(value, amount, 1) if amount else value

    def lifted(value, rows):
        return pltpu.roll(value, rows % 8, 0) if rows % 8 else value

    def side_by_side(values):
        result = values[0]
        for k in range(1, group_size):
            result = jnp.where(lane_group == k, values[k], result)
        return result

    sub_row = lax.broadcasted_iota(jnp.int32, (8, lanes), 0)
    for block in range(cls_size):
        part = slots[block * padded : (block + 1) * padded]
        for to_dom in range(dom_size):
            place, member = to_dom // group_size, to_dom % group_size
            tile = part[:, place * lanes : (place + 1) * lanes]
            for w in range(whole):
                values = []
                for k in range(group_size):
                    top = 8 * (k * whole + w)
                    values.append(turned(tile[top : top + 8], k - member))
                stage[to_dom, block, 8 * w : 8 * w + 8, :] = side_by_side(values)
            rest = tile[8 * whole * group_size : class_count]
            values = [
                turned(lifted(rest, -left_over * k), k - member) for k in range(group_size)
            ]
            norm_row = lifted(turned(tile[class_count:padded], -member), left_over)
            mixed = jnp.where(sub_row < left_over, side_by_side(values), norm_row)
            stage[to_dom, block, 8 * whole : piece_rows, :] = mixed[: piece_rows - 8 * whole]

    posts = []
    for index, (to_dom, to_cls) in enumerate(partners):
        copy = pltpu.make_async_remote_copy(
            src_ref=stage.at[to_dom, to_cls],
            dst_ref=landed.at[cls, dom],
            send_sem=post_send.at[index],
            recv_sem=post_recv.at[cls, dom],
            device_id=(to_dom, to_cls),
            device_id_type=MESH,
        )
        copy.start()
        posts.append(copy)
    landed[cls, dom] = stage[dom, cls]
    for copy in sends:
        copy.wait_send()
    for copy in posts:
        copy.wait_send()
    for from_dom, from_cls in reversed(partners):
        pltpu.make_async_remote_copy(
            src_ref=stage.at[from_dom, from_cls],
            dst_ref=landed.at[from_cls, from_dom],
            send_sem=post_send.at[0],
            recv_sem=post_recv.at[from_cls, from_dom],
            device_id=(from_dom, from_cls),
            device_id_type=MESH,
        ).wait_recv()

    def pad_rows(value):
        empty = jnp.zeros((8 - value.shape[0], lanes), jnp.float32)
        return jnp.concatenate([value, empty], axis=0)

    for from_cls in range(cls_size):
        for place in range(dom_size // group_size):
            low = from_cls * slot_count + place * lanes
            got = [landed[from_cls, place * group_size + member] for member in range(group_size)]
            for k in range(group_size):
                for w in range(whole):
                    top = 8 * (k * whole + w)
                    out_ref[top : top + 8, low : low + lanes] = side_by_side(
                        [
                            turned(value[8 * w : 8 * w + 8], member - k)
                            for member, value in enumerate(got)
                        ]
                    )
                top = 8 * whole * group_size + left_over * k
                out_ref[top : top + left_over, low : low + lanes] = side_by_side(
                    [
                        turned(pad_rows(value[8 * whole :]), member - k)
                        for member, value in enumerate(got)
                    ]
                )[:left_over]
            log_ref[:, low : low + lanes] = side_by_side(
                [turned(pad_rows(value[8 * whole :]), member) for member, value in enumerate(got)]
            )[left_over : left_over + 1]


def kernel_shards(images, destinations, group_ids, offsets, inv_noise, ctf_table, references):
    dom_size = lax.axis_size("dom")
    cls_size = lax.axis_size("cls")
    local_count, columns = images.shape
    kept = inv_noise.shape[0]
    group_count = ctf_table.shape[0]
    shift_count = offsets.shape[0]
    class_count, block_columns = references.shape
    slot_count = 2 * local_count
    lanes = 128
    piece_rows = class_count // (lanes // (slot_count // dom_size)) + 1
    padded = class_count + 8
    device_count = dom_size * cls_size
    table_rows = -(-shift_count // 8) * 8
    vmem = pl.BlockSpec(memory_space=pltpu.VMEM)
    hbm = pl.BlockSpec(memory_space=pltpu.HBM)
    posteriors, log_norms = pl.pallas_call(
        functools.partial(e_step_kernel, dom_size, cls_size),
        out_shape=(
            jax.ShapeDtypeStruct((class_count, cls_size * slot_count), jnp.float32),
            jax.ShapeDtypeStruct((1, cls_size * slot_count), jnp.float32),
        ),
        in_specs=[pl.BlockSpec(memory_space=pltpu.SMEM), hbm, vmem, vmem, hbm, hbm, hbm],
        out_specs=(vmem, vmem),
        scratch_shapes=[
            pltpu.VMEM((local_count, columns), jnp.bfloat16),
            pltpu.VMEM((1, kept), jnp.float32),
            pltpu.VMEM((group_count, kept), jnp.float32),
            pltpu.VMEM((class_count, block_columns), jnp.bfloat16),
            pltpu.VMEM((2, dom_size, cls_size, padded, block_columns // 2), jnp.bfloat16),
            pltpu.VMEM((shift_count * local_count, columns), jnp.bfloat16),
            pltpu.VMEM((3 * group_count, kept), jnp.bfloat16),
            pltpu.VMEM((table_rows, kept), jnp.float32),
            pltpu.VMEM((table_rows, kept), jnp.float32),
            pltpu.VMEM((cls_size * padded, shift_count * local_count), jnp.float32),
            pltpu.VMEM((2, cls_size, 8, block_columns // 2), jnp.float32),
            pltpu.VMEM((slot_count, 3 * local_count), jnp.bfloat16),
            pltpu.VMEM((3 * group_count, local_count), jnp.bfloat16),
            pltpu.VMEM((dom_size, cls_size, piece_rows, lanes), jnp.float32),
            pltpu.VMEM((cls_size, dom_size, piece_rows, lanes), jnp.float32),
            pltpu.SemaphoreType.DMA((4,)),
            pltpu.SemaphoreType.DMA((2 * device_count + dom_size,)),
            pltpu.SemaphoreType.DMA((2, dom_size, cls_size)),
            pltpu.SemaphoreType.DMA((device_count,)),
            pltpu.SemaphoreType.DMA((cls_size, dom_size)),
        ],
        compiler_params=pltpu.CompilerParams(
            collective_id=0, has_side_effects=True, vmem_limit_bytes=24 * 1024 * 1024
        ),
    )(
        offsets.T,
        images,
        destinations.T,
        group_ids[None, :],
        inv_noise[None, :],
        ctf_table,
        references,
    )
    return (posteriors.T, log_norms[0])


def fits_kernel(mesh, images, ctf_table, references):
    dom_size, cls_size = mesh.shape["dom"], mesh.shape["cls"]
    local_count = images.shape[0] // (dom_size * cls_size)
    capacity = 2 * local_count // dom_size
    class_count = references.shape[0] // cls_size
    half_columns = references.shape[1] // dom_size // 2
    if cls_size != 4 or dom_size % 2 or local_count != 128 or 128 % capacity:
        return False
    group_size = 128 // capacity
    return (
        group_size > 1
        and dom_size % group_size == 0
        and class_count % 8 == 0
        and class_count % (8 * group_size) == 8
        and 8 // group_size * group_size == 8
        and 8 // group_size < 8
        and dom_size & (dom_size - 1) == 0
        and (class_count + 8) % 16 == 0
        and half_columns % 128 == 0
        and 3 * (class_count + 8) < half_columns
        and ctf_table.shape[0] == 16
    )


def solution(mesh):
    def e_step(*arrays):
        shards = kernel_shards if fits_kernel(mesh, arrays[0], arrays[-2], arrays[-1]) else plain_shards
        return mapped(mesh, shards)(*arrays)

    return e_step


def mapped(mesh, shards):
    return jax.shard_map(
        shards,
        mesh=mesh,
        in_specs=(
            P(("dom", "cls"), None),
            P(("dom", "cls"), None),
            P(("dom", "cls")),
            P(),
            P(),
            P(),
            P("cls", "dom"),
        ),
        out_specs=(P("dom", "cls"), P("dom")),
        check_vma=False,
    )
```

```python
import functools
import math

import jax
import jax.numpy as jnp
from jax import lax
from jax.experimental import pallas as pl
from jax.experimental.pallas import tpu as pltpu
from jax.sharding import PartitionSpec as P

SIDE = 64


def phase_tables(offsets, kept):
    freq_index = jnp.arange(kept, dtype=jnp.int32)
    half_side = SIDE // 2
    row_freq = freq_index // half_side
    col_freq = freq_index % half_side
    row_freq = jnp.where(row_freq >= half_side, row_freq - SIDE, row_freq)
    turns = jnp.mod(offsets[:, 0:1] * row_freq[None, :] + offsets[:, 1:2] * col_freq[None, :], SIDE)
    angles = turns.astype(jnp.float32) * (2.0 * math.pi / SIDE)
    return (jnp.cos(angles), jnp.sin(angles))


def shifted_rows(images, group_hot, offsets, inv_noise, ctf_table):
    kept = inv_noise.shape[0]
    cosines, sines = phase_tables(offsets, kept)
    ctf_rows = jnp.dot(
        group_hot, ctf_table, precision=lax.Precision.HIGHEST, preferred_element_type=jnp.float32
    )
    weight = inv_noise[None, :] * ctf_rows
    real_part = images[:, :kept].astype(jnp.float32)
    imag_part = images[:, kept:].astype(jnp.float32)
    pieces = []
    for shift_index in range(offsets.shape[0]):
        cosine = cosines[shift_index][None, :]
        sine = sines[shift_index][None, :]
        both = jnp.concatenate(
            [
                weight * (real_part * cosine - imag_part * sine),
                weight * (real_part * sine + imag_part * cosine),
            ],
            axis=1,
        )
        pieces.append(both.astype(jnp.bfloat16))
    return jnp.concatenate(pieces, axis=0)


def slots_of(target, dom_size, capacity):
    local_count = target.shape[0]
    target_hot = (target[:, None] == jnp.arange(dom_size, dtype=jnp.int32)[None, :]).astype(
        jnp.float32
    )
    local_index = jnp.arange(local_count, dtype=jnp.int32)
    lower = (local_index[:, None] > local_index[None, :]).astype(jnp.float32)
    earlier = jnp.dot(lower, target_hot, preferred_element_type=jnp.float32)
    position_rank = jnp.sum(earlier * target_hot, axis=1).astype(jnp.int32)
    return target * capacity + position_rank


def plain_shards(images, destinations, group_ids, offsets, inv_noise, ctf_table, references):
    dom_size = lax.axis_size("dom")
    cls_size = lax.axis_size("cls")
    local_count = images.shape[0]
    shift_count = offsets.shape[0]
    group_count = ctf_table.shape[0]
    class_count = references.shape[0]
    capacity = 2 * local_count // dom_size
    slot_count = dom_size * capacity
    class_rows = lax.all_gather(references, "cls", axis=0, tiled=True)
    every_ref = lax.all_gather(class_rows, "dom", axis=1, tiled=True)
    slot_of = slots_of(destinations[:, 0], dom_size, capacity)
    chosen = (jnp.arange(slot_count, dtype=jnp.int32)[:, None] == slot_of[None, :]).astype(
        jnp.float32
    )
    group_hot = (group_ids[:, None] == jnp.arange(group_count, dtype=jnp.int32)[None, :]).astype(
        jnp.float32
    )
    noise_ctf = inv_noise[None, :] * ctf_table * ctf_table
    noise_terms = jnp.concatenate([noise_ctf, noise_ctf], axis=1)
    shifted = shifted_rows(images, group_hot, offsets, inv_noise, ctf_table)
    contract = (((1,), (1,)), ((), ()))
    cross = lax.dot_general(shifted, every_ref, contract, preferred_element_type=jnp.float32)
    ref_float = every_ref.astype(jnp.float32)
    norms = lax.dot_general(
        noise_terms,
        ref_float * ref_float,
        contract,
        precision=lax.Precision.HIGHEST,
        preferred_element_type=jnp.float32,
    )
    selected = jnp.dot(
        group_hot, norms, precision=lax.Precision.HIGHEST, preferred_element_type=jnp.float32
    )
    scores = cross.reshape(shift_count, local_count, -1) - 0.5 * selected[None, :, :]
    row_peak = jnp.max(scores, axis=(0, 2))
    weights = jnp.exp(scores - row_peak[None, :, None])
    row_total = jnp.sum(weights, axis=(0, 2))
    log_norm = row_peak + jnp.log(row_total)
    posterior = jnp.sum(weights, axis=0) / row_total[:, None]
    posterior = posterior.reshape(local_count, cls_size, class_count)
    spread = jnp.broadcast_to(log_norm[:, None, None], (local_count, cls_size, 1))
    rows = jnp.concatenate([posterior, spread], axis=2).reshape(local_count, -1)
    slots = jnp.dot(
        chosen, rows, precision=lax.Precision.HIGHEST, preferred_element_type=jnp.float32
    )
    blocks = slots.reshape(dom_size, capacity, cls_size, class_count + 1).transpose(0, 2, 1, 3)
    blocks = blocks.reshape(dom_size * cls_size, capacity, class_count + 1)
    blocks = lax.all_to_all(blocks, ("dom", "cls"), split_axis=0, concat_axis=0, tiled=True)
    blocks = blocks.reshape(dom_size, cls_size, capacity, class_count + 1).transpose(1, 0, 2, 3)
    blocks = blocks.reshape(cls_size * slot_count, class_count + 1)
    return (blocks[:, :class_count], blocks[:, class_count])


MESH = pl.DeviceIdType.MESH
NT_DIMS = (((1,), (1,)), ((), ()))


def three_parts(value):
    high = value.astype(jnp.bfloat16)
    rest = value - high.astype(jnp.float32)
    middle = rest.astype(jnp.bfloat16)
    low = (rest - middle.astype(jnp.float32)).astype(jnp.bfloat16)
    return [high, middle, low]


def quarter_turns(turns):
    quarter, eighth = SIDE // 4, SIDE // 8
    quadrant = (turns + eighth) // quarter
    angle = (turns - quadrant * quarter).astype(jnp.float32) * (2.0 * math.pi / SIDE)
    square = angle * angle
    sine = 1.0 / 362880.0
    for term in (-1.0 / 5040.0, 1.0 / 120.0, -1.0 / 6.0, 1.0):
        sine = sine * square + term
    sine = sine * angle
    cosine = -1.0 / 3628800.0
    for term in (1.0 / 40320.0, -1.0 / 720.0, 1.0 / 24.0, -0.5, 1.0):
        cosine = cosine * square + term
    quadrant = quadrant & 3
    odd = (quadrant & 1) == 1
    first = jnp.where(odd, sine, cosine)
    second = jnp.where(odd, cosine, sine)
    return (
        jnp.where((quadrant == 1) | (quadrant == 2), -first, first),
        jnp.where(quadrant >= 2, -second, second),
    )


def e_step_kernel(
    dom_size,
    cls_size,
    offsets_ref,
    images_hbm,
    target_ref,
    group_ref,
    inv_noise_hbm,
    ctf_hbm,
    refs_hbm,
    landed,
    images_ref,
    inv_noise_ref,
    ctf_ref,
    refs_ref,
    held,
    shifted,
    ctf_parts,
    cosines,
    sines,
    cross,
    norms,
    slot_hot,
    group_hot_rows,
    stage,
    load_sem,
    send_sem,
    recv_sem,
    post_send,
    post_recv,
    own_sem,
):
    z_size = dom_size // 2
    class_count, block_columns = refs_ref.shape
    half_columns = block_columns // 2
    padded = held.shape[3]
    local_count = images_ref.shape[0]
    kept = inv_noise_ref.shape[1]
    group_count = ctf_ref.shape[0]
    shift_count = offsets_ref.shape[1]
    slot_count = slot_hot.shape[0]
    capacity = slot_count // dom_size
    piece_rows, lanes = stage.shape[2:]
    group_size = lanes // capacity
    dom = lax.axis_index("dom")
    cls = lax.axis_index("cls")
    z, x = dom // 2, dom % 2
    y, core = cls // 2, cls % 2

    loads = [
        pltpu.make_async_copy(source, place, load_sem.at[index])
        for index, (source, place) in enumerate(
            [
                (refs_hbm, refs_ref),
                (ctf_hbm, ctf_ref),
                (inv_noise_hbm, inv_noise_ref),
                (images_hbm, images_ref),
            ]
        )
    ]
    for load in loads:
        load.start()
    barrier = pltpu.get_barrier_semaphore()
    partners = [
        (lax.rem(dom + i, dom_size), lax.rem(cls + j, cls_size))
        for i in sorted(range(dom_size), key=lambda i: (abs(i - dom_size // 2), i))
        for j in range(cls_size)
        if i or j
    ]
    for partner in partners:
        pl.semaphore_signal(barrier, inc=1, device_id=partner, device_id_type=MESH)

    for load in loads[:3]:
        load.wait()
    wide = refs_ref[...].astype(jnp.float32)
    squares = jnp.concatenate(
        [wide * wide, jnp.zeros((padded - class_count, block_columns), jnp.float32)], axis=0
    )
    high = squares.astype(jnp.bfloat16)
    rest = (squares - high.astype(jnp.float32)).astype(jnp.bfloat16)
    low = pl.multiple_of(lax.rem(dom * block_columns, kept), block_columns)
    own_ctf = ctf_ref[:, pl.ds(low, block_columns)]
    noise_terms = inv_noise_ref[:, pl.ds(low, block_columns)] * own_ctf * own_ctf
    sums = lax.dot_general(
        jnp.concatenate(three_parts(noise_terms), axis=0),
        jnp.concatenate([high, rest], axis=0),
        NT_DIMS,
        preferred_element_type=jnp.float32,
    )
    sums = sums[:, :padded] + sums[:, padded:]
    own_norms = (
        sums[:group_count] + sums[group_count : 2 * group_count] + sums[2 * group_count :]
    )
    tail = jnp.concatenate(
        [part.astype(jnp.float32) for part in three_parts(own_norms)]
        + [jnp.zeros((group_count, half_columns - 3 * padded), jnp.float32)],
        axis=1,
    )
    for half in range(2):
        rows = wide[:, half * half_columns : (half + 1) * half_columns]
        extra = padded - class_count
        block = jnp.concatenate([rows, tail[half * extra : (half + 1) * extra]], axis=0)
        held[half, dom, cls] = block.astype(jnp.bfloat16)
    pl.semaphore_wait(barrier, len(partners))

    sends = []

    def block_copy(half, block_dom, block_cls, device, index):
        halves, sem = (slice(None), 0) if half is None else (half, half)
        block = held.at[halves, block_dom, block_cls]
        return pltpu.make_async_remote_copy(
            src_ref=block,
            dst_ref=block,
            send_sem=send_sem.at[index],
            recv_sem=recv_sem.at[sem, block_dom, block_cls],
            device_id=device,
            device_id_type=MESH,
        )

    def send(half, block_dom, block_cls, device):
        copy = block_copy(half, block_dom, block_cls, device, len(sends))
        copy.start()
        sends.append(copy)

    def arrived(half, block_dom, block_cls):
        block_copy(half, block_dom, block_cls, over_core, 0).wait_recv()

    def z_partner(step):
        other, bit = z, 1
        while bit < z_size:
            if step & bit:
                other = other + bit - 2 * bit * ((z // bit) % 2)
            bit *= 2
        return other

    over_x = (z * 2 + (1 - x), cls)
    over_y = (dom, (1 - y) * 2 + core)
    over_core = (dom, y * 2 + (1 - core))

    send(0, dom, cls, over_x)
    send(1, dom, cls, over_y)
    for step in range(1, min(2, z_size)):
        send(None, dom, cls, (z_partner(step) * 2 + x, cls))
    send(1, dom, cls, over_x)
    send(0, dom, cls, over_y)
    for step in range(2, z_size):
        send(None, dom, cls, (z_partner(step) * 2 + x, cls))
    send(None, dom, cls, over_core)

    table_shape = (cosines.shape[0], kept)
    freq = lax.broadcasted_iota(jnp.int32, table_shape, 1)
    shift_row = lax.broadcasted_iota(jnp.int32, table_shape, 0)
    half_side = SIDE // 2
    row_freq = freq // half_side
    col_freq = freq % half_side
    row_freq = jnp.where(row_freq >= half_side, row_freq - SIDE, row_freq)
    turns = jnp.zeros(table_shape, jnp.int32)
    for t in range(shift_count):
        turn = offsets_ref[0, t] * row_freq + offsets_ref[1, t] * col_freq
        turns = jnp.where(shift_row == t, turn & (SIDE - 1), turns)
    cosines[...], sines[...] = quarter_turns(turns)
    for index, part in enumerate(three_parts(ctf_ref[...])):
        ctf_parts[index * group_count : (index + 1) * group_count, :] = part
    square = (local_count, local_count)
    sub = lax.broadcasted_iota(jnp.int32, square, 0)
    lane = lax.broadcasted_iota(jnp.int32, square, 1)
    group_row = group_ref[...]
    group_col = jnp.sum(jnp.where(sub == lane, group_row, 0), axis=1, keepdims=True)
    part_lane = lax.broadcasted_iota(jnp.int32, (local_count, 3 * group_count), 1)
    group_hot = jnp.where(part_lane % group_count == group_col, 1.0, 0.0).astype(jnp.bfloat16)

    chunk = kept // 4

    def shift_chunk(step):
        low = step * chunk
        columns = slice(low, low + chunk)
        imag_columns = slice(kept + low, kept + low + chunk)
        weight = inv_noise_ref[:, columns] * jnp.dot(
            group_hot, ctf_parts[:, columns], preferred_element_type=jnp.float32
        )
        real_part = images_ref[:, columns].astype(jnp.float32)
        imag_part = images_ref[:, imag_columns].astype(jnp.float32)
        for t in range(shift_count):
            cosine = cosines[t : t + 1, columns]
            sine = sines[t : t + 1, columns]
            rows = slice(t * local_count, (t + 1) * local_count)
            shifted[rows, columns] = (
                weight * (real_part * cosine - imag_part * sine)
            ).astype(jnp.bfloat16)
            shifted[rows, imag_columns] = (
                weight * (real_part * sine + imag_part * cosine)
            ).astype(jnp.bfloat16)

    hot_rows = lax.broadcasted_iota(jnp.int32, group_hot_rows.shape, 0)
    group_hot_rows[...] = jnp.where(hot_rows % group_count == group_row, 1.0, 0.0).astype(
        jnp.bfloat16
    )
    target_row = target_ref[...]
    target_col = jnp.sum(jnp.where(sub == lane, target_row, 0), axis=1, keepdims=True)
    ahead = (target_col == target_row) & (sub < lane)
    rank = jnp.sum(jnp.where(ahead, 1, 0), axis=0, keepdims=True)
    slot_of = target_row * capacity + rank
    slot = lax.broadcasted_iota(jnp.int32, (slot_count, local_count), 0)
    hot = jnp.where(slot == slot_of, 1.0, 0.0).astype(jnp.bfloat16)
    for index in range(3):
        slot_hot[:, index * local_count : (index + 1) * local_count] = hot
    cross[...] = jnp.zeros_like(cross)
    norms[...] = jnp.zeros_like(norms)

    def from_z(step):
        block = z_partner(step) * 2 + x
        arrived(None, block, cls)
        send(0, block, cls, over_x)
        send(1, block, cls, over_y)
        send(1, block, cls, over_x)
        send(0, block, cls, over_y)
        send(None, block, cls, over_core)

    def from_first(step):
        near, far = z_partner(step) * 2 + x, z_partner(step) * 2 + (1 - x)
        arrived(0, far, cls)
        if step % 2 == 0:
            send(0, far, cls, over_y)
        arrived(1, near, over_y[1])
        if step % 2 == 0:
            send(1, near, over_y[1], over_x)
        send(0, far, cls, over_core)
        send(1, near, over_y[1], over_core)

    def from_last(step):
        near, far = z_partner(step) * 2 + x, z_partner(step) * 2 + (1 - x)
        arrived(0, near, over_y[1])
        send(0, near, over_y[1], over_core)
        arrived(1, far, cls)
        send(1, far, cls, over_core)
        if step % 2 == 0:
            arrived(0, far, over_y[1])
            arrived(1, far, over_y[1])
            if z_size > 1:
                send(None, far, over_y[1], (z_partner(1) * 2 + x, cls))
        else:
            arrived(None, far, over_y[1])
        send(None, far, over_y[1], over_core)

    sibling, far_sibling = over_core[1], (1 - y) * 2 + (1 - core)

    def add_block(block_dom):
        rows = jnp.concatenate(
            [held[half, block_dom].reshape(cls_size * padded, half_columns) for half in range(2)],
            axis=1,
        )
        low = pl.multiple_of(block_dom * block_columns, block_columns)
        cross[...] += lax.dot_general(
            rows, shifted[:, pl.ds(low, block_columns)], NT_DIMS, preferred_element_type=jnp.float32
        )
        for half in range(2):
            last_rows = held[half, block_dom, :, padded - 16 : padded, :].astype(jnp.float32)
            norms[half] += last_rows[:, 8:16, :]

    def multiply(step):
        while chunks:
            shift_chunk(chunks.pop(0))
        near, far = z_partner(step) * 2 + x, z_partner(step) * 2 + (1 - x)
        arrived(None, near, sibling)
        arrived(0, near, far_sibling)
        arrived(1, near, far_sibling)
        add_block(near)
        arrived(0, far, sibling)
        arrived(1, far, sibling)
        arrived(None, far, far_sibling)
        add_block(far)

    chunks = list(range(4))
    loads[3].wait()
    shift_chunk(chunks.pop(0))
    for step in range(z_size + 2):
        if 0 < step < z_size:
            from_z(step)
        if step == 1:
            shift_chunk(chunks.pop(0))
        if step >= 2:
            multiply(step - 2)
        if step < z_size:
            from_first(step)
        if step == 1:
            shift_chunk(chunks.pop(0))
        if 0 < step <= z_size:
            from_last(step - 1)

    selected = []
    for block in range(cls_size):
        both = jnp.concatenate([norms[0, block], norms[1, block]], axis=0)
        total_norm = sum(both[:, p * padded : (p + 1) * padded] for p in range(3))
        selected.append(
            lax.dot_general(
                jnp.concatenate(three_parts(total_norm), axis=0),
                group_hot_rows[...],
                (((0,), (0,)), ((), ())),
                preferred_element_type=jnp.float32,
            )
        )
    selected = 0.5 * jnp.concatenate(selected, axis=0)
    row = lax.broadcasted_iota(jnp.int32, (cls_size * padded, local_count), 0) % padded
    real_row = row < class_count
    scores = []
    for t in range(shift_count):
        value = cross[:, t * local_count : (t + 1) * local_count] - selected
        scores.append(jnp.where(real_row, value, -jnp.inf))
    peak = functools.reduce(jnp.maximum, scores)
    peak = jnp.max(peak, axis=0, keepdims=True)
    weights = functools.reduce(jnp.add, [jnp.exp(value - peak) for value in scores])
    total = jnp.sum(weights, axis=0, keepdims=True)
    log_norm = peak + jnp.log(total)
    table = jnp.where(row == class_count, log_norm, weights / total)

    slots = lax.dot_general(
        jnp.concatenate(three_parts(table), axis=1),
        slot_hot[...],
        NT_DIMS,
        preferred_element_type=jnp.float32,
    )
    lane_group = lax.broadcasted_iota(jnp.int32, (8, lanes), 1) // capacity
    whole = class_count // (8 * group_size)
    left_over = (class_count - whole * 8 * group_size) // group_size

    def turned(value, groups):
        amount = groups % group_size * capacity
        return pltpu.roll(value, amount, 1) if amount else value

    def lifted(value, rows):
        return pltpu.roll(value, rows % 8, 0) if rows % 8 else value

    def side_by_side(values):
        result = values[0]
        for k in range(1, group_size):
            result = jnp.where(lane_group == k, values[k], result)
        return result

    sub_row = lax.broadcasted_iota(jnp.int32, (8, lanes), 0)
    for block in range(cls_size):
        part = slots[block * padded : (block + 1) * padded]
        for to_dom in range(dom_size):
            place, member = to_dom // group_size, to_dom % group_size
            tile = part[:, place * lanes : (place + 1) * lanes]
            for w in range(whole):
                values = []
                for k in range(group_size):
                    top = 8 * (k * whole + w)
                    values.append(turned(tile[top : top + 8], k - member))
                stage[to_dom, block, 8 * w : 8 * w + 8, :] = side_by_side(values)
            rest = tile[8 * whole * group_size : class_count]
            values = [
                turned(lifted(rest, -left_over * k), k - member) for k in range(group_size)
            ]
            norm_row = lifted(turned(tile[class_count:padded], -member), left_over)
            mixed = jnp.where(sub_row < left_over, side_by_side(values), norm_row)
            stage[to_dom, block, 8 * whole : piece_rows, :] = mixed[: piece_rows - 8 * whole]

    posts = []
    for index, (to_dom, to_cls) in enumerate(partners):
        copy = pltpu.make_async_remote_copy(
            src_ref=stage.at[to_dom, to_cls],
            dst_ref=landed.at[cls, dom],
            send_sem=post_send.at[index],
            recv_sem=post_recv.at[cls, dom],
            device_id=(to_dom, to_cls),
            device_id_type=MESH,
        )
        copy.start()
        posts.append(copy)
    own = pltpu.make_async_copy(stage.at[dom, cls], landed.at[cls, dom], own_sem)
    own.start()
    for copy in sends:
        copy.wait_send()
    for copy in posts:
        copy.wait_send()
    own.wait()
    for from_dom, from_cls in reversed(partners):
        pltpu.make_async_remote_copy(
            src_ref=stage.at[from_dom, from_cls],
            dst_ref=landed.at[from_cls, from_dom],
            send_sem=post_send.at[0],
            recv_sem=post_recv.at[from_cls, from_dom],
            device_id=(from_dom, from_cls),
            device_id_type=MESH,
        ).wait_recv()


def unpack_kernel(capacity, landed, out_ref, log_ref):
    dom_size, piece_rows, lanes = landed.shape[1:]
    class_count = out_ref.shape[0]
    group_size = lanes // capacity
    lane_group = lax.broadcasted_iota(jnp.int32, (8, lanes), 1) // capacity
    whole = class_count // (8 * group_size)
    left_over = (class_count - whole * 8 * group_size) // group_size

    def turned(value, groups):
        amount = groups % group_size * capacity
        return pltpu.roll(value, amount, 1) if amount else value

    def side_by_side(values):
        result = values[0]
        for k in range(1, group_size):
            result = jnp.where(lane_group == k, values[k], result)
        return result

    def pad_rows(value):
        empty = jnp.zeros((8 - value.shape[0], lanes), jnp.float32)
        return jnp.concatenate([value, empty], axis=0)

    for place in range(dom_size // group_size):
        low = place * lanes
        got = [landed[0, place * group_size + member] for member in range(group_size)]
        for k in range(group_size):
            for w in range(whole):
                top = 8 * (k * whole + w)
                out_ref[top : top + 8, low : low + lanes] = side_by_side(
                    [
                        turned(value[8 * w : 8 * w + 8], member - k)
                        for member, value in enumerate(got)
                    ]
                )
            top = 8 * whole * group_size + left_over * k
            out_ref[top : top + left_over, low : low + lanes] = side_by_side(
                [
                    turned(pad_rows(value[8 * whole :]), member - k)
                    for member, value in enumerate(got)
                ]
            )[:left_over]
        log_ref[:, low : low + lanes] = side_by_side(
            [turned(pad_rows(value[8 * whole :]), member) for member, value in enumerate(got)]
        )[left_over : left_over + 1]


def kernel_shards(images, destinations, group_ids, offsets, inv_noise, ctf_table, references):
    dom_size = lax.axis_size("dom")
    cls_size = lax.axis_size("cls")
    local_count, columns = images.shape
    kept = inv_noise.shape[0]
    group_count = ctf_table.shape[0]
    shift_count = offsets.shape[0]
    class_count, block_columns = references.shape
    slot_count = 2 * local_count
    lanes = 128
    piece_rows = class_count // (lanes // (slot_count // dom_size)) + 1
    padded = class_count + 8
    device_count = dom_size * cls_size
    table_rows = -(-shift_count // 8) * 8
    vmem = pl.BlockSpec(memory_space=pltpu.VMEM)
    hbm = pl.BlockSpec(memory_space=pltpu.HBM)
    packed = pl.pallas_call(
        functools.partial(e_step_kernel, dom_size, cls_size),
        out_shape=jax.ShapeDtypeStruct((cls_size, dom_size, piece_rows, lanes), jnp.float32),
        in_specs=[pl.BlockSpec(memory_space=pltpu.SMEM), hbm, vmem, vmem, hbm, hbm, hbm],
        out_specs=hbm,
        scratch_shapes=[
            pltpu.VMEM((local_count, columns), jnp.bfloat16),
            pltpu.VMEM((1, kept), jnp.float32),
            pltpu.VMEM((group_count, kept), jnp.float32),
            pltpu.VMEM((class_count, block_columns), jnp.bfloat16),
            pltpu.VMEM((2, dom_size, cls_size, padded, block_columns // 2), jnp.bfloat16),
            pltpu.VMEM((shift_count * local_count, columns), jnp.bfloat16),
            pltpu.VMEM((3 * group_count, kept), jnp.bfloat16),
            pltpu.VMEM((table_rows, kept), jnp.float32),
            pltpu.VMEM((table_rows, kept), jnp.float32),
            pltpu.VMEM((cls_size * padded, shift_count * local_count), jnp.float32),
            pltpu.VMEM((2, cls_size, 8, block_columns // 2), jnp.float32),
            pltpu.VMEM((slot_count, 3 * local_count), jnp.bfloat16),
            pltpu.VMEM((3 * group_count, local_count), jnp.bfloat16),
            pltpu.VMEM((dom_size, cls_size, piece_rows, lanes), jnp.float32),
            pltpu.SemaphoreType.DMA((4,)),
            pltpu.SemaphoreType.DMA((2 * device_count + dom_size,)),
            pltpu.SemaphoreType.DMA((2, dom_size, cls_size)),
            pltpu.SemaphoreType.DMA((device_count,)),
            pltpu.SemaphoreType.DMA((cls_size, dom_size)),
            pltpu.SemaphoreType.DMA,
        ],
        compiler_params=pltpu.CompilerParams(
            collective_id=0, has_side_effects=True, vmem_limit_bytes=56 * 1024 * 1024
        ),
    )(
        offsets.T,
        images,
        destinations.T,
        group_ids[None, :],
        inv_noise[None, :],
        ctf_table,
        references,
    )
    posteriors, log_norms = pl.pallas_call(
        functools.partial(unpack_kernel, slot_count // dom_size),
        out_shape=(
            jax.ShapeDtypeStruct((class_count, cls_size * slot_count), jnp.float32),
            jax.ShapeDtypeStruct((1, cls_size * slot_count), jnp.float32),
        ),
        grid=(cls_size,),
        in_specs=[pl.BlockSpec((1, dom_size, piece_rows, lanes), lambda c: (c, 0, 0, 0))],
        out_specs=(
            pl.BlockSpec((class_count, slot_count), lambda c: (0, c)),
            pl.BlockSpec((1, slot_count), lambda c: (0, c)),
        ),
    )(packed)
    return (posteriors.T, log_norms[0])


def fits_kernel(mesh, images, ctf_table, references):
    dom_size, cls_size = mesh.shape["dom"], mesh.shape["cls"]
    local_count = images.shape[0] // (dom_size * cls_size)
    capacity = 2 * local_count // dom_size
    class_count = references.shape[0] // cls_size
    half_columns = references.shape[1] // dom_size // 2
    if cls_size != 4 or dom_size % 2 or local_count != 128 or 128 % capacity:
        return False
    group_size = 128 // capacity
    return (
        group_size > 1
        and dom_size % group_size == 0
        and class_count % 8 == 0
        and class_count % (8 * group_size) == 8
        and 8 // group_size * group_size == 8
        and 8 // group_size < 8
        and dom_size & (dom_size - 1) == 0
        and (class_count + 8) % 16 == 0
        and half_columns % 128 == 0
        and 3 * (class_count + 8) < half_columns
        and ctf_table.shape[0] == 16
    )


def solution(mesh):
    def e_step(*arrays):
        shards = kernel_shards if fits_kernel(mesh, arrays[0], arrays[-2], arrays[-1]) else plain_shards
        return mapped(mesh, shards)(*arrays)

    return e_step


def mapped(mesh, shards):
    return jax.shard_map(
        shards,
        mesh=mesh,
        in_specs=(
            P(("dom", "cls"), None),
            P(("dom", "cls"), None),
            P(("dom", "cls")),
            P(),
            P(),
            P(),
            P("cls", "dom"),
        ),
        out_specs=(P("dom", "cls"), P("dom")),
        check_vma=False,
    )
```

```python
import functools
import math

import jax
import jax.numpy as jnp
from jax import lax
from jax.experimental import pallas as pl
from jax.experimental.pallas import tpu as pltpu
from jax.sharding import PartitionSpec as P

SIDE = 64


def phase_tables(offsets, kept):
    freq_index = jnp.arange(kept, dtype=jnp.int32)
    half_side = SIDE // 2
    row_freq = freq_index // half_side
    col_freq = freq_index % half_side
    row_freq = jnp.where(row_freq >= half_side, row_freq - SIDE, row_freq)
    turns = jnp.mod(offsets[:, 0:1] * row_freq[None, :] + offsets[:, 1:2] * col_freq[None, :], SIDE)
    angles = turns.astype(jnp.float32) * (2.0 * math.pi / SIDE)
    return (jnp.cos(angles), jnp.sin(angles))


def shifted_rows(images, group_hot, offsets, inv_noise, ctf_table):
    kept = inv_noise.shape[0]
    cosines, sines = phase_tables(offsets, kept)
    ctf_rows = jnp.dot(
        group_hot, ctf_table, precision=lax.Precision.HIGHEST, preferred_element_type=jnp.float32
    )
    weight = inv_noise[None, :] * ctf_rows
    real_part = images[:, :kept].astype(jnp.float32)
    imag_part = images[:, kept:].astype(jnp.float32)
    pieces = []
    for shift_index in range(offsets.shape[0]):
        cosine = cosines[shift_index][None, :]
        sine = sines[shift_index][None, :]
        both = jnp.concatenate(
            [
                weight * (real_part * cosine - imag_part * sine),
                weight * (real_part * sine + imag_part * cosine),
            ],
            axis=1,
        )
        pieces.append(both.astype(jnp.bfloat16))
    return jnp.concatenate(pieces, axis=0)


def slots_of(target, dom_size, capacity):
    local_count = target.shape[0]
    target_hot = (target[:, None] == jnp.arange(dom_size, dtype=jnp.int32)[None, :]).astype(
        jnp.float32
    )
    local_index = jnp.arange(local_count, dtype=jnp.int32)
    lower = (local_index[:, None] > local_index[None, :]).astype(jnp.float32)
    earlier = jnp.dot(lower, target_hot, preferred_element_type=jnp.float32)
    position_rank = jnp.sum(earlier * target_hot, axis=1).astype(jnp.int32)
    return target * capacity + position_rank


def plain_shards(images, destinations, group_ids, offsets, inv_noise, ctf_table, references):
    dom_size = lax.axis_size("dom")
    cls_size = lax.axis_size("cls")
    local_count = images.shape[0]
    shift_count = offsets.shape[0]
    group_count = ctf_table.shape[0]
    class_count = references.shape[0]
    capacity = 2 * local_count // dom_size
    slot_count = dom_size * capacity
    class_rows = lax.all_gather(references, "cls", axis=0, tiled=True)
    every_ref = lax.all_gather(class_rows, "dom", axis=1, tiled=True)
    slot_of = slots_of(destinations[:, 0], dom_size, capacity)
    chosen = (jnp.arange(slot_count, dtype=jnp.int32)[:, None] == slot_of[None, :]).astype(
        jnp.float32
    )
    group_hot = (group_ids[:, None] == jnp.arange(group_count, dtype=jnp.int32)[None, :]).astype(
        jnp.float32
    )
    noise_ctf = inv_noise[None, :] * ctf_table * ctf_table
    noise_terms = jnp.concatenate([noise_ctf, noise_ctf], axis=1)
    shifted = shifted_rows(images, group_hot, offsets, inv_noise, ctf_table)
    contract = (((1,), (1,)), ((), ()))
    cross = lax.dot_general(shifted, every_ref, contract, preferred_element_type=jnp.float32)
    ref_float = every_ref.astype(jnp.float32)
    norms = lax.dot_general(
        noise_terms,
        ref_float * ref_float,
        contract,
        precision=lax.Precision.HIGHEST,
        preferred_element_type=jnp.float32,
    )
    selected = jnp.dot(
        group_hot, norms, precision=lax.Precision.HIGHEST, preferred_element_type=jnp.float32
    )
    scores = cross.reshape(shift_count, local_count, -1) - 0.5 * selected[None, :, :]
    row_peak = jnp.max(scores, axis=(0, 2))
    weights = jnp.exp(scores - row_peak[None, :, None])
    row_total = jnp.sum(weights, axis=(0, 2))
    log_norm = row_peak + jnp.log(row_total)
    posterior = jnp.sum(weights, axis=0) / row_total[:, None]
    posterior = posterior.reshape(local_count, cls_size, class_count)
    spread = jnp.broadcast_to(log_norm[:, None, None], (local_count, cls_size, 1))
    rows = jnp.concatenate([posterior, spread], axis=2).reshape(local_count, -1)
    slots = jnp.dot(
        chosen, rows, precision=lax.Precision.HIGHEST, preferred_element_type=jnp.float32
    )
    blocks = slots.reshape(dom_size, capacity, cls_size, class_count + 1).transpose(0, 2, 1, 3)
    blocks = blocks.reshape(dom_size * cls_size, capacity, class_count + 1)
    blocks = lax.all_to_all(blocks, ("dom", "cls"), split_axis=0, concat_axis=0, tiled=True)
    blocks = blocks.reshape(dom_size, cls_size, capacity, class_count + 1).transpose(1, 0, 2, 3)
    blocks = blocks.reshape(cls_size * slot_count, class_count + 1)
    return (blocks[:, :class_count], blocks[:, class_count])


MESH = pl.DeviceIdType.MESH
NT_DIMS = (((1,), (1,)), ((), ()))


def three_parts(value):
    high = value.astype(jnp.bfloat16)
    rest = value - high.astype(jnp.float32)
    middle = rest.astype(jnp.bfloat16)
    low = (rest - middle.astype(jnp.float32)).astype(jnp.bfloat16)
    return [high, middle, low]


def quarter_turns(turns):
    quarter, eighth = SIDE // 4, SIDE // 8
    quadrant = (turns + eighth) // quarter
    angle = (turns - quadrant * quarter).astype(jnp.float32) * (2.0 * math.pi / SIDE)
    square = angle * angle
    sine = 1.0 / 362880.0
    for term in (-1.0 / 5040.0, 1.0 / 120.0, -1.0 / 6.0, 1.0):
        sine = sine * square + term
    sine = sine * angle
    cosine = -1.0 / 3628800.0
    for term in (1.0 / 40320.0, -1.0 / 720.0, 1.0 / 24.0, -0.5, 1.0):
        cosine = cosine * square + term
    quadrant = quadrant & 3
    odd = (quadrant & 1) == 1
    first = jnp.where(odd, sine, cosine)
    second = jnp.where(odd, cosine, sine)
    return (
        jnp.where((quadrant == 1) | (quadrant == 2), -first, first),
        jnp.where(quadrant >= 2, -second, second),
    )


def e_step_kernel(
    dom_size,
    cls_size,
    offsets_ref,
    images_hbm,
    target_ref,
    group_ref,
    inv_noise_hbm,
    ctf_hbm,
    refs_hbm,
    landed,
    images_ref,
    inv_noise_ref,
    ctf_ref,
    refs_ref,
    held,
    shifted,
    ctf_parts,
    cosines,
    sines,
    cross,
    norms,
    slot_hot,
    group_hot_rows,
    slots_ref,
    stage,
    load_sem,
    send_sem,
    recv_sem,
    post_send,
    post_recv,
    own_sem,
):
    z_size = dom_size // 2
    class_count, block_columns = refs_ref.shape
    half_columns = block_columns // 2
    padded = held.shape[3]
    local_count = images_ref.shape[0]
    kept = inv_noise_ref.shape[1]
    group_count = ctf_ref.shape[0]
    shift_count = offsets_ref.shape[1]
    slot_count = slot_hot.shape[0]
    capacity = slot_count // dom_size
    piece_rows, lanes = stage.shape[2:]
    group_size = lanes // capacity
    dom = lax.axis_index("dom")
    cls = lax.axis_index("cls")
    z, x = dom // 2, dom % 2
    y, core = cls // 2, cls % 2

    loads = [
        pltpu.make_async_copy(source, place, load_sem.at[index])
        for index, (source, place) in enumerate(
            [
                (refs_hbm, refs_ref),
                (ctf_hbm, ctf_ref),
                (inv_noise_hbm, inv_noise_ref),
                (images_hbm, images_ref),
            ]
        )
    ]
    for load in loads:
        load.start()
    barrier = pltpu.get_barrier_semaphore()
    partners = [
        [
            (lax.rem(dom + i, dom_size), lax.rem(cls + j, cls_size))
            for i in sorted(range(dom_size), key=lambda i: (abs(i - dom_size // 2), i))
            if i or j
        ]
        for j in range(cls_size)
    ]
    every_partner = sum(partners, [])
    for partner in every_partner:
        pl.semaphore_signal(barrier, inc=1, device_id=partner, device_id_type=MESH)

    for load in loads[:3]:
        load.wait()
    wide = refs_ref[...].astype(jnp.float32)
    squares = jnp.concatenate(
        [wide * wide, jnp.zeros((padded - class_count, block_columns), jnp.float32)], axis=0
    )
    high = squares.astype(jnp.bfloat16)
    rest = (squares - high.astype(jnp.float32)).astype(jnp.bfloat16)
    low = pl.multiple_of(lax.rem(dom * block_columns, kept), block_columns)
    own_ctf = ctf_ref[:, pl.ds(low, block_columns)]
    noise_terms = inv_noise_ref[:, pl.ds(low, block_columns)] * own_ctf * own_ctf
    sums = lax.dot_general(
        jnp.concatenate(three_parts(noise_terms), axis=0),
        jnp.concatenate([high, rest], axis=0),
        NT_DIMS,
        preferred_element_type=jnp.float32,
    )
    sums = sums[:, :padded] + sums[:, padded:]
    own_norms = (
        sums[:group_count] + sums[group_count : 2 * group_count] + sums[2 * group_count :]
    )
    tail = jnp.concatenate(
        [part.astype(jnp.float32) for part in three_parts(own_norms)]
        + [jnp.zeros((group_count, half_columns - 3 * padded), jnp.float32)],
        axis=1,
    )
    for half in range(2):
        rows = wide[:, half * half_columns : (half + 1) * half_columns]
        extra = padded - class_count
        block = jnp.concatenate([rows, tail[half * extra : (half + 1) * extra]], axis=0)
        held[half, dom, cls] = block.astype(jnp.bfloat16)
    pl.semaphore_wait(barrier, len(every_partner))

    sends = []

    def block_copy(half, block_dom, block_cls, device, index):
        halves, sem = (slice(None), 0) if half is None else (half, half)
        block = held.at[halves, block_dom, block_cls]
        return pltpu.make_async_remote_copy(
            src_ref=block,
            dst_ref=block,
            send_sem=send_sem.at[index],
            recv_sem=recv_sem.at[sem, block_dom, block_cls],
            device_id=device,
            device_id_type=MESH,
        )

    def send(half, block_dom, block_cls, device):
        copy = block_copy(half, block_dom, block_cls, device, len(sends))
        copy.start()
        sends.append(copy)

    def arrived(half, block_dom, block_cls):
        block_copy(half, block_dom, block_cls, over_core, 0).wait_recv()

    def z_partner(step):
        other, bit = z, 1
        while bit < z_size:
            if step & bit:
                other = other + bit - 2 * bit * ((z // bit) % 2)
            bit *= 2
        return other

    over_x = (z * 2 + (1 - x), cls)
    over_y = (dom, (1 - y) * 2 + core)
    over_core = (dom, y * 2 + (1 - core))

    send(0, dom, cls, over_x)
    send(1, dom, cls, over_y)
    for step in range(1, min(2, z_size)):
        send(None, dom, cls, (z_partner(step) * 2 + x, cls))
    send(1, dom, cls, over_x)
    send(0, dom, cls, over_y)
    for step in range(2, z_size):
        send(None, dom, cls, (z_partner(step) * 2 + x, cls))
    send(None, dom, cls, over_core)

    table_shape = (cosines.shape[0], kept)
    freq = lax.broadcasted_iota(jnp.int32, table_shape, 1)
    shift_row = lax.broadcasted_iota(jnp.int32, table_shape, 0)
    half_side = SIDE // 2
    row_freq = freq // half_side
    col_freq = freq % half_side
    row_freq = jnp.where(row_freq >= half_side, row_freq - SIDE, row_freq)
    turns = jnp.zeros(table_shape, jnp.int32)
    for t in range(shift_count):
        turn = offsets_ref[0, t] * row_freq + offsets_ref[1, t] * col_freq
        turns = jnp.where(shift_row == t, turn & (SIDE - 1), turns)
    cosines[...], sines[...] = quarter_turns(turns)
    for index, part in enumerate(three_parts(ctf_ref[...])):
        ctf_parts[index * group_count : (index + 1) * group_count, :] = part
    square = (local_count, local_count)
    sub = lax.broadcasted_iota(jnp.int32, square, 0)
    lane = lax.broadcasted_iota(jnp.int32, square, 1)
    group_row = group_ref[...]
    group_col = jnp.sum(jnp.where(sub == lane, group_row, 0), axis=1, keepdims=True)
    part_lane = lax.broadcasted_iota(jnp.int32, (local_count, 3 * group_count), 1)
    group_hot = jnp.where(part_lane % group_count == group_col, 1.0, 0.0).astype(jnp.bfloat16)

    chunk = kept // 4

    def shift_chunk(step):
        low = step * chunk
        columns = slice(low, low + chunk)
        imag_columns = slice(kept + low, kept + low + chunk)
        weight = inv_noise_ref[:, columns] * jnp.dot(
            group_hot, ctf_parts[:, columns], preferred_element_type=jnp.float32
        )
        real_part = images_ref[:, columns].astype(jnp.float32)
        imag_part = images_ref[:, imag_columns].astype(jnp.float32)
        for t in range(shift_count):
            cosine = cosines[t : t + 1, columns]
            sine = sines[t : t + 1, columns]
            rows = slice(t * local_count, (t + 1) * local_count)
            shifted[rows, columns] = (
                weight * (real_part * cosine - imag_part * sine)
            ).astype(jnp.bfloat16)
            shifted[rows, imag_columns] = (
                weight * (real_part * sine + imag_part * cosine)
            ).astype(jnp.bfloat16)

    hot_rows = lax.broadcasted_iota(jnp.int32, group_hot_rows.shape, 0)
    group_hot_rows[...] = jnp.where(hot_rows % group_count == group_row, 1.0, 0.0).astype(
        jnp.bfloat16
    )
    target_row = target_ref[...]
    target_col = jnp.sum(jnp.where(sub == lane, target_row, 0), axis=1, keepdims=True)
    ahead = (target_col == target_row) & (sub < lane)
    rank = jnp.sum(jnp.where(ahead, 1, 0), axis=0, keepdims=True)
    slot_of = target_row * capacity + rank
    slot = lax.broadcasted_iota(jnp.int32, (slot_count, local_count), 0)
    hot = jnp.where(slot == slot_of, 1.0, 0.0).astype(jnp.bfloat16)
    for index in range(3):
        slot_hot[:, index * local_count : (index + 1) * local_count] = hot
    cross[...] = jnp.zeros_like(cross)
    norms[...] = jnp.zeros_like(norms)

    def from_z(step):
        block = z_partner(step) * 2 + x
        arrived(None, block, cls)
        send(0, block, cls, over_x)
        send(1, block, cls, over_y)
        send(1, block, cls, over_x)
        send(0, block, cls, over_y)
        send(None, block, cls, over_core)

    def from_first(step):
        near, far = z_partner(step) * 2 + x, z_partner(step) * 2 + (1 - x)
        arrived(0, far, cls)
        if step % 2 == 0:
            send(0, far, cls, over_y)
        arrived(1, near, over_y[1])
        if step % 2 == 0:
            send(1, near, over_y[1], over_x)
        send(0, far, cls, over_core)
        send(1, near, over_y[1], over_core)

    def from_last(step):
        near, far = z_partner(step) * 2 + x, z_partner(step) * 2 + (1 - x)
        arrived(0, near, over_y[1])
        send(0, near, over_y[1], over_core)
        arrived(1, far, cls)
        send(1, far, cls, over_core)
        if step % 2 == 0:
            arrived(0, far, over_y[1])
            arrived(1, far, over_y[1])
            if z_size > 1:
                send(None, far, over_y[1], (z_partner(1) * 2 + x, cls))
        else:
            arrived(None, far, over_y[1])
        send(None, far, over_y[1], over_core)

    sibling, far_sibling = over_core[1], (1 - y) * 2 + (1 - core)

    def add_block(block_dom):
        rows = jnp.concatenate(
            [held[half, block_dom].reshape(cls_size * padded, half_columns) for half in range(2)],
            axis=1,
        )
        low = pl.multiple_of(block_dom * block_columns, block_columns)
        cross[...] += lax.dot_general(
            rows, shifted[:, pl.ds(low, block_columns)], NT_DIMS, preferred_element_type=jnp.float32
        )
        for half in range(2):
            last_rows = held[half, block_dom, :, padded - 16 : padded, :].astype(jnp.float32)
            norms[half] += last_rows[:, 8:16, :]

    def multiply_near(step):
        while chunks:
            shift_chunk(chunks.pop(0))
        near = z_partner(step) * 2 + x
        arrived(None, near, sibling)
        arrived(0, near, far_sibling)
        arrived(1, near, far_sibling)
        add_block(near)

    def multiply_far(step):
        far = z_partner(step) * 2 + (1 - x)
        arrived(0, far, sibling)
        arrived(1, far, sibling)
        arrived(None, far, far_sibling)
        add_block(far)

    chunks = list(range(4))
    loads[3].wait()
    shift_chunk(chunks.pop(0))
    for step in range(z_size + 2):
        if 0 < step < z_size:
            from_z(step)
        if step == 1:
            shift_chunk(chunks.pop(0))
        if step >= 2:
            multiply_near(step - 2)
        if step < z_size:
            from_first(step)
        if step >= 2:
            multiply_far(step - 2)
        if step == 1:
            shift_chunk(chunks.pop(0))
        if 0 < step <= z_size:
            from_last(step - 1)

    selected = []
    for block in range(cls_size):
        both = jnp.concatenate([norms[0, block], norms[1, block]], axis=0)
        total_norm = sum(both[:, p * padded : (p + 1) * padded] for p in range(3))
        selected.append(
            lax.dot_general(
                jnp.concatenate(three_parts(total_norm), axis=0),
                group_hot_rows[...],
                (((0,), (0,)), ((), ())),
                preferred_element_type=jnp.float32,
            )
        )
    selected = 0.5 * jnp.concatenate(selected, axis=0)
    row = lax.broadcasted_iota(jnp.int32, (cls_size * padded, local_count), 0) % padded
    real_row = row < class_count
    scores = []
    for t in range(shift_count):
        value = cross[:, t * local_count : (t + 1) * local_count] - selected
        scores.append(jnp.where(real_row, value, -jnp.inf))
    peak = functools.reduce(jnp.maximum, scores)
    peak = jnp.max(peak, axis=0, keepdims=True)
    weights = functools.reduce(jnp.add, [jnp.exp(value - peak) for value in scores])
    total = jnp.sum(weights, axis=0, keepdims=True)
    log_norm = peak + jnp.log(total)
    table = jnp.where(row == class_count, log_norm, weights / total)

    slots_ref[...] = lax.dot_general(
        jnp.concatenate(three_parts(table), axis=1),
        slot_hot[...],
        NT_DIMS,
        preferred_element_type=jnp.float32,
    )
    lane_group = lax.broadcasted_iota(jnp.int32, (8, lanes), 1) // capacity
    whole = class_count // (8 * group_size)
    left_over = (class_count - whole * 8 * group_size) // group_size

    def turned(value, groups):
        amount = groups % group_size * capacity
        return pltpu.roll(value, amount, 1) if amount else value

    def lifted(value, rows):
        return pltpu.roll(value, rows % 8, 0) if rows % 8 else value

    def side_by_side(values):
        result = values[0]
        for k in range(1, group_size):
            result = jnp.where(lane_group == k, values[k], result)
        return result

    sub_row = lax.broadcasted_iota(jnp.int32, (8, lanes), 0)
    posts = []
    for turn in range(cls_size):
        block = lax.rem(cls + turn, cls_size)
        part = slots_ref[pl.ds(pl.multiple_of(block * padded, 16), padded), :]
        for to_dom in range(dom_size):
            place, member = to_dom // group_size, to_dom % group_size
            tile = part[:, place * lanes : (place + 1) * lanes]
            for w in range(whole):
                values = []
                for k in range(group_size):
                    top = 8 * (k * whole + w)
                    values.append(turned(tile[top : top + 8], k - member))
                stage[to_dom, block, 8 * w : 8 * w + 8, :] = side_by_side(values)
            rest = tile[8 * whole * group_size : class_count]
            values = [
                turned(lifted(rest, -left_over * k), k - member) for k in range(group_size)
            ]
            norm_row = lifted(turned(tile[class_count:padded], -member), left_over)
            mixed = jnp.where(sub_row < left_over, side_by_side(values), norm_row)
            stage[to_dom, block, 8 * whole : piece_rows, :] = mixed[: piece_rows - 8 * whole]
        for to_dom, to_cls in partners[turn]:
            copy = pltpu.make_async_remote_copy(
                src_ref=stage.at[to_dom, to_cls],
                dst_ref=landed.at[cls, dom],
                send_sem=post_send.at[len(posts)],
                recv_sem=post_recv.at[cls, dom],
                device_id=(to_dom, to_cls),
                device_id_type=MESH,
            )
            copy.start()
            posts.append(copy)
    own = pltpu.make_async_copy(stage.at[dom, cls], landed.at[cls, dom], own_sem)
    own.start()
    for copy in sends:
        copy.wait_send()
    for copy in posts:
        copy.wait_send()
    own.wait()
    for from_dom, from_cls in every_partner:
        pltpu.make_async_remote_copy(
            src_ref=stage.at[from_dom, from_cls],
            dst_ref=landed.at[from_cls, from_dom],
            send_sem=post_send.at[0],
            recv_sem=post_recv.at[from_cls, from_dom],
            device_id=(from_dom, from_cls),
            device_id_type=MESH,
        ).wait_recv()


def unpack_kernel(
    capacity, landed_hbm, out_hbm, log_hbm, landed, out_ref, log_ref, in_sem, out_sem, log_sem
):
    cls_size, dom_size, piece_rows, lanes = landed.shape
    class_count = out_ref.shape[0]
    group_size = lanes // capacity
    lane_group = lax.broadcasted_iota(jnp.int32, (8, lanes), 1) // capacity
    whole = class_count // (8 * group_size)
    left_over = (class_count - whole * 8 * group_size) // group_size

    def turned(value, groups):
        amount = groups % group_size * capacity
        return pltpu.roll(value, amount, 1) if amount else value

    def side_by_side(values):
        result = values[0]
        for k in range(1, group_size):
            result = jnp.where(lane_group == k, values[k], result)
        return result

    def pad_rows(value):
        empty = jnp.zeros((8 - value.shape[0], lanes), jnp.float32)
        return jnp.concatenate([value, empty], axis=0)

    slot_count = dom_size * capacity
    loads = [
        pltpu.make_async_copy(landed_hbm.at[block], landed.at[block], in_sem.at[block])
        for block in range(cls_size)
    ]
    for load in loads:
        load.start()
    stores = []
    for block in range(cls_size):
        loads[block].wait()
        for place in range(dom_size // group_size):
            low = block * slot_count + place * lanes
            got = [landed[block, place * group_size + member] for member in range(group_size)]
            for k in range(group_size):
                for w in range(whole):
                    top = 8 * (k * whole + w)
                    out_ref[top : top + 8, low : low + lanes] = side_by_side(
                        [
                            turned(value[8 * w : 8 * w + 8], member - k)
                            for member, value in enumerate(got)
                        ]
                    )
                top = 8 * whole * group_size + left_over * k
                out_ref[top : top + left_over, low : low + lanes] = side_by_side(
                    [
                        turned(pad_rows(value[8 * whole :]), member - k)
                        for member, value in enumerate(got)
                    ]
                )[:left_over]
            log_ref[:, low : low + lanes] = side_by_side(
                [turned(pad_rows(value[8 * whole :]), member) for member, value in enumerate(got)]
            )[left_over : left_over + 1]
        columns = slice(block * slot_count, (block + 1) * slot_count)
        store = pltpu.make_async_copy(
            out_ref.at[:, columns], out_hbm.at[:, columns], out_sem.at[block]
        )
        store.start()
        stores.append(store)
    store = pltpu.make_async_copy(log_ref, log_hbm, log_sem)
    store.start()
    for store in stores + [store]:
        store.wait()


def kernel_shards(images, destinations, group_ids, offsets, inv_noise, ctf_table, references):
    dom_size = lax.axis_size("dom")
    cls_size = lax.axis_size("cls")
    local_count, columns = images.shape
    kept = inv_noise.shape[0]
    group_count = ctf_table.shape[0]
    shift_count = offsets.shape[0]
    class_count, block_columns = references.shape
    slot_count = 2 * local_count
    lanes = 128
    piece_rows = class_count // (lanes // (slot_count // dom_size)) + 1
    padded = class_count + 8
    device_count = dom_size * cls_size
    table_rows = -(-shift_count // 8) * 8
    vmem = pl.BlockSpec(memory_space=pltpu.VMEM)
    hbm = pl.BlockSpec(memory_space=pltpu.HBM)
    packed = pl.pallas_call(
        functools.partial(e_step_kernel, dom_size, cls_size),
        out_shape=jax.ShapeDtypeStruct((cls_size, dom_size, piece_rows, lanes), jnp.float32),
        in_specs=[pl.BlockSpec(memory_space=pltpu.SMEM), hbm, vmem, vmem, hbm, hbm, hbm],
        out_specs=hbm,
        scratch_shapes=[
            pltpu.VMEM((local_count, columns), jnp.bfloat16),
            pltpu.VMEM((1, kept), jnp.float32),
            pltpu.VMEM((group_count, kept), jnp.float32),
            pltpu.VMEM((class_count, block_columns), jnp.bfloat16),
            pltpu.VMEM((2, dom_size, cls_size, padded, block_columns // 2), jnp.bfloat16),
            pltpu.VMEM((shift_count * local_count, columns), jnp.bfloat16),
            pltpu.VMEM((3 * group_count, kept), jnp.bfloat16),
            pltpu.VMEM((table_rows, kept), jnp.float32),
            pltpu.VMEM((table_rows, kept), jnp.float32),
            pltpu.VMEM((cls_size * padded, shift_count * local_count), jnp.float32),
            pltpu.VMEM((2, cls_size, 8, block_columns // 2), jnp.float32),
            pltpu.VMEM((slot_count, 3 * local_count), jnp.bfloat16),
            pltpu.VMEM((3 * group_count, local_count), jnp.bfloat16),
            pltpu.VMEM((cls_size * padded, slot_count), jnp.float32),
            pltpu.VMEM((dom_size, cls_size, piece_rows, lanes), jnp.float32),
            pltpu.SemaphoreType.DMA((4,)),
            pltpu.SemaphoreType.DMA((2 * device_count + dom_size,)),
            pltpu.SemaphoreType.DMA((2, dom_size, cls_size)),
            pltpu.SemaphoreType.DMA((device_count,)),
            pltpu.SemaphoreType.DMA((cls_size, dom_size)),
            pltpu.SemaphoreType.DMA,
        ],
        compiler_params=pltpu.CompilerParams(
            collective_id=0, has_side_effects=True, vmem_limit_bytes=56 * 1024 * 1024
        ),
    )(
        offsets.T,
        images,
        destinations.T,
        group_ids[None, :],
        inv_noise[None, :],
        ctf_table,
        references,
    )
    posteriors, log_norms = pl.pallas_call(
        functools.partial(unpack_kernel, slot_count // dom_size),
        out_shape=(
            jax.ShapeDtypeStruct((class_count, cls_size * slot_count), jnp.float32),
            jax.ShapeDtypeStruct((1, cls_size * slot_count), jnp.float32),
        ),
        in_specs=[hbm],
        out_specs=(hbm, hbm),
        scratch_shapes=[
            pltpu.VMEM((cls_size, dom_size, piece_rows, lanes), jnp.float32),
            pltpu.VMEM((class_count, cls_size * slot_count), jnp.float32),
            pltpu.VMEM((1, cls_size * slot_count), jnp.float32),
            pltpu.SemaphoreType.DMA((cls_size,)),
            pltpu.SemaphoreType.DMA((cls_size,)),
            pltpu.SemaphoreType.DMA,
        ],
        compiler_params=pltpu.CompilerParams(vmem_limit_bytes=56 * 1024 * 1024),
    )(packed)
    return (posteriors.T, log_norms[0])


def fits_kernel(mesh, images, ctf_table, references):
    dom_size, cls_size = mesh.shape["dom"], mesh.shape["cls"]
    local_count = images.shape[0] // (dom_size * cls_size)
    capacity = 2 * local_count // dom_size
    class_count = references.shape[0] // cls_size
    half_columns = references.shape[1] // dom_size // 2
    if cls_size != 4 or dom_size % 2 or local_count != 128 or 128 % capacity:
        return False
    group_size = 128 // capacity
    return (
        group_size > 1
        and dom_size % group_size == 0
        and class_count % 8 == 0
        and class_count % (8 * group_size) == 8
        and 8 // group_size * group_size == 8
        and 8 // group_size < 8
        and dom_size & (dom_size - 1) == 0
        and (class_count + 8) % 16 == 0
        and half_columns % 128 == 0
        and 3 * (class_count + 8) < half_columns
        and ctf_table.shape[0] == 16
    )


def solution(mesh):
    def e_step(*arrays):
        shards = kernel_shards if fits_kernel(mesh, arrays[0], arrays[-2], arrays[-1]) else plain_shards
        return mapped(mesh, shards)(*arrays)

    return e_step


def mapped(mesh, shards):
    return jax.shard_map(
        shards,
        mesh=mesh,
        in_specs=(
            P(("dom", "cls"), None),
            P(("dom", "cls"), None),
            P(("dom", "cls")),
            P(),
            P(),
            P(),
            P("cls", "dom"),
        ),
        out_specs=(P("dom", "cls"), P("dom")),
        check_vma=False,
    )
```

```python
import functools
import math

import jax
import jax.numpy as jnp
from jax import lax
from jax.experimental import pallas as pl
from jax.experimental.pallas import tpu as pltpu
from jax.sharding import PartitionSpec as P

SIDE = 64


def phase_tables(offsets, kept):
    freq_index = jnp.arange(kept, dtype=jnp.int32)
    half_side = SIDE // 2
    row_freq = freq_index // half_side
    col_freq = freq_index % half_side
    row_freq = jnp.where(row_freq >= half_side, row_freq - SIDE, row_freq)
    turns = jnp.mod(offsets[:, 0:1] * row_freq[None, :] + offsets[:, 1:2] * col_freq[None, :], SIDE)
    angles = turns.astype(jnp.float32) * (2.0 * math.pi / SIDE)
    return (jnp.cos(angles), jnp.sin(angles))


def shifted_rows(images, group_hot, offsets, inv_noise, ctf_table):
    kept = inv_noise.shape[0]
    cosines, sines = phase_tables(offsets, kept)
    ctf_rows = jnp.dot(
        group_hot, ctf_table, precision=lax.Precision.HIGHEST, preferred_element_type=jnp.float32
    )
    weight = inv_noise[None, :] * ctf_rows
    real_part = images[:, :kept].astype(jnp.float32)
    imag_part = images[:, kept:].astype(jnp.float32)
    pieces = []
    for shift_index in range(offsets.shape[0]):
        cosine = cosines[shift_index][None, :]
        sine = sines[shift_index][None, :]
        both = jnp.concatenate(
            [
                weight * (real_part * cosine - imag_part * sine),
                weight * (real_part * sine + imag_part * cosine),
            ],
            axis=1,
        )
        pieces.append(both.astype(jnp.bfloat16))
    return jnp.concatenate(pieces, axis=0)


def slots_of(target, dom_size, capacity):
    local_count = target.shape[0]
    target_hot = (target[:, None] == jnp.arange(dom_size, dtype=jnp.int32)[None, :]).astype(
        jnp.float32
    )
    local_index = jnp.arange(local_count, dtype=jnp.int32)
    lower = (local_index[:, None] > local_index[None, :]).astype(jnp.float32)
    earlier = jnp.dot(lower, target_hot, preferred_element_type=jnp.float32)
    position_rank = jnp.sum(earlier * target_hot, axis=1).astype(jnp.int32)
    return target * capacity + position_rank


def plain_shards(images, destinations, group_ids, offsets, inv_noise, ctf_table, references):
    dom_size = lax.axis_size("dom")
    cls_size = lax.axis_size("cls")
    local_count = images.shape[0]
    shift_count = offsets.shape[0]
    group_count = ctf_table.shape[0]
    class_count = references.shape[0]
    capacity = 2 * local_count // dom_size
    slot_count = dom_size * capacity
    class_rows = lax.all_gather(references, "cls", axis=0, tiled=True)
    every_ref = lax.all_gather(class_rows, "dom", axis=1, tiled=True)
    slot_of = slots_of(destinations[:, 0], dom_size, capacity)
    chosen = (jnp.arange(slot_count, dtype=jnp.int32)[:, None] == slot_of[None, :]).astype(
        jnp.float32
    )
    group_hot = (group_ids[:, None] == jnp.arange(group_count, dtype=jnp.int32)[None, :]).astype(
        jnp.float32
    )
    noise_ctf = inv_noise[None, :] * ctf_table * ctf_table
    noise_terms = jnp.concatenate([noise_ctf, noise_ctf], axis=1)
    shifted = shifted_rows(images, group_hot, offsets, inv_noise, ctf_table)
    contract = (((1,), (1,)), ((), ()))
    cross = lax.dot_general(shifted, every_ref, contract, preferred_element_type=jnp.float32)
    ref_float = every_ref.astype(jnp.float32)
    norms = lax.dot_general(
        noise_terms,
        ref_float * ref_float,
        contract,
        precision=lax.Precision.HIGHEST,
        preferred_element_type=jnp.float32,
    )
    selected = jnp.dot(
        group_hot, norms, precision=lax.Precision.HIGHEST, preferred_element_type=jnp.float32
    )
    scores = cross.reshape(shift_count, local_count, -1) - 0.5 * selected[None, :, :]
    row_peak = jnp.max(scores, axis=(0, 2))
    weights = jnp.exp(scores - row_peak[None, :, None])
    row_total = jnp.sum(weights, axis=(0, 2))
    log_norm = row_peak + jnp.log(row_total)
    posterior = jnp.sum(weights, axis=0) / row_total[:, None]
    posterior = posterior.reshape(local_count, cls_size, class_count)
    spread = jnp.broadcast_to(log_norm[:, None, None], (local_count, cls_size, 1))
    rows = jnp.concatenate([posterior, spread], axis=2).reshape(local_count, -1)
    slots = jnp.dot(
        chosen, rows, precision=lax.Precision.HIGHEST, preferred_element_type=jnp.float32
    )
    blocks = slots.reshape(dom_size, capacity, cls_size, class_count + 1).transpose(0, 2, 1, 3)
    blocks = blocks.reshape(dom_size * cls_size, capacity, class_count + 1)
    blocks = lax.all_to_all(blocks, ("dom", "cls"), split_axis=0, concat_axis=0, tiled=True)
    blocks = blocks.reshape(dom_size, cls_size, capacity, class_count + 1).transpose(1, 0, 2, 3)
    blocks = blocks.reshape(cls_size * slot_count, class_count + 1)
    return (blocks[:, :class_count], blocks[:, class_count])


MESH = pl.DeviceIdType.MESH
NT_DIMS = (((1,), (1,)), ((), ()))


def three_parts(value):
    high = value.astype(jnp.bfloat16)
    rest = value - high.astype(jnp.float32)
    middle = rest.astype(jnp.bfloat16)
    low = (rest - middle.astype(jnp.float32)).astype(jnp.bfloat16)
    return [high, middle, low]


def quarter_turns(turns):
    quarter, eighth = SIDE // 4, SIDE // 8
    quadrant = (turns + eighth) // quarter
    angle = (turns - quadrant * quarter).astype(jnp.float32) * (2.0 * math.pi / SIDE)
    square = angle * angle
    sine = 1.0 / 362880.0
    for term in (-1.0 / 5040.0, 1.0 / 120.0, -1.0 / 6.0, 1.0):
        sine = sine * square + term
    sine = sine * angle
    cosine = -1.0 / 3628800.0
    for term in (1.0 / 40320.0, -1.0 / 720.0, 1.0 / 24.0, -0.5, 1.0):
        cosine = cosine * square + term
    quadrant = quadrant & 3
    odd = (quadrant & 1) == 1
    first = jnp.where(odd, sine, cosine)
    second = jnp.where(odd, cosine, sine)
    return (
        jnp.where((quadrant == 1) | (quadrant == 2), -first, first),
        jnp.where(quadrant >= 2, -second, second),
    )


def e_step_kernel(
    dom_size,
    cls_size,
    offsets_ref,
    images_hbm,
    target_ref,
    group_ref,
    inv_noise_hbm,
    ctf_hbm,
    refs_hbm,
    landed,
    images_ref,
    inv_noise_ref,
    ctf_ref,
    refs_ref,
    held,
    shifted,
    ctf_parts,
    cosines,
    sines,
    cross,
    norms,
    slot_hot,
    group_hot_rows,
    slots_ref,
    stage,
    load_sem,
    send_sem,
    recv_sem,
    post_send,
    post_recv,
    own_sem,
):
    z_size = dom_size // 2
    class_count, block_columns = refs_ref.shape
    half_columns = block_columns // 2
    padded = held.shape[3]
    local_count = images_ref.shape[0]
    kept = inv_noise_ref.shape[1]
    group_count = ctf_ref.shape[0]
    shift_count = offsets_ref.shape[1]
    slot_count = slot_hot.shape[0]
    capacity = slot_count // dom_size
    piece_rows, lanes = stage.shape[2:]
    group_size = lanes // capacity
    dom = lax.axis_index("dom")
    cls = lax.axis_index("cls")
    z, x = dom // 2, dom % 2
    y, core = cls // 2, cls % 2

    loads = [
        pltpu.make_async_copy(source, place, load_sem.at[index])
        for index, (source, place) in enumerate(
            [
                (refs_hbm, refs_ref),
                (ctf_hbm, ctf_ref),
                (inv_noise_hbm, inv_noise_ref),
                (images_hbm, images_ref),
            ]
        )
    ]
    for load in loads:
        load.start()
    barrier = pltpu.get_barrier_semaphore()
    partners = [
        [
            (lax.rem(dom + i, dom_size), lax.rem(cls + j, cls_size))
            for i in sorted(range(dom_size), key=lambda i: (abs(i - dom_size // 2), i))
            if i or j
        ]
        for j in range(cls_size)
    ]
    every_partner = sum(partners, [])
    def z_partner(step):
        other, bit = z, 1
        while bit < z_size:
            if step & bit:
                other = other + bit - 2 * bit * ((z // bit) % 2)
            bit *= 2
        return other

    order = list(range(0, z_size, 2)) + list(range(1, z_size, 2))
    over_x = (z * 2 + (1 - x), cls)
    over_y = (dom, (1 - y) * 2 + core)
    over_core = (dom, y * 2 + (1 - core))
    neighbours = [over_x, over_y, over_core]
    neighbours += [(z_partner(step) * 2 + x, cls) for step in order[1:]]
    for partner in neighbours:
        pl.semaphore_signal(barrier, inc=1, device_id=partner, device_id_type=MESH)

    for load in loads[:3]:
        load.wait()
    wide = refs_ref[...].astype(jnp.float32)
    squares = jnp.concatenate(
        [wide * wide, jnp.zeros((padded - class_count, block_columns), jnp.float32)], axis=0
    )
    high = squares.astype(jnp.bfloat16)
    rest = (squares - high.astype(jnp.float32)).astype(jnp.bfloat16)
    low = pl.multiple_of(lax.rem(dom * block_columns, kept), block_columns)
    own_ctf = ctf_ref[:, pl.ds(low, block_columns)]
    noise_terms = inv_noise_ref[:, pl.ds(low, block_columns)] * own_ctf * own_ctf
    sums = lax.dot_general(
        jnp.concatenate(three_parts(noise_terms), axis=0),
        jnp.concatenate([high, rest], axis=0),
        NT_DIMS,
        preferred_element_type=jnp.float32,
    )
    sums = sums[:, :padded] + sums[:, padded:]
    own_norms = (
        sums[:group_count] + sums[group_count : 2 * group_count] + sums[2 * group_count :]
    )
    tail = jnp.concatenate(
        [part.astype(jnp.float32) for part in three_parts(own_norms)]
        + [jnp.zeros((group_count, half_columns - 3 * padded), jnp.float32)],
        axis=1,
    )
    for half in range(2):
        rows = wide[:, half * half_columns : (half + 1) * half_columns]
        extra = padded - class_count
        block = jnp.concatenate([rows, tail[half * extra : (half + 1) * extra]], axis=0)
        held[half, dom, cls] = block.astype(jnp.bfloat16)
    pl.semaphore_wait(barrier, len(neighbours))

    sends = []

    def block_copy(half, block_dom, block_cls, device, index):
        halves, sem = (slice(None), 0) if half is None else (half, half)
        block = held.at[halves, block_dom, block_cls]
        return pltpu.make_async_remote_copy(
            src_ref=block,
            dst_ref=block,
            send_sem=send_sem.at[index],
            recv_sem=recv_sem.at[sem, block_dom, block_cls],
            device_id=device,
            device_id_type=MESH,
        )

    def send(half, block_dom, block_cls, device):
        copy = block_copy(half, block_dom, block_cls, device, len(sends))
        copy.start()
        sends.append(copy)

    def arrived(half, block_dom, block_cls):
        block_copy(half, block_dom, block_cls, over_core, 0).wait_recv()

    send(0, dom, cls, over_x)
    send(1, dom, cls, over_y)
    for step in order[1:2]:
        send(None, dom, cls, (z_partner(step) * 2 + x, cls))
    send(1, dom, cls, over_x)
    send(0, dom, cls, over_y)
    for step in order[2:]:
        send(None, dom, cls, (z_partner(step) * 2 + x, cls))
    send(None, dom, cls, over_core)

    table_shape = (cosines.shape[0], kept)
    freq = lax.broadcasted_iota(jnp.int32, table_shape, 1)
    shift_row = lax.broadcasted_iota(jnp.int32, table_shape, 0)
    half_side = SIDE // 2
    row_freq = freq // half_side
    col_freq = freq % half_side
    row_freq = jnp.where(row_freq >= half_side, row_freq - SIDE, row_freq)
    turns = jnp.zeros(table_shape, jnp.int32)
    for t in range(shift_count):
        turn = offsets_ref[0, t] * row_freq + offsets_ref[1, t] * col_freq
        turns = jnp.where(shift_row == t, turn & (SIDE - 1), turns)
    cosines[...], sines[...] = quarter_turns(turns)
    for index, part in enumerate(three_parts(ctf_ref[...])):
        ctf_parts[index * group_count : (index + 1) * group_count, :] = part
    square = (local_count, local_count)
    sub = lax.broadcasted_iota(jnp.int32, square, 0)
    lane = lax.broadcasted_iota(jnp.int32, square, 1)
    group_row = group_ref[...]
    group_col = jnp.sum(jnp.where(sub == lane, group_row, 0), axis=1, keepdims=True)
    part_lane = lax.broadcasted_iota(jnp.int32, (local_count, 3 * group_count), 1)
    group_hot = jnp.where(part_lane % group_count == group_col, 1.0, 0.0).astype(jnp.bfloat16)

    chunk = kept // 4

    def shift_chunk(step):
        low = step * chunk
        columns = slice(low, low + chunk)
        imag_columns = slice(kept + low, kept + low + chunk)
        weight = inv_noise_ref[:, columns] * jnp.dot(
            group_hot, ctf_parts[:, columns], preferred_element_type=jnp.float32
        )
        real_part = images_ref[:, columns].astype(jnp.float32)
        imag_part = images_ref[:, imag_columns].astype(jnp.float32)
        for t in range(shift_count):
            cosine = cosines[t : t + 1, columns]
            sine = sines[t : t + 1, columns]
            rows = slice(t * local_count, (t + 1) * local_count)
            shifted[rows, columns] = (
                weight * (real_part * cosine - imag_part * sine)
            ).astype(jnp.bfloat16)
            shifted[rows, imag_columns] = (
                weight * (real_part * sine + imag_part * cosine)
            ).astype(jnp.bfloat16)

    hot_rows = lax.broadcasted_iota(jnp.int32, group_hot_rows.shape, 0)
    group_hot_rows[...] = jnp.where(hot_rows % group_count == group_row, 1.0, 0.0).astype(
        jnp.bfloat16
    )
    target_row = target_ref[...]
    target_col = jnp.sum(jnp.where(sub == lane, target_row, 0), axis=1, keepdims=True)
    ahead = (target_col == target_row) & (sub < lane)
    rank = jnp.sum(jnp.where(ahead, 1, 0), axis=0, keepdims=True)
    slot_of = target_row * capacity + rank
    slot = lax.broadcasted_iota(jnp.int32, (slot_count, local_count), 0)
    hot = jnp.where(slot == slot_of, 1.0, 0.0).astype(jnp.bfloat16)
    for index in range(3):
        slot_hot[:, index * local_count : (index + 1) * local_count] = hot
    cross[...] = jnp.zeros_like(cross)
    norms[...] = jnp.zeros_like(norms)

    def from_z(step):
        block = z_partner(step) * 2 + x
        arrived(None, block, cls)
        send(0, block, cls, over_x)
        send(1, block, cls, over_y)
        send(1, block, cls, over_x)
        send(0, block, cls, over_y)
        send(None, block, cls, over_core)

    def from_first(step):
        near, far = z_partner(step) * 2 + x, z_partner(step) * 2 + (1 - x)
        arrived(0, far, cls)
        if step % 2 == 0:
            send(0, far, cls, over_y)
        arrived(1, near, over_y[1])
        if step % 2 == 0:
            send(1, near, over_y[1], over_x)
        send(0, far, cls, over_core)
        send(1, near, over_y[1], over_core)

    def from_last(step):
        near, far = z_partner(step) * 2 + x, z_partner(step) * 2 + (1 - x)
        arrived(0, near, over_y[1])
        send(0, near, over_y[1], over_core)
        arrived(1, far, cls)
        send(1, far, cls, over_core)
        if step % 2 == 0:
            arrived(0, far, over_y[1])
            arrived(1, far, over_y[1])
            if z_size > 1:
                send(None, far, over_y[1], (z_partner(1) * 2 + x, cls))
        else:
            arrived(None, far, over_y[1])
        send(None, far, over_y[1], over_core)

    sibling, far_sibling = over_core[1], (1 - y) * 2 + (1 - core)

    def add_block(block_dom):
        rows = jnp.concatenate(
            [held[half, block_dom].reshape(cls_size * padded, half_columns) for half in range(2)],
            axis=1,
        )
        low = pl.multiple_of(block_dom * block_columns, block_columns)
        cross[...] += lax.dot_general(
            rows, shifted[:, pl.ds(low, block_columns)], NT_DIMS, preferred_element_type=jnp.float32
        )
        for half in range(2):
            last_rows = held[half, block_dom, :, padded - 16 : padded, :].astype(jnp.float32)
            norms[half] += last_rows[:, 8:16, :]

    def multiply_near(step):
        while chunks:
            shift_chunk(chunks.pop(0))
        near = z_partner(step) * 2 + x
        arrived(None, near, sibling)
        arrived(0, near, far_sibling)
        arrived(1, near, far_sibling)
        add_block(near)

    def multiply_far(step):
        far = z_partner(step) * 2 + (1 - x)
        arrived(0, far, sibling)
        arrived(1, far, sibling)
        arrived(None, far, far_sibling)
        add_block(far)

    chunks = list(range(4))
    loads[3].wait()
    shift_chunk(chunks.pop(0))
    for turn in range(z_size + 2):
        if 0 < turn < z_size:
            from_z(order[turn])
        if turn == 1:
            shift_chunk(chunks.pop(0))
        if turn >= 2:
            multiply_near(order[turn - 2])
        if turn < z_size:
            from_first(order[turn])
        if turn >= 2:
            multiply_far(order[turn - 2])
        if turn == 1:
            shift_chunk(chunks.pop(0))
        if 0 < turn <= z_size:
            from_last(order[turn - 1])

    selected = []
    for block in range(cls_size):
        both = jnp.concatenate([norms[0, block], norms[1, block]], axis=0)
        total_norm = sum(both[:, p * padded : (p + 1) * padded] for p in range(3))
        selected.append(
            lax.dot_general(
                jnp.concatenate(three_parts(total_norm), axis=0),
                group_hot_rows[...],
                (((0,), (0,)), ((), ())),
                preferred_element_type=jnp.float32,
            )
        )
    selected = 0.5 * jnp.concatenate(selected, axis=0)
    row = lax.broadcasted_iota(jnp.int32, (cls_size * padded, local_count), 0) % padded
    real_row = row < class_count
    scores = []
    for t in range(shift_count):
        value = cross[:, t * local_count : (t + 1) * local_count] - selected
        scores.append(jnp.where(real_row, value, -jnp.inf))
    peak = functools.reduce(jnp.maximum, scores)
    peak = jnp.max(peak, axis=0, keepdims=True)
    weights = functools.reduce(jnp.add, [jnp.exp(value - peak) for value in scores])
    total = jnp.sum(weights, axis=0, keepdims=True)
    log_norm = peak + jnp.log(total)
    table = jnp.where(row == class_count, log_norm, weights / total)

    slots_ref[...] = lax.dot_general(
        jnp.concatenate(three_parts(table), axis=1),
        slot_hot[...],
        NT_DIMS,
        preferred_element_type=jnp.float32,
    )
    lane_group = lax.broadcasted_iota(jnp.int32, (8, lanes), 1) // capacity
    whole = class_count // (8 * group_size)
    left_over = (class_count - whole * 8 * group_size) // group_size

    def turned(value, groups):
        amount = groups % group_size * capacity
        return pltpu.roll(value, amount, 1) if amount else value

    def lifted(value, rows):
        return pltpu.roll(value, rows % 8, 0) if rows % 8 else value

    def side_by_side(values):
        result = values[0]
        for k in range(1, group_size):
            result = jnp.where(lane_group == k, values[k], result)
        return result

    sub_row = lax.broadcasted_iota(jnp.int32, (8, lanes), 0)
    posts = []
    for turn in range(cls_size):
        block = lax.rem(cls + turn, cls_size)
        part = slots_ref[pl.ds(pl.multiple_of(block * padded, 16), padded), :]
        for to_dom in range(dom_size):
            place, member = to_dom // group_size, to_dom % group_size
            tile = part[:, place * lanes : (place + 1) * lanes]
            for w in range(whole):
                values = []
                for k in range(group_size):
                    top = 8 * (k * whole + w)
                    values.append(turned(tile[top : top + 8], k - member))
                stage[to_dom, block, 8 * w : 8 * w + 8, :] = side_by_side(values)
            rest = tile[8 * whole * group_size : class_count]
            values = [
                turned(lifted(rest, -left_over * k), k - member) for k in range(group_size)
            ]
            norm_row = lifted(turned(tile[class_count:padded], -member), left_over)
            mixed = jnp.where(sub_row < left_over, side_by_side(values), norm_row)
            stage[to_dom, block, 8 * whole : piece_rows, :] = mixed[: piece_rows - 8 * whole]
        for to_dom, to_cls in partners[turn]:
            copy = pltpu.make_async_remote_copy(
                src_ref=stage.at[to_dom, to_cls],
                dst_ref=landed.at[cls, dom],
                send_sem=post_send.at[len(posts)],
                recv_sem=post_recv.at[cls, dom],
                device_id=(to_dom, to_cls),
                device_id_type=MESH,
            )
            copy.start()
            posts.append(copy)
    own = pltpu.make_async_copy(stage.at[dom, cls], landed.at[cls, dom], own_sem)
    own.start()
    for copy in sends:
        copy.wait_send()
    for copy in posts:
        copy.wait_send()
    own.wait()
    for from_dom, from_cls in every_partner:
        pltpu.make_async_remote_copy(
            src_ref=stage.at[from_dom, from_cls],
            dst_ref=landed.at[from_cls, from_dom],
            send_sem=post_send.at[0],
            recv_sem=post_recv.at[from_cls, from_dom],
            device_id=(from_dom, from_cls),
            device_id_type=MESH,
        ).wait_recv()


def unpack_kernel(
    capacity, landed_hbm, out_hbm, log_hbm, landed, out_ref, log_ref, in_sem, out_sem, log_sem
):
    cls_size, dom_size, piece_rows, lanes = landed.shape
    class_count = out_ref.shape[0]
    group_size = lanes // capacity
    lane_group = lax.broadcasted_iota(jnp.int32, (8, lanes), 1) // capacity
    whole = class_count // (8 * group_size)
    left_over = (class_count - whole * 8 * group_size) // group_size

    def turned(value, groups):
        amount = groups % group_size * capacity
        return pltpu.roll(value, amount, 1) if amount else value

    def side_by_side(values):
        result = values[0]
        for k in range(1, group_size):
            result = jnp.where(lane_group == k, values[k], result)
        return result

    def pad_rows(value):
        empty = jnp.zeros((8 - value.shape[0], lanes), jnp.float32)
        return jnp.concatenate([value, empty], axis=0)

    slot_count = dom_size * capacity
    loads = [
        pltpu.make_async_copy(landed_hbm.at[block], landed.at[block], in_sem.at[block])
        for block in range(cls_size)
    ]
    for load in loads:
        load.start()
    stores = []
    for block in range(cls_size):
        loads[block].wait()
        for place in range(dom_size // group_size):
            low = block * slot_count + place * lanes
            got = [landed[block, place * group_size + member] for member in range(group_size)]
            for k in range(group_size):
                for w in range(whole):
                    top = 8 * (k * whole + w)
                    out_ref[top : top + 8, low : low + lanes] = side_by_side(
                        [
                            turned(value[8 * w : 8 * w + 8], member - k)
                            for member, value in enumerate(got)
                        ]
                    )
                top = 8 * whole * group_size + left_over * k
                out_ref[top : top + left_over, low : low + lanes] = side_by_side(
                    [
                        turned(pad_rows(value[8 * whole :]), member - k)
                        for member, value in enumerate(got)
                    ]
                )[:left_over]
            log_ref[:, low : low + lanes] = side_by_side(
                [turned(pad_rows(value[8 * whole :]), member) for member, value in enumerate(got)]
            )[left_over : left_over + 1]
        columns = slice(block * slot_count, (block + 1) * slot_count)
        store = pltpu.make_async_copy(
            out_ref.at[:, columns], out_hbm.at[:, columns], out_sem.at[block]
        )
        store.start()
        stores.append(store)
    store = pltpu.make_async_copy(log_ref, log_hbm, log_sem)
    store.start()
    for store in stores + [store]:
        store.wait()


def kernel_shards(images, destinations, group_ids, offsets, inv_noise, ctf_table, references):
    dom_size = lax.axis_size("dom")
    cls_size = lax.axis_size("cls")
    local_count, columns = images.shape
    kept = inv_noise.shape[0]
    group_count = ctf_table.shape[0]
    shift_count = offsets.shape[0]
    class_count, block_columns = references.shape
    slot_count = 2 * local_count
    lanes = 128
    piece_rows = class_count // (lanes // (slot_count // dom_size)) + 1
    padded = class_count + 8
    device_count = dom_size * cls_size
    table_rows = -(-shift_count // 8) * 8
    vmem = pl.BlockSpec(memory_space=pltpu.VMEM)
    hbm = pl.BlockSpec(memory_space=pltpu.HBM)
    packed = pl.pallas_call(
        functools.partial(e_step_kernel, dom_size, cls_size),
        out_shape=jax.ShapeDtypeStruct((cls_size, dom_size, piece_rows, lanes), jnp.float32),
        in_specs=[pl.BlockSpec(memory_space=pltpu.SMEM), hbm, vmem, vmem, hbm, hbm, hbm],
        out_specs=hbm,
        scratch_shapes=[
            pltpu.VMEM((local_count, columns), jnp.bfloat16),
            pltpu.VMEM((1, kept), jnp.float32),
            pltpu.VMEM((group_count, kept), jnp.float32),
            pltpu.VMEM((class_count, block_columns), jnp.bfloat16),
            pltpu.VMEM((2, dom_size, cls_size, padded, block_columns // 2), jnp.bfloat16),
            pltpu.VMEM((shift_count * local_count, columns), jnp.bfloat16),
            pltpu.VMEM((3 * group_count, kept), jnp.bfloat16),
            pltpu.VMEM((table_rows, kept), jnp.float32),
            pltpu.VMEM((table_rows, kept), jnp.float32),
            pltpu.VMEM((cls_size * padded, shift_count * local_count), jnp.float32),
            pltpu.VMEM((2, cls_size, 8, block_columns // 2), jnp.float32),
            pltpu.VMEM((slot_count, 3 * local_count), jnp.bfloat16),
            pltpu.VMEM((3 * group_count, local_count), jnp.bfloat16),
            pltpu.VMEM((cls_size * padded, slot_count), jnp.float32),
            pltpu.VMEM((dom_size, cls_size, piece_rows, lanes), jnp.float32),
            pltpu.SemaphoreType.DMA((4,)),
            pltpu.SemaphoreType.DMA((2 * device_count + dom_size,)),
            pltpu.SemaphoreType.DMA((2, dom_size, cls_size)),
            pltpu.SemaphoreType.DMA((device_count,)),
            pltpu.SemaphoreType.DMA((cls_size, dom_size)),
            pltpu.SemaphoreType.DMA,
        ],
        compiler_params=pltpu.CompilerParams(
            collective_id=0, has_side_effects=True, vmem_limit_bytes=56 * 1024 * 1024
        ),
    )(
        offsets.T,
        images,
        destinations.T,
        group_ids[None, :],
        inv_noise[None, :],
        ctf_table,
        references,
    )
    posteriors, log_norms = pl.pallas_call(
        functools.partial(unpack_kernel, slot_count // dom_size),
        out_shape=(
            jax.ShapeDtypeStruct((class_count, cls_size * slot_count), jnp.float32),
            jax.ShapeDtypeStruct((1, cls_size * slot_count), jnp.float32),
        ),
        in_specs=[hbm],
        out_specs=(hbm, hbm),
        scratch_shapes=[
            pltpu.VMEM((cls_size, dom_size, piece_rows, lanes), jnp.float32),
            pltpu.VMEM((class_count, cls_size * slot_count), jnp.float32),
            pltpu.VMEM((1, cls_size * slot_count), jnp.float32),
            pltpu.SemaphoreType.DMA((cls_size,)),
            pltpu.SemaphoreType.DMA((cls_size,)),
            pltpu.SemaphoreType.DMA,
        ],
        compiler_params=pltpu.CompilerParams(vmem_limit_bytes=56 * 1024 * 1024),
    )(packed)
    return (posteriors.T, log_norms[0])


def fits_kernel(mesh, images, ctf_table, references):
    dom_size, cls_size = mesh.shape["dom"], mesh.shape["cls"]
    local_count = images.shape[0] // (dom_size * cls_size)
    capacity = 2 * local_count // dom_size
    class_count = references.shape[0] // cls_size
    half_columns = references.shape[1] // dom_size // 2
    if cls_size != 4 or dom_size % 2 or local_count != 128 or 128 % capacity:
        return False
    group_size = 128 // capacity
    return (
        group_size > 1
        and dom_size % group_size == 0
        and class_count % 8 == 0
        and class_count % (8 * group_size) == 8
        and 8 // group_size * group_size == 8
        and 8 // group_size < 8
        and dom_size & (dom_size - 1) == 0
        and (class_count + 8) % 16 == 0
        and half_columns % 128 == 0
        and 3 * (class_count + 8) < half_columns
        and ctf_table.shape[0] == 16
    )


def solution(mesh):
    def e_step(*arrays):
        shards = kernel_shards if fits_kernel(mesh, arrays[0], arrays[-2], arrays[-1]) else plain_shards
        return mapped(mesh, shards)(*arrays)

    return e_step


def mapped(mesh, shards):
    return jax.shard_map(
        shards,
        mesh=mesh,
        in_specs=(
            P(("dom", "cls"), None),
            P(("dom", "cls"), None),
            P(("dom", "cls")),
            P(),
            P(),
            P(),
            P("cls", "dom"),
        ),
        out_specs=(P("dom", "cls"), P("dom")),
        check_vma=False,
    )
```

```python
import functools
import math

import jax
import jax.numpy as jnp
from jax import lax
from jax.experimental import pallas as pl
from jax.experimental.pallas import tpu as pltpu
from jax.sharding import PartitionSpec as P

SIDE = 64


def phase_tables(offsets, kept):
    freq_index = jnp.arange(kept, dtype=jnp.int32)
    half_side = SIDE // 2
    row_freq = freq_index // half_side
    col_freq = freq_index % half_side
    row_freq = jnp.where(row_freq >= half_side, row_freq - SIDE, row_freq)
    turns = jnp.mod(offsets[:, 0:1] * row_freq[None, :] + offsets[:, 1:2] * col_freq[None, :], SIDE)
    angles = turns.astype(jnp.float32) * (2.0 * math.pi / SIDE)
    return (jnp.cos(angles), jnp.sin(angles))


def shifted_rows(images, group_hot, offsets, inv_noise, ctf_table):
    kept = inv_noise.shape[0]
    cosines, sines = phase_tables(offsets, kept)
    ctf_rows = jnp.dot(
        group_hot, ctf_table, precision=lax.Precision.HIGHEST, preferred_element_type=jnp.float32
    )
    weight = inv_noise[None, :] * ctf_rows
    real_part = images[:, :kept].astype(jnp.float32)
    imag_part = images[:, kept:].astype(jnp.float32)
    pieces = []
    for shift_index in range(offsets.shape[0]):
        cosine = cosines[shift_index][None, :]
        sine = sines[shift_index][None, :]
        both = jnp.concatenate(
            [
                weight * (real_part * cosine - imag_part * sine),
                weight * (real_part * sine + imag_part * cosine),
            ],
            axis=1,
        )
        pieces.append(both.astype(jnp.bfloat16))
    return jnp.concatenate(pieces, axis=0)


def slots_of(target, dom_size, capacity):
    local_count = target.shape[0]
    target_hot = (target[:, None] == jnp.arange(dom_size, dtype=jnp.int32)[None, :]).astype(
        jnp.float32
    )
    local_index = jnp.arange(local_count, dtype=jnp.int32)
    lower = (local_index[:, None] > local_index[None, :]).astype(jnp.float32)
    earlier = jnp.dot(lower, target_hot, preferred_element_type=jnp.float32)
    position_rank = jnp.sum(earlier * target_hot, axis=1).astype(jnp.int32)
    return target * capacity + position_rank


def plain_shards(images, destinations, group_ids, offsets, inv_noise, ctf_table, references):
    dom_size = lax.axis_size("dom")
    cls_size = lax.axis_size("cls")
    local_count = images.shape[0]
    shift_count = offsets.shape[0]
    group_count = ctf_table.shape[0]
    class_count = references.shape[0]
    capacity = 2 * local_count // dom_size
    slot_count = dom_size * capacity
    class_rows = lax.all_gather(references, "cls", axis=0, tiled=True)
    every_ref = lax.all_gather(class_rows, "dom", axis=1, tiled=True)
    slot_of = slots_of(destinations[:, 0], dom_size, capacity)
    chosen = (jnp.arange(slot_count, dtype=jnp.int32)[:, None] == slot_of[None, :]).astype(
        jnp.float32
    )
    group_hot = (group_ids[:, None] == jnp.arange(group_count, dtype=jnp.int32)[None, :]).astype(
        jnp.float32
    )
    noise_ctf = inv_noise[None, :] * ctf_table * ctf_table
    noise_terms = jnp.concatenate([noise_ctf, noise_ctf], axis=1)
    shifted = shifted_rows(images, group_hot, offsets, inv_noise, ctf_table)
    contract = (((1,), (1,)), ((), ()))
    cross = lax.dot_general(shifted, every_ref, contract, preferred_element_type=jnp.float32)
    ref_float = every_ref.astype(jnp.float32)
    norms = lax.dot_general(
        noise_terms,
        ref_float * ref_float,
        contract,
        precision=lax.Precision.HIGHEST,
        preferred_element_type=jnp.float32,
    )
    selected = jnp.dot(
        group_hot, norms, precision=lax.Precision.HIGHEST, preferred_element_type=jnp.float32
    )
    scores = cross.reshape(shift_count, local_count, -1) - 0.5 * selected[None, :, :]
    row_peak = jnp.max(scores, axis=(0, 2))
    weights = jnp.exp(scores - row_peak[None, :, None])
    row_total = jnp.sum(weights, axis=(0, 2))
    log_norm = row_peak + jnp.log(row_total)
    posterior = jnp.sum(weights, axis=0) / row_total[:, None]
    posterior = posterior.reshape(local_count, cls_size, class_count)
    spread = jnp.broadcast_to(log_norm[:, None, None], (local_count, cls_size, 1))
    rows = jnp.concatenate([posterior, spread], axis=2).reshape(local_count, -1)
    slots = jnp.dot(
        chosen, rows, precision=lax.Precision.HIGHEST, preferred_element_type=jnp.float32
    )
    blocks = slots.reshape(dom_size, capacity, cls_size, class_count + 1).transpose(0, 2, 1, 3)
    blocks = blocks.reshape(dom_size * cls_size, capacity, class_count + 1)
    blocks = lax.all_to_all(blocks, ("dom", "cls"), split_axis=0, concat_axis=0, tiled=True)
    blocks = blocks.reshape(dom_size, cls_size, capacity, class_count + 1).transpose(1, 0, 2, 3)
    blocks = blocks.reshape(cls_size * slot_count, class_count + 1)
    return (blocks[:, :class_count], blocks[:, class_count])


MESH = pl.DeviceIdType.MESH
NT_DIMS = (((1,), (1,)), ((), ()))


def three_parts(value):
    high = value.astype(jnp.bfloat16)
    rest = value - high.astype(jnp.float32)
    middle = rest.astype(jnp.bfloat16)
    low = (rest - middle.astype(jnp.float32)).astype(jnp.bfloat16)
    return [high, middle, low]


def quarter_turns(turns):
    quarter, eighth = SIDE // 4, SIDE // 8
    quadrant = (turns + eighth) // quarter
    angle = (turns - quadrant * quarter).astype(jnp.float32) * (2.0 * math.pi / SIDE)
    square = angle * angle
    sine = 1.0 / 362880.0
    for term in (-1.0 / 5040.0, 1.0 / 120.0, -1.0 / 6.0, 1.0):
        sine = sine * square + term
    sine = sine * angle
    cosine = -1.0 / 3628800.0
    for term in (1.0 / 40320.0, -1.0 / 720.0, 1.0 / 24.0, -0.5, 1.0):
        cosine = cosine * square + term
    quadrant = quadrant & 3
    odd = (quadrant & 1) == 1
    first = jnp.where(odd, sine, cosine)
    second = jnp.where(odd, cosine, sine)
    return (
        jnp.where((quadrant == 1) | (quadrant == 2), -first, first),
        jnp.where(quadrant >= 2, -second, second),
    )


def e_step_kernel(
    dom_size,
    cls_size,
    offsets_ref,
    images_hbm,
    target_ref,
    group_ref,
    inv_noise_hbm,
    ctf_hbm,
    refs_hbm,
    landed,
    images_ref,
    inv_noise_ref,
    ctf_ref,
    refs_ref,
    held,
    shifted,
    ctf_parts,
    cosines,
    sines,
    cross,
    norms,
    slot_hot,
    group_hot_rows,
    slots_ref,
    stage,
    load_sem,
    send_sem,
    recv_sem,
    post_send,
    post_recv,
    own_sem,
):
    z_size = dom_size // 2
    class_count, block_columns = refs_ref.shape
    half_columns = block_columns // 2
    padded = held.shape[3]
    local_count = images_ref.shape[0]
    kept = inv_noise_ref.shape[1]
    group_count = ctf_ref.shape[0]
    shift_count = offsets_ref.shape[1]
    slot_count = slot_hot.shape[0]
    capacity = slot_count // dom_size
    piece_rows, lanes = stage.shape[2:]
    group_size = lanes // capacity
    dom = lax.axis_index("dom")
    cls = lax.axis_index("cls")
    z, x = dom // 2, dom % 2
    y, core = cls // 2, cls % 2

    loads = [
        pltpu.make_async_copy(source, place, load_sem.at[index])
        for index, (source, place) in enumerate(
            [
                (refs_hbm, refs_ref),
                (ctf_hbm, ctf_ref),
                (inv_noise_hbm, inv_noise_ref),
                (images_hbm, images_ref),
            ]
        )
    ]
    for load in loads:
        load.start()
    barrier = pltpu.get_barrier_semaphore()
    partners = [
        [
            (lax.rem(dom + i, dom_size), lax.rem(cls + j, cls_size))
            for i in sorted(range(dom_size), key=lambda i: (abs(i - dom_size // 2), i))
            if i or j
        ]
        for j in range(cls_size)
    ]
    every_partner = sum(partners, [])
    def z_partner(step):
        other, bit = z, 1
        while bit < z_size:
            if step & bit:
                other = other + bit - 2 * bit * ((z // bit) % 2)
            bit *= 2
        return other

    order = list(range(0, z_size, 2)) + list(range(1, z_size, 2))
    over_x = (z * 2 + (1 - x), cls)
    over_y = (dom, (1 - y) * 2 + core)
    over_core = (dom, y * 2 + (1 - core))
    neighbours = [over_x, over_y, over_core]
    neighbours += [(z_partner(step) * 2 + x, cls) for step in order[1:]]
    for partner in neighbours:
        pl.semaphore_signal(barrier, inc=1, device_id=partner, device_id_type=MESH)

    for load in loads[:3]:
        load.wait()
    wide = refs_ref[...].astype(jnp.float32)
    squares = jnp.concatenate(
        [wide * wide, jnp.zeros((padded - class_count, block_columns), jnp.float32)], axis=0
    )
    high = squares.astype(jnp.bfloat16)
    rest = (squares - high.astype(jnp.float32)).astype(jnp.bfloat16)
    low = pl.multiple_of(lax.rem(dom * block_columns, kept), block_columns)
    own_ctf = ctf_ref[:, pl.ds(low, block_columns)]
    noise_terms = inv_noise_ref[:, pl.ds(low, block_columns)] * own_ctf * own_ctf
    sums = lax.dot_general(
        jnp.concatenate(three_parts(noise_terms), axis=0),
        jnp.concatenate([high, rest], axis=0),
        NT_DIMS,
        preferred_element_type=jnp.float32,
    )
    sums = sums[:, :padded] + sums[:, padded:]
    own_norms = (
        sums[:group_count] + sums[group_count : 2 * group_count] + sums[2 * group_count :]
    )
    tail = jnp.concatenate(
        [part.astype(jnp.float32) for part in three_parts(own_norms)]
        + [jnp.zeros((group_count, half_columns - 3 * padded), jnp.float32)],
        axis=1,
    )
    for half in range(2):
        rows = wide[:, half * half_columns : (half + 1) * half_columns]
        extra = padded - class_count
        block = jnp.concatenate([rows, tail[half * extra : (half + 1) * extra]], axis=0)
        held[half, dom, cls] = block.astype(jnp.bfloat16)
    pl.semaphore_wait(barrier, len(neighbours))

    sends = []

    def block_copy(half, block_dom, block_cls, device, index):
        halves, sem = (slice(None), 0) if half is None else (half, half)
        block = held.at[halves, block_dom, block_cls]
        return pltpu.make_async_remote_copy(
            src_ref=block,
            dst_ref=block,
            send_sem=send_sem.at[index],
            recv_sem=recv_sem.at[sem, block_dom, block_cls],
            device_id=device,
            device_id_type=MESH,
        )

    def send(half, block_dom, block_cls, device):
        copy = block_copy(half, block_dom, block_cls, device, len(sends))
        copy.start()
        sends.append(copy)

    def arrived(half, block_dom, block_cls):
        block_copy(half, block_dom, block_cls, over_core, 0).wait_recv()

    send(0, dom, cls, over_x)
    send(1, dom, cls, over_y)
    for step in order[1:2]:
        send(None, dom, cls, (z_partner(step) * 2 + x, cls))
    send(1, dom, cls, over_x)
    send(0, dom, cls, over_y)
    for step in order[2:]:
        send(None, dom, cls, (z_partner(step) * 2 + x, cls))
    send(None, dom, cls, over_core)

    table_shape = (cosines.shape[0], kept)
    freq = lax.broadcasted_iota(jnp.int32, table_shape, 1)
    shift_row = lax.broadcasted_iota(jnp.int32, table_shape, 0)
    half_side = SIDE // 2
    row_freq = freq // half_side
    col_freq = freq % half_side
    row_freq = jnp.where(row_freq >= half_side, row_freq - SIDE, row_freq)
    turns = jnp.zeros(table_shape, jnp.int32)
    for t in range(shift_count):
        turn = offsets_ref[0, t] * row_freq + offsets_ref[1, t] * col_freq
        turns = jnp.where(shift_row == t, turn & (SIDE - 1), turns)
    cosines[...], sines[...] = quarter_turns(turns)
    for index, part in enumerate(three_parts(ctf_ref[...])):
        ctf_parts[index * group_count : (index + 1) * group_count, :] = part
    square = (local_count, local_count)
    sub = lax.broadcasted_iota(jnp.int32, square, 0)
    lane = lax.broadcasted_iota(jnp.int32, square, 1)
    group_row = group_ref[...]
    group_col = jnp.sum(jnp.where(sub == lane, group_row, 0), axis=1, keepdims=True)
    part_lane = lax.broadcasted_iota(jnp.int32, (local_count, 3 * group_count), 1)
    group_hot = jnp.where(part_lane % group_count == group_col, 1.0, 0.0).astype(jnp.bfloat16)

    chunk = kept // 4

    def shift_chunk(step):
        low = step * chunk
        columns = slice(low, low + chunk)
        imag_columns = slice(kept + low, kept + low + chunk)
        weight = inv_noise_ref[:, columns] * jnp.dot(
            group_hot, ctf_parts[:, columns], preferred_element_type=jnp.float32
        )
        real_part = images_ref[:, columns].astype(jnp.float32)
        imag_part = images_ref[:, imag_columns].astype(jnp.float32)
        for t in range(shift_count):
            cosine = cosines[t : t + 1, columns]
            sine = sines[t : t + 1, columns]
            rows = slice(t * local_count, (t + 1) * local_count)
            shifted[rows, columns] = (
                weight * (real_part * cosine - imag_part * sine)
            ).astype(jnp.bfloat16)
            shifted[rows, imag_columns] = (
                weight * (real_part * sine + imag_part * cosine)
            ).astype(jnp.bfloat16)

    hot_rows = lax.broadcasted_iota(jnp.int32, group_hot_rows.shape, 0)
    group_hot_rows[...] = jnp.where(hot_rows % group_count == group_row, 1.0, 0.0).astype(
        jnp.bfloat16
    )
    target_row = target_ref[...]
    target_col = jnp.sum(jnp.where(sub == lane, target_row, 0), axis=1, keepdims=True)
    ahead = (target_col == target_row) & (sub < lane)
    rank = jnp.sum(jnp.where(ahead, 1, 0), axis=0, keepdims=True)
    slot_of = target_row * capacity + rank
    slot = lax.broadcasted_iota(jnp.int32, (slot_count, local_count), 0)
    hot = jnp.where(slot == slot_of, 1.0, 0.0).astype(jnp.bfloat16)
    for index in range(3):
        slot_hot[:, index * local_count : (index + 1) * local_count] = hot
    cross[...] = jnp.zeros_like(cross)
    norms[...] = jnp.zeros_like(norms)

    def from_z(step):
        block = z_partner(step) * 2 + x
        arrived(None, block, cls)
        send(0, block, cls, over_x)
        send(1, block, cls, over_y)
        send(1, block, cls, over_x)
        send(0, block, cls, over_y)
        send(None, block, cls, over_core)

    def from_first(step):
        near, far = z_partner(step) * 2 + x, z_partner(step) * 2 + (1 - x)
        arrived(0, far, cls)
        if step % 2 == 0:
            send(0, far, cls, over_y)
        arrived(1, near, over_y[1])
        if step % 2 == 0:
            send(1, near, over_y[1], over_x)
        send(0, far, cls, over_core)
        send(1, near, over_y[1], over_core)

    def from_last(step):
        near, far = z_partner(step) * 2 + x, z_partner(step) * 2 + (1 - x)
        arrived(0, near, over_y[1])
        send(0, near, over_y[1], over_core)
        arrived(1, far, cls)
        send(1, far, cls, over_core)
        if step % 2 == 0:
            arrived(0, far, over_y[1])
            arrived(1, far, over_y[1])
            if z_size > 1:
                send(None, far, over_y[1], (z_partner(1) * 2 + x, cls))
        else:
            arrived(None, far, over_y[1])
        send(None, far, over_y[1], over_core)

    sibling, far_sibling = over_core[1], (1 - y) * 2 + (1 - core)

    def add_block(block_dom):
        rows = jnp.concatenate(
            [held[half, block_dom].reshape(cls_size * padded, half_columns) for half in range(2)],
            axis=1,
        )
        low = pl.multiple_of(block_dom * block_columns, block_columns)
        cross[...] += lax.dot_general(
            rows, shifted[:, pl.ds(low, block_columns)], NT_DIMS, preferred_element_type=jnp.float32
        )
        for half in range(2):
            last_rows = held[half, block_dom, :, padded - 16 : padded, :].astype(jnp.float32)
            norms[half] += last_rows[:, 8:16, :]

    def multiply_near(step):
        while chunks:
            shift_chunk(chunks.pop(0))
        near = z_partner(step) * 2 + x
        arrived(None, near, sibling)
        arrived(0, near, far_sibling)
        arrived(1, near, far_sibling)
        add_block(near)

    def multiply_far(step):
        far = z_partner(step) * 2 + (1 - x)
        arrived(0, far, sibling)
        arrived(1, far, sibling)
        arrived(None, far, far_sibling)
        add_block(far)

    chunks = list(range(4))
    loads[3].wait()
    shift_chunk(chunks.pop(0))
    for turn in range(z_size + 2):
        if 0 < turn < z_size:
            from_z(order[turn])
        if turn == 1:
            shift_chunk(chunks.pop(0))
        if turn >= 2:
            multiply_near(order[turn - 2])
        if turn < z_size:
            from_first(order[turn])
        if turn == 1:
            shift_chunk(chunks.pop(0))
        if 0 < turn <= z_size:
            from_last(order[turn - 1])
        if turn >= 2:
            multiply_far(order[turn - 2])

    selected = []
    for block in range(cls_size):
        both = jnp.concatenate([norms[0, block], norms[1, block]], axis=0)
        total_norm = sum(both[:, p * padded : (p + 1) * padded] for p in range(3))
        selected.append(
            lax.dot_general(
                jnp.concatenate(three_parts(total_norm), axis=0),
                group_hot_rows[...],
                (((0,), (0,)), ((), ())),
                preferred_element_type=jnp.float32,
            )
        )
    selected = 0.5 * jnp.concatenate(selected, axis=0)
    row = lax.broadcasted_iota(jnp.int32, (cls_size * padded, local_count), 0) % padded
    real_row = row < class_count
    scores = []
    for t in range(shift_count):
        value = cross[:, t * local_count : (t + 1) * local_count] - selected
        scores.append(jnp.where(real_row, value, -jnp.inf))
    peak = functools.reduce(jnp.maximum, scores)
    peak = jnp.max(peak, axis=0, keepdims=True)
    weights = functools.reduce(jnp.add, [jnp.exp(value - peak) for value in scores])
    total = jnp.sum(weights, axis=0, keepdims=True)
    log_norm = peak + jnp.log(total)
    table = jnp.where(row == class_count, log_norm, weights / total)

    slots_ref[...] = lax.dot_general(
        jnp.concatenate(three_parts(table), axis=1),
        slot_hot[...],
        NT_DIMS,
        preferred_element_type=jnp.float32,
    )
    lane_group = lax.broadcasted_iota(jnp.int32, (8, lanes), 1) // capacity
    whole = class_count // (8 * group_size)
    left_over = (class_count - whole * 8 * group_size) // group_size

    def turned(value, groups):
        amount = groups % group_size * capacity
        return pltpu.roll(value, amount, 1) if amount else value

    def lifted(value, rows):
        return pltpu.roll(value, rows % 8, 0) if rows % 8 else value

    def side_by_side(values):
        result = values[0]
        for k in range(1, group_size):
            result = jnp.where(lane_group == k, values[k], result)
        return result

    sub_row = lax.broadcasted_iota(jnp.int32, (8, lanes), 0)
    posts = []
    for turn in range(cls_size):
        block = lax.rem(cls + turn, cls_size)
        part = slots_ref[pl.ds(pl.multiple_of(block * padded, 16), padded), :]
        for to_dom in range(dom_size):
            place, member = to_dom // group_size, to_dom % group_size
            tile = part[:, place * lanes : (place + 1) * lanes]
            for w in range(whole):
                values = []
                for k in range(group_size):
                    top = 8 * (k * whole + w)
                    values.append(turned(tile[top : top + 8], k - member))
                stage[to_dom, block, 8 * w : 8 * w + 8, :] = side_by_side(values)
            rest = tile[8 * whole * group_size : class_count]
            values = [
                turned(lifted(rest, -left_over * k), k - member) for k in range(group_size)
            ]
            norm_row = lifted(turned(tile[class_count:padded], -member), left_over)
            mixed = jnp.where(sub_row < left_over, side_by_side(values), norm_row)
            stage[to_dom, block, 8 * whole : piece_rows, :] = mixed[: piece_rows - 8 * whole]
        for to_dom, to_cls in partners[turn]:
            copy = pltpu.make_async_remote_copy(
                src_ref=stage.at[to_dom, to_cls],
                dst_ref=landed.at[cls, dom],
                send_sem=post_send.at[len(posts)],
                recv_sem=post_recv.at[cls, dom],
                device_id=(to_dom, to_cls),
                device_id_type=MESH,
            )
            copy.start()
            posts.append(copy)
    own = pltpu.make_async_copy(stage.at[dom, cls], landed.at[cls, dom], own_sem)
    own.start()
    for copy in sends:
        copy.wait_send()
    for copy in posts:
        copy.wait_send()
    own.wait()
    for from_dom, from_cls in every_partner:
        pltpu.make_async_remote_copy(
            src_ref=stage.at[from_dom, from_cls],
            dst_ref=landed.at[from_cls, from_dom],
            send_sem=post_send.at[0],
            recv_sem=post_recv.at[from_cls, from_dom],
            device_id=(from_dom, from_cls),
            device_id_type=MESH,
        ).wait_recv()


def unpack_kernel(
    capacity, landed_hbm, out_hbm, log_hbm, landed, out_ref, log_ref, in_sem, out_sem, log_sem
):
    cls_size, dom_size, piece_rows, lanes = landed.shape
    class_count = out_ref.shape[0]
    group_size = lanes // capacity
    lane_group = lax.broadcasted_iota(jnp.int32, (8, lanes), 1) // capacity
    whole = class_count // (8 * group_size)
    left_over = (class_count - whole * 8 * group_size) // group_size

    def turned(value, groups):
        amount = groups % group_size * capacity
        return pltpu.roll(value, amount, 1) if amount else value

    def side_by_side(values):
        result = values[0]
        for k in range(1, group_size):
            result = jnp.where(lane_group == k, values[k], result)
        return result

    def pad_rows(value):
        empty = jnp.zeros((8 - value.shape[0], lanes), jnp.float32)
        return jnp.concatenate([value, empty], axis=0)

    slot_count = dom_size * capacity
    loads = [
        pltpu.make_async_copy(landed_hbm.at[block], landed.at[block], in_sem.at[block])
        for block in range(cls_size)
    ]
    for load in loads:
        load.start()
    stores = []
    for block in range(cls_size):
        loads[block].wait()
        for place in range(dom_size // group_size):
            low = block * slot_count + place * lanes
            got = [landed[block, place * group_size + member] for member in range(group_size)]
            for k in range(group_size):
                for w in range(whole):
                    top = 8 * (k * whole + w)
                    out_ref[top : top + 8, low : low + lanes] = side_by_side(
                        [
                            turned(value[8 * w : 8 * w + 8], member - k)
                            for member, value in enumerate(got)
                        ]
                    )
                top = 8 * whole * group_size + left_over * k
                out_ref[top : top + left_over, low : low + lanes] = side_by_side(
                    [
                        turned(pad_rows(value[8 * whole :]), member - k)
                        for member, value in enumerate(got)
                    ]
                )[:left_over]
            log_ref[:, low : low + lanes] = side_by_side(
                [turned(pad_rows(value[8 * whole :]), member) for member, value in enumerate(got)]
            )[left_over : left_over + 1]
        columns = slice(block * slot_count, (block + 1) * slot_count)
        store = pltpu.make_async_copy(
            out_ref.at[:, columns], out_hbm.at[:, columns], out_sem.at[block]
        )
        store.start()
        stores.append(store)
    store = pltpu.make_async_copy(log_ref, log_hbm, log_sem)
    store.start()
    for store in stores + [store]:
        store.wait()


def kernel_shards(images, destinations, group_ids, offsets, inv_noise, ctf_table, references):
    dom_size = lax.axis_size("dom")
    cls_size = lax.axis_size("cls")
    local_count, columns = images.shape
    kept = inv_noise.shape[0]
    group_count = ctf_table.shape[0]
    shift_count = offsets.shape[0]
    class_count, block_columns = references.shape
    slot_count = 2 * local_count
    lanes = 128
    piece_rows = class_count // (lanes // (slot_count // dom_size)) + 1
    padded = class_count + 8
    device_count = dom_size * cls_size
    table_rows = -(-shift_count // 8) * 8
    vmem = pl.BlockSpec(memory_space=pltpu.VMEM)
    hbm = pl.BlockSpec(memory_space=pltpu.HBM)
    packed = pl.pallas_call(
        functools.partial(e_step_kernel, dom_size, cls_size),
        out_shape=jax.ShapeDtypeStruct((cls_size, dom_size, piece_rows, lanes), jnp.float32),
        in_specs=[pl.BlockSpec(memory_space=pltpu.SMEM), hbm, vmem, vmem, hbm, hbm, hbm],
        out_specs=hbm,
        scratch_shapes=[
            pltpu.VMEM((local_count, columns), jnp.bfloat16),
            pltpu.VMEM((1, kept), jnp.float32),
            pltpu.VMEM((group_count, kept), jnp.float32),
            pltpu.VMEM((class_count, block_columns), jnp.bfloat16),
            pltpu.VMEM((2, dom_size, cls_size, padded, block_columns // 2), jnp.bfloat16),
            pltpu.VMEM((shift_count * local_count, columns), jnp.bfloat16),
            pltpu.VMEM((3 * group_count, kept), jnp.bfloat16),
            pltpu.VMEM((table_rows, kept), jnp.float32),
            pltpu.VMEM((table_rows, kept), jnp.float32),
            pltpu.VMEM((cls_size * padded, shift_count * local_count), jnp.float32),
            pltpu.VMEM((2, cls_size, 8, block_columns // 2), jnp.float32),
            pltpu.VMEM((slot_count, 3 * local_count), jnp.bfloat16),
            pltpu.VMEM((3 * group_count, local_count), jnp.bfloat16),
            pltpu.VMEM((cls_size * padded, slot_count), jnp.float32),
            pltpu.VMEM((dom_size, cls_size, piece_rows, lanes), jnp.float32),
            pltpu.SemaphoreType.DMA((4,)),
            pltpu.SemaphoreType.DMA((2 * device_count + dom_size,)),
            pltpu.SemaphoreType.DMA((2, dom_size, cls_size)),
            pltpu.SemaphoreType.DMA((device_count,)),
            pltpu.SemaphoreType.DMA((cls_size, dom_size)),
            pltpu.SemaphoreType.DMA,
        ],
        compiler_params=pltpu.CompilerParams(
            collective_id=0, has_side_effects=True, vmem_limit_bytes=56 * 1024 * 1024
        ),
    )(
        offsets.T,
        images,
        destinations.T,
        group_ids[None, :],
        inv_noise[None, :],
        ctf_table,
        references,
    )
    posteriors, log_norms = pl.pallas_call(
        functools.partial(unpack_kernel, slot_count // dom_size),
        out_shape=(
            jax.ShapeDtypeStruct((class_count, cls_size * slot_count), jnp.float32),
            jax.ShapeDtypeStruct((1, cls_size * slot_count), jnp.float32),
        ),
        in_specs=[hbm],
        out_specs=(hbm, hbm),
        scratch_shapes=[
            pltpu.VMEM((cls_size, dom_size, piece_rows, lanes), jnp.float32),
            pltpu.VMEM((class_count, cls_size * slot_count), jnp.float32),
            pltpu.VMEM((1, cls_size * slot_count), jnp.float32),
            pltpu.SemaphoreType.DMA((cls_size,)),
            pltpu.SemaphoreType.DMA((cls_size,)),
            pltpu.SemaphoreType.DMA,
        ],
        compiler_params=pltpu.CompilerParams(vmem_limit_bytes=56 * 1024 * 1024),
    )(packed)
    return (posteriors.T, log_norms[0])


def fits_kernel(mesh, images, ctf_table, references):
    dom_size, cls_size = mesh.shape["dom"], mesh.shape["cls"]
    local_count = images.shape[0] // (dom_size * cls_size)
    capacity = 2 * local_count // dom_size
    class_count = references.shape[0] // cls_size
    half_columns = references.shape[1] // dom_size // 2
    if cls_size != 4 or dom_size % 2 or local_count != 128 or 128 % capacity:
        return False
    group_size = 128 // capacity
    return (
        group_size > 1
        and dom_size % group_size == 0
        and class_count % 8 == 0
        and class_count % (8 * group_size) == 8
        and 8 // group_size * group_size == 8
        and 8 // group_size < 8
        and dom_size & (dom_size - 1) == 0
        and (class_count + 8) % 16 == 0
        and half_columns % 128 == 0
        and 3 * (class_count + 8) < half_columns
        and ctf_table.shape[0] == 16
    )


def solution(mesh):
    def e_step(*arrays):
        shards = kernel_shards if fits_kernel(mesh, arrays[0], arrays[-2], arrays[-1]) else plain_shards
        return mapped(mesh, shards)(*arrays)

    return e_step


def mapped(mesh, shards):
    return jax.shard_map(
        shards,
        mesh=mesh,
        in_specs=(
            P(("dom", "cls"), None),
            P(("dom", "cls"), None),
            P(("dom", "cls")),
            P(),
            P(),
            P(),
            P("cls", "dom"),
        ),
        out_specs=(P("dom", "cls"), P("dom")),
        check_vma=False,
    )
```
